32 devices in a mesh: gx: 4 (over x, core), gy: 8 (over z, y).
Axes of the slice: x: 2, y: 2, z: 4, core: 2. Of those that a mesh axis runs over, the one named last changes fastest.
Arguments:
- adj_electric: float32 [3, 128, 64, 128], P(None, 'gx', 'gy'), may hold values from -6 to 6
- adj_magnetic: float32 [3, 128, 64, 128], P(None, 'gx', 'gy'), may hold values from -6 to 6
- polarization: float32 [3, 128, 64, 128], P(None, 'gx', 'gy'), may hold values from -6 to 6
- pol_rate: float32 [3, 128, 64, 128], P(None, 'gx', 'gy'), may hold values from -6 to 6
- density: float32 [128, 64, 128], P('gx', 'gy'), may hold values from 0 to 1
- forward_rate: float32 [2, 3, 128, 64, 128], P(None, None, 'gx', 'gy'), may hold values from -6 to 6
- design_mask: int32 [128, 64, 128], P('gx', 'gy'), may hold values 0 or 1
- partner_rows: int32 [64], P('gy'), may hold values from 0 to 7, as said below
- filter_radius: int32 [128, 64], P('gx', 'gy'), may hold values from 1 to 4
Outputs:
- electric_out: float32 [3, 128, 64, 128], P(None, 'gx', 'gy')
- magnetic_out: float32 [3, 128, 64, 128], P(None, 'gx', 'gy')
- density_out: float32 [128, 64, 128], P('gx', 'gy')
The draws below stay inside these ranges and needn't reach their ends.
Inputs may be any that keep to these rules, and one draw needn't show every extreme that they name: `partner_rows`: within each block of 8 rows the values are a permutation of 0 to 7.
All inputs are finite; a program needn't handle non-finite values. No bound on the sum of `design_mask` on one device may be relied on, other than what follows from the above.
Results may differ from the reference program's by a relative error of at most 0.0001.
Values sent between devices are 32-bit elements; how exact they have to be, the bound alone decides.
No kernel may reach another device: no remote copies, remote signals or barrier semaphores. Data moves between devices by JAX's collectives and lax.ppermute only.
A program may use at most 64 MiB of HBM per device.

```python
import math
import jax
import jax.numpy as jnp
from jax import lax

CY = 8
STEPS = 2
RMAX = 4
NX = 128
NY = 64
NZ = 128


def draw_partner_rows(key, part):
    blocks = NY // CY
    keys = jax.random.split(jax.random.fold_in(key, 11), blocks)
    perms = jax.vmap(lambda single: jax.random.permutation(single, CY))(keys)
    return perms.reshape(NY).astype(jnp.int32)


def draw_filter_radius(key, part):
    first, second, third = jax.random.split(jax.random.fold_in(key, 23), 3)
    radius = jax.random.randint(first, (NX, NY), 1, RMAX + 1)
    where_x = jax.random.randint(second, (), 0, NX)
    where_y = jax.random.randint(third, (), 0, NY)
    return radius.at[where_x, where_y].set(RMAX).astype(jnp.int32)


def plant(result, key, low, largest):
    longest = result.shape.index(max(result.shape))
    spots = []
    for shift in (0, 1):
        where = [jax.random.randint(jax.random.fold_in(key, axis), (), 0, length) for axis, length in enumerate(result.shape)]
        where[longest] = (where[longest] + shift) % result.shape[longest]
        spots.append(tuple(where))
    return result.at[spots[0]].set(low).at[spots[1]].set(largest)


def shard_levels(rng, extent, cuts, least, high):
    factor_of = 1.0
    for position, parts in cuts:
        draws = jax.random.uniform(jax.random.fold_in(jax.random.fold_in(rng, 6), position), (parts,), jnp.float32, least / len(cuts), high / len(cuts))
        factor_of = factor_of * jnp.repeat(jnp.exp(draws), extent[position] // parts).reshape((-1,) + (1,) * (len(extent) - 1 - position))
    return factor_of


def noise(stream_key, shape, scale, bound, pieces=(), kind=jnp.bfloat16):
    level = shard_levels(stream_key, shape, pieces, -0.22, 0.18) if pieces else 1.0
    entries = jax.random.normal(stream_key, shape, jnp.float32) * scale * level
    return jnp.minimum(jnp.maximum(entries, -bound), bound).astype(kind)


def setup_inputs(seed: int = 0) -> dict:
    streams_of = jax.random.split(jax.random.key(seed), 10)
    adj_electric = noise(streams_of[0], (3, NX, NY, NZ), 1.0, 6.0, ((1, 4), (2, 8)), jnp.float32)
    adj_magnetic = noise(streams_of[1], (3, NX, NY, NZ), 1.0, 6.0, ((1, 4), (2, 8)), jnp.float32)
    polarization = noise(streams_of[2], (3, NX, NY, NZ), 1.0, 6.0, ((1, 4), (2, 8)), jnp.float32)
    pol_rate = noise(streams_of[3], (3, NX, NY, NZ), 1.0, 6.0, ((1, 4), (2, 8)), jnp.float32)
    density = jnp.clip(1.0 * jax.random.uniform(streams_of[4], (NX, NY, NZ), jnp.float32) ** shard_levels(streams_of[4], (NX, NY, NZ), ((0, 4), (1, 8)), -0.2, 0.2), 0.0, 1.0)
    forward_rate = noise(streams_of[5], (STEPS, 3, NX, NY, NZ), 1.0, 6.0, ((2, 4), (3, 8)), jnp.float32)
    design_mask = plant((jax.random.randint(streams_of[6], (NX, NY, NZ), 0, 4) < 3).astype(jnp.int32), jax.random.fold_in(streams_of[6], 1), 0, 1)
    partner_rows = draw_partner_rows(jax.random.fold_in(streams_of[9], 71), 0)
    filter_radius = draw_filter_radius(jax.random.fold_in(streams_of[9], 71), 0)
    return dict(adj_electric=adj_electric, adj_magnetic=adj_magnetic, polarization=polarization, pol_rate=pol_rate, density=density, forward_rate=forward_rate, design_mask=design_mask, partner_rows=partner_rows, filter_radius=filter_radius)


COURANT = 0.5
DAMPING = 0.9
OMEGA_SQUARED = 0.3
LORENTZ_STRENGTH = 2.0
EPS_MATERIAL = 4.0
UPDATE_STEP = 0.25
SHARPNESS = 4.0
THRESHOLD = 0.5

def ahead(values, dimension):
    count = values.shape[dimension]
    rest = lax.slice_in_dim(values, 1, count, axis=dimension)
    edge = jnp.zeros_like(lax.slice_in_dim(values, 0, 1, axis=dimension))
    return jnp.concatenate([rest, edge], dimension)

def behind(values, dimension):
    count = values.shape[dimension]
    rest = lax.slice_in_dim(values, 0, count - 1, axis=dimension)
    edge = jnp.zeros_like(lax.slice_in_dim(values, 0, 1, axis=dimension))
    return jnp.concatenate([edge, rest], dimension)

def advance(electric, magnetic, polar_now, velocity, material, inside):
    eps_local = 1.0 + (EPS_MATERIAL - 1.0) * material
    e_x, e_y, e_z = (electric[0], electric[1], electric[2])
    curl_e = jnp.stack([ahead(e_z, 1) - e_z - (ahead(e_y, 2) - e_y), ahead(e_x, 2) - e_x - (ahead(e_z, 0) - e_z), ahead(e_y, 0) - e_y - (ahead(e_x, 1) - e_x)])
    magnetic = (magnetic - COURANT * curl_e) * inside
    h_x, h_y, h_z = (magnetic[0], magnetic[1], magnetic[2])
    curl_h = jnp.stack([h_z - behind(h_z, 1) - (h_y - behind(h_y, 2)), h_x - behind(h_x, 2) - (h_z - behind(h_z, 0)), h_y - behind(h_y, 0) - (h_x - behind(h_x, 1))])
    velocity = DAMPING * velocity - OMEGA_SQUARED * polar_now + OMEGA_SQUARED * LORENTZ_STRENGTH * material * electric
    polar_now = polar_now + velocity
    electric = (electric + (COURANT * curl_h - velocity) / eps_local) * inside
    return (electric, magnetic, polar_now, velocity)

def project(filtered):
    top = math.tanh(SHARPNESS * THRESHOLD)
    bottom = top + math.tanh(SHARPNESS * (1.0 - THRESHOLD))
    return (top + jnp.tanh(SHARPNESS * (filtered - THRESHOLD))) / bottom

def reference(adj_electric, adj_magnetic, polarization, pol_rate, density, forward_rate, design_mask, partner_rows, filter_radius):
    electric, magnetic, polar_now, velocity = (adj_electric, adj_magnetic, polarization, pol_rate)
    gradient = jnp.zeros(density.shape, jnp.float32)
    for step_index in range(STEPS):
        electric, magnetic, polar_now, velocity = advance(electric, magnetic, polar_now, velocity, density, 1.0)
        gradient = gradient + lax.optimization_barrier(jnp.sum(electric * forward_rate[step_index], axis=0))
    row_index = jnp.arange(NY, dtype=jnp.int32) // CY * CY + partner_rows.astype(jnp.int32)
    mirrored = jnp.take(gradient[::-1], row_index, axis=1)
    symmetric = 0.5 * (gradient + mirrored)
    updated = density - UPDATE_STEP * design_mask.astype(jnp.float32) * symmetric
    width = RMAX - 1
    framed = jnp.pad(updated, ((width, width), (width, width), (0, 0)))
    covered = jnp.pad(jnp.ones((NX, NY, 1), jnp.float32), ((width, width), (width, width), (0, 0)))
    radius = filter_radius.astype(jnp.float32)[:, :, None]
    numer = jnp.zeros(density.shape, jnp.float32)
    denom = jnp.zeros((NX, NY, 1), jnp.float32)
    for shift_x in range(-width, width + 1):
        for shift_y in range(-width, width + 1):
            distance = math.sqrt(shift_x * shift_x + shift_y * shift_y)
            weight = jnp.maximum(radius - distance, 0.0)
            window = framed[width + shift_x:width + shift_x + NX, width + shift_y:width + shift_y + NY, :]
            inside = covered[width + shift_x:width + shift_x + NX, width + shift_y:width + shift_y + NY, :]
            numer = numer + weight * (inside * window)
            denom = denom + weight * inside
    density_out = project(numer / denom)
    return (electric, magnetic, density_out)
```

```python
import functools
import math

import jax
import jax.numpy as jnp
from jax import lax
from jax.experimental import pallas as pl
from jax.experimental.pallas import tpu as pltpu
from jax.sharding import PartitionSpec as P

STEPS = 2
RMAX = 4

COURANT = 0.5
DAMPING = 0.9
OMEGA_SQUARED = 0.3
LORENTZ_STRENGTH = 2.0
EPS_MATERIAL = 4.0
UPDATE_STEP = 0.25
SHARPNESS = 4.0
THRESHOLD = 0.5

AXES = ("gx", "gy")
WIDTH = RMAX - 1
SLOTS = 20
BASE = 8
EXTRA = 8
VMEM = pltpu.VMEM


def x_even(x, y, nx, ny):
    return x ^ 1, y


def x_odd(x, y, nx, ny):
    other = x + 1 if x % 2 else x - 1
    return (other, y) if 0 <= other < nx else (x, y ^ 1)


def y_even(x, y, nx, ny):
    return x, y ^ 1


def y_odd(x, y, nx, ny):
    other = y + 1 if y % 2 else y - 1
    return (x, other) if 0 <= other < ny else (x ^ 1, y)


def mirror(x, y, nx, ny):
    return nx - 1 - x, y


def mirror_even(x, y, nx, ny):
    return nx - 1 - (x ^ 1), y


def mirror_odd(x, y, nx, ny):
    other = x + 1 if x % 2 else x - 1
    return (nx - 1 - other, y) if 0 <= other < nx else (nx - 1 - x, y)


def send(block, rule):
    nx, ny = lax.axis_size("gx"), lax.axis_size("gy")
    route = []
    for x in range(nx):
        for y in range(ny):
            to_x, to_y = rule(x, y, nx, ny)
            route.append((x * ny + y, to_x * ny + to_y))
    return lax.ppermute(block, AXES, route)


def odd_x():
    return lax.rem(lax.axis_index("gx"), 2) == 1


def odd_y():
    return lax.rem(lax.axis_index("gy"), 2) == 1


def edges():
    x, y = lax.axis_index("gx"), lax.axis_index("gy")
    return (x > 0, x < lax.axis_size("gx") - 1, y > 0, y < lax.axis_size("gy") - 1)


def rows_of(shape):
    return lax.broadcasted_iota(jnp.int32, shape, len(shape) - 2)


def lanes_of(shape):
    return lax.broadcasted_iota(jnp.int32, shape, len(shape) - 1)


def ahead_z(v):
    depth = v.shape[-1]
    return jnp.where(lanes_of(v.shape) == depth - 1, 0.0, pltpu.roll(v, depth - 1, v.ndim - 1))


def behind_z(v):
    return jnp.where(lanes_of(v.shape) == 0, 0.0, pltpu.roll(v, 1, v.ndim - 1))


def ahead_y(v, edge=0.0):
    rows = v.shape[-2]
    return jnp.where(rows_of(v.shape) == rows - 1, edge, pltpu.roll(v, rows - 1, v.ndim - 2))


def behind_y(v, edge=0.0):
    return jnp.where(rows_of(v.shape) == 0, edge, pltpu.roll(v, 1, v.ndim - 2))


def keep(flag, v):
    return jnp.where(flag, v, 0.0)


def call(kernel, outs, args, aliases=None, flops=0):
    args = [a if m is pltpu.SMEM else pltpu.with_memory_space_constraint(a, VMEM) for a, m in [(a, VMEM) for a in args]]
    shapes = tuple(VMEM(s, jnp.float32) for s in outs)
    spec = pl.BlockSpec(memory_space=VMEM)
    traffic = 4 * (sum(math.prod(s) for s in outs) + sum(math.prod(a.shape) for a in args))
    return pl.pallas_call(
        kernel,
        out_shape=shapes,
        in_specs=[spec] * len(args),
        out_specs=tuple([spec] * len(outs)),
        input_output_aliases=aliases or {},
        cost_estimate=pl.CostEstimate(flops=flops, bytes_accessed=traffic, transcendentals=0),
        compiler_params=pltpu.CompilerParams(vmem_limit_bytes=16 * 2**20),
    )(*args)


def pack_x(n, r, e, h, p, q, d, m, even_out, odd_out):
    odd = odd_x()
    for out, low in ((even_out, odd), (odd_out, jnp.logical_not(odd))):
        near = jnp.where(low, 0, n - 1)
        step = jnp.where(low, 1, -1)
        at = [pl.ds(pl.multiple_of((near + k * step) * r, r), r) for k in range(WIDTH)]

        def put(slot, v):
            out[slot * r : (slot + 1) * r, :] = v

        for c in range(3):
            put(c, e[c, at[0], :])
            put(3 + c, h[c, at[0], :])
            put(6 + c, DAMPING * q[c, at[0], :] - OMEGA_SQUARED * p[c, at[0], :])
            put(10 + c, e[c, at[1], :])
        put(9, d[at[0], :])
        put(13, h[1, at[1], :])
        put(14, h[2, at[1], :])
        put(15, d[at[1], :])
        put(16, d[at[2], :])
        for k in range(WIDTH):
            put(17 + k, m[at[k], :].astype(jnp.float32))


def new_h(h, e, e_next, edge_x=0.0, edge_z=0.0):
    ex, ey, ez = e
    return (
        h[0] - COURANT * ((ahead_y(ez, edge_z) - ez) - (ahead_z(ey) - ey)),
        h[1] - COURANT * ((ahead_z(ex) - ex) - (e_next[2] - ez)),
        h[2] - COURANT * ((e_next[1] - ey) - (ahead_y(ex, edge_x) - ex)),
    )


def curl_h(h, h_last, edge_x=0.0, edge_z=0.0):
    hx, hy, hz = h
    return (
        (hz - behind_y(hz, edge_z)) - (hy - behind_z(hy)),
        (hx - behind_z(hx)) - (hz - h_last[2]),
        (hy - h_last[1]) - (hx - behind_y(hx, edge_x)),
    )


def half_over_eps(d):
    return COURANT / (1.0 + (EPS_MATERIAL - 1.0) * d)


def step_inner(n, r, block, e, h, p, q, d, h_out, e_out, c_out, t_out):
    def plane(ref, x, c=None):
        at = pl.ds(pl.multiple_of(x * r, r), r)
        return ref[at, :] if c is None else ref[c, at, :]

    def put(ref, x, v, c=None):
        at = pl.ds(pl.multiple_of(x * r, r), r)
        if c is None:
            ref[at, :] = v
        else:
            ref[c, at, :] = v

    def one(x, last):
        now = [plane(e, x, c) for c in range(3)]
        nxt = [plane(e, jnp.minimum(x + 1, n - 1), c) for c in range(3)]
        mine = new_h([plane(h, x, c) for c in range(3)], now, nxt)
        dd = plane(d, x)
        half = half_over_eps(dd)
        put(c_out, x + 1, half)
        curl = curl_h(mine, last)
        for c in range(3):
            old = plane(p, x, c)
            rate = DAMPING * plane(q, x, c) - OMEGA_SQUARED * old + (OMEGA_SQUARED * LORENTZ_STRENGTH) * dd * now[c]
            put(t_out, x, (DAMPING - OMEGA_SQUARED) * rate - OMEGA_SQUARED * old, c)
            put(h_out, x + 1, mine[c], c)
            put(e_out, x + 1, now[c] + half * (curl[c] - 2.0 * rate), c)
        return mine

    def body(i, last):
        for k in range(block):
            last = one(i * block + k, last)
        return last

    zero = jnp.zeros((r, e.shape[-1]), jnp.float32)
    lax.fori_loop(0, n // block, body, (zero, zero, zero))


def step_edges(n, r, e, h, p, q, d, even, odd, h_in, e_in, c_in, h_out, e_out, c_out, rows_out, even_y, odd_y_out):
    del h_in, e_in, c_in
    flip = odd_x()
    below, above, _, _ = edges()

    def lo(slot):
        at = slice(slot * r, (slot + 1) * r)
        return keep(below, jnp.where(flip, even[at, :], odd[at, :]))

    def hi(slot):
        at = slice(slot * r, (slot + 1) * r)
        return keep(above, jnp.where(flip, odd[at, :], even[at, :]))

    def own(ref, x):
        return [ref[c, x * r : (x + 1) * r, :] for c in range(3)]

    def at(x):
        return slice((x + 1) * r, (x + 2) * r)

    e_m2, e_m1 = [lo(10), lo(11), lo(12)], [lo(0), lo(1), lo(2)]
    e_n, e_n1 = [hi(0), hi(1), hi(2)], [hi(10), hi(11), hi(12)]
    e_0, e_l = own(e, 0), own(e, n - 1)
    h_m2 = new_h([lo(13), lo(13), lo(14)], e_m2, e_m1)
    h_m1 = [keep(below, v) for v in new_h([lo(3), lo(4), lo(5)], e_m1, e_0)]
    h_l = new_h(own(h, n - 1), e_l, e_n)
    h_n = new_h([hi(3), hi(4), hi(5)], e_n, e_n1)
    h_0 = [h_out[c, at(0), :] for c in range(3)]
    h_l1 = [h_out[c, at(n - 2), :] for c in range(3)]

    def new_e(x, electric, magnetic, last, drift, density, flag=None):
        half = half_over_eps(density)
        if flag is not None:
            half = keep(flag, half)
            c_out[at(x), :] = half
        curl = curl_h(magnetic, last)
        for c in range(3):
            rate = drift[c] + (OMEGA_SQUARED * LORENTZ_STRENGTH) * density * electric[c]
            e_out[c, at(x), :] = electric[c] + half * (curl[c] - 2.0 * rate)

    def drift(x):
        return [DAMPING * b - OMEGA_SQUARED * a for a, b in zip(own(p, x), own(q, x))]

    for c in range(3):
        h_out[c, at(-1), :] = h_m1[c]
        h_out[c, at(n - 1), :] = h_l[c]
        h_out[c, at(n), :] = h_n[c]
    new_e(-1, e_m1, h_m1, h_m2, [lo(6), lo(7), lo(8)], lo(9), below)
    new_e(0, e_0, h_0, h_m1, drift(0), d[:r, :])
    new_e(n - 1, e_l, h_l, h_l1, drift(n - 1), d[(n - 1) * r :, :])
    new_e(n, e_n, h_n, h_l, [hi(6), hi(7), hi(8)], hi(9), above)

    for k, c in enumerate((0, 2)):
        rows_out[k, BASE - 1 : BASE, :] = e_m1[c][:1]
        rows_out[k, BASE : BASE + n, :] = e[c, pl.ds(0, n, stride=r), :]
        rows_out[k, BASE + n : BASE + n + 1, :] = e_n[c][:1]

    def row(ref, y, first, c=None):
        start = (first + 1) * r + y
        if c is None:
            return ref[pl.ds(start, n, stride=r), :]
        return ref[c, pl.ds(start, n, stride=r), :]

    last = r - 1
    g_x, g_z = row(h_out, last, 0, 0), row(h_out, last, 0, 2)
    a_x, a_y, a_y1, a_z = (row(e_out, last, 0, 0), row(e_out, last, 0, 1), row(e_out, last, 1, 1), row(e_out, last, 0, 2))
    up = [
        g_x,
        g_z,
        g_x + COURANT * a_z + COURANT * (ahead_z(a_y) - a_y),
        g_z - COURANT * (a_y1 - a_y) - COURANT * a_x,
        row(c_out, last, 0),
    ]
    down = [row(e_out, 0, 0, 0), row(e_out, 0, 0, 2), row(c_out, 0, 0), rows_out[0, BASE : BASE + n, :], rows_out[1, BASE : BASE + n, :]]
    flip_y = odd_y()
    for k in range(5):
        even_y[k * n : (k + 1) * n, :] = jnp.where(flip_y, down[k], up[k])
        odd_y_out[k * n : (k + 1) * n, :] = jnp.where(flip_y, up[k], down[k])
    up_more = [
        h_m1[0][last:],
        h_n[0][last:],
        h_m1[2][last:],
        c_out[(n + 1) * r + last : (n + 1) * r + last + 1, :],
    ]
    down_more = [
        e_out[0, 0:1, :],
        c_out[0:1, :],
        e_m2[0][:1],
        e_m1[0][:1],
        e_m1[2][:1],
        e_n[0][:1],
        e_n[2][:1],
    ]
    zero = jnp.zeros_like(up_more[0])
    for k in range(EXTRA):
        u = up_more[k] if k < len(up_more) else zero
        v = down_more[k] if k < len(down_more) else zero
        even_y[5 * n + k : 5 * n + k + 1, :] = jnp.where(flip_y, v, u)
        odd_y_out[5 * n + k : 5 * n + k + 1, :] = jnp.where(flip_y, u, v)


def step_last(n, r, block, h, e, c_ref, t, d, rows, even, odd, f, e_out, h_out, g_out, edge_out, hs, es, fix, h_edge):
    flip = odd_y()
    below, above, low, high = edges()
    hxm, hzm, dx, dz, ry, exp_, ezp, hxm2, hzm2, wm = range(10)
    last = r - 1

    def up(k, size=None):
        start, size = (k * n, n) if size is None else (5 * n + k, 1)
        return keep(low, jnp.where(flip, even[start : start + size, :], odd[start : start + size, :]))

    def down(k, size=None):
        start, size = (k * n, n) if size is None else (5 * n + k, 1)
        return keep(high, jnp.where(flip, odd[start : start + size, :], even[start : start + size, :]))

    def put(which, v, x=0):
        fix[which, BASE + x : BASE + x + v.shape[0], :] = v

    def get(which, x=0, size=n):
        return fix[which, BASE + x : BASE + x + size, :]

    def row_e(k, x=0, size=n):
        return rows[k, BASE + x : BASE + x + size, :]

    def strided(ref, y, c, x=0):
        return ref[c, pl.ds((x + 1) * r + y, n, stride=r), :]

    put(hxm, up(0) - COURANT * keep(low, row_e(1)))
    put(hxm, up(0, 1) - COURANT * keep(low, row_e(1, -1, 1)), -1)
    put(hxm, up(1, 1) - COURANT * keep(low, row_e(1, n, 1)), n)
    put(hzm, up(1) + COURANT * keep(low, row_e(0)))
    put(hzm, up(2, 1) + COURANT * keep(low, row_e(0, -1, 1)), -1)
    put(hzm, jnp.zeros((1, hs.shape[-1]), jnp.float32), n)
    put(dz, COURANT * down(3))
    put(dz, COURANT * down(2, 1), -2)
    put(dz, COURANT * down(3, 1), -1)
    put(dz, COURANT * down(5, 1), n)
    put(dx, -COURANT * down(4))
    put(dx, -COURANT * down(4, 1), -1)
    put(dx, -COURANT * down(6, 1), n)
    for x, size in ((0, n), (-1, 1), (n, 1)):
        delta = get(dx, x, size)
        put(ry, delta - behind_z(delta) - get(dz, x, size) + get(dz, x - 1, size), x)

    shape = (r, hs.shape[-1])
    first_row, last_row = rows_of(shape) == 0, rows_of(shape) == last

    def spread(which, x):
        return fix[which, pl.ds(BASE + x, 1), :]

    def amend(x):
        at = pl.ds(pl.multiple_of((x + 1) * r, r), r)
        half = c_ref[at, :]
        d_x, d_z = jnp.where(last_row, spread(dx, x), 0.0), jnp.where(last_row, spread(dz, x), 0.0)
        hs[0, at, :] = h[0, at, :] + d_x
        hs[1, at, :] = h[1, at, :]
        hs[2, at, :] = h[2, at, :] + d_z
        es[0, at, :] = e[0, at, :] + half * jnp.where(first_row, -spread(hzm, x), d_z)
        es[1, at, :] = e[1, at, :] + half * jnp.where(last_row, spread(ry, x), 0.0)
        es[2, at, :] = e[2, at, :] + half * jnp.where(first_row, spread(hxm, x), -d_x)

    def amend_block(i, carry):
        for k in range(block):
            amend(i * block + k)
        return carry

    amend(-1)
    amend(n)
    lax.fori_loop(0, n // block, amend_block, 0)

    half = down(2)
    put(exp_, down(0) - half * strided(hs, last, 2))
    put(exp_, down(0, 1) - down(1, 1) * hs[2, last : last + 1, :], -1)
    put(ezp, down(1) + half * strided(hs, last, 0))
    half = up(4)

    def gain(x, size, factor):
        delta = -COURANT * row_e(1, x, size)
        step = COURANT * (row_e(0, x, size) - row_e(0, x - 1, size))
        return factor * (delta - behind_z(delta) - step)

    put(wm, gain(0, n, half))
    put(wm, gain(n, 1, up(3, 1)), n)
    delta_x, delta_z = -COURANT * row_e(1), COURANT * row_e(0)
    change = get(wm)
    put(
        hxm2,
        keep(
            low,
            up(2) + delta_x - COURANT * half * delta_x + COURANT * (ahead_z(change) - change) - COURANT * strided(es, 0, 2),
        ),
    )
    put(
        hzm2,
        keep(
            low,
            up(3) + delta_z - COURANT * (get(wm, 1) - change) - COURANT * half * delta_z + COURANT * strided(es, 0, 0),
        ),
    )

    def fields(ref, x):
        at = pl.ds(pl.multiple_of((x + 1) * r, r), r)
        return [ref[c, at, :] for c in range(3)]

    def second_h(x):
        return new_h(fields(hs, x), fields(es, x), fields(es, x + 1), spread(exp_, x), spread(ezp, x))

    def one(x, last_h):
        now = fields(es, x)
        mine = second_h(x)
        at = pl.ds(pl.multiple_of(x * r, r), r)
        half = c_ref[pl.ds(pl.multiple_of((x + 1) * r, r), r), :]
        dd = d[at, :]
        curl = curl_h(mine, last_h, spread(hxm2, x), spread(hzm2, x))
        total = None
        for c in range(3):
            rate = t[c, at, :] + (OMEGA_SQUARED * LORENTZ_STRENGTH) * dd * now[c]
            after = now[c] + half * (curl[c] - 2.0 * rate)
            e_out[c, at, :] = after
            h_out[c, at, :] = mine[c]
            part = now[c] * f[c, at, :] + after * f[3 + c, at, :]
            total = part if total is None else total + part
        g_out[at, :] = total
        return mine

    def body(i, last_h):
        for k in range(block):
            last_h = one(i * block + k, last_h)
        return last_h

    start = tuple(keep(below, v) for v in second_h(-1))
    lax.fori_loop(0, n // block, body, start)
    first = jnp.where(odd_x(), 0, n - WIDTH)
    edge_out[...] = g_out[pl.ds(pl.multiple_of(first * r, r), WIDTH * r), :]


def update(n, r, generic, *refs):
    if generic:
        g, other, edge, edge_m, far, far_m, d, m, even, odd, order, u_out, even_y, odd_y_out, u_pad = refs
    else:
        g, other, edge, edge_m, d, m, even, odd, order, u_out, even_y, odd_y_out, u_pad = refs
    flip = odd_x()
    below, above, _, _ = edges()
    perm = order[...]

    def paired(v):
        return jnp.take_along_axis(v, perm, axis=0, mode="promise_in_bounds")

    def plane(ref, x):
        return ref[pl.ds(pl.multiple_of(x * r, r), r), :]

    def put(k, v):
        at = pl.ds(pl.multiple_of(k * r, r), r)
        u_out[at, :] = v
        u_pad[at, :] = v

    scale = 0.5 * UPDATE_STEP
    for x in range(n):
        put(x + WIDTH, plane(d, x) - scale * plane(m, x).astype(jnp.float32) * (plane(g, x) + paired(plane(other, n - 1 - x))))
    slots = (9, 15, 16)
    for j in range(WIDTH):
        high, low = n + WIDTH + j, WIDTH - 1 - j
        back, forth = jnp.where(flip, j, WIDTH - 1 - j), jnp.where(flip, WIDTH - 1 - j, j)
        u = plane(even, slots[j]) - scale * plane(even, 17 + j) * (plane(edge, forth) + paired(plane(edge_m, back)))
        put(jnp.where(flip, low, high), u)
        if generic:
            near, mirrored = plane(far, back), plane(far_m, forth)
        else:
            near = plane(other, jnp.where(flip, j, n - 1 - j))
            mirrored = plane(g, jnp.where(flip, n - 1 - j, j))
        u = plane(odd, slots[j]) - scale * plane(odd, 17 + j) * (near + paired(mirrored))
        put(jnp.where(flip, high, low), keep(jnp.where(flip, above, below), u))
    flip_y = odd_y()
    wide = u_pad.shape[0] // r
    for j in range(WIDTH):
        upper = u_pad[pl.ds(r - WIDTH + j, wide, stride=r), :]
        lower = u_pad[pl.ds(j, wide, stride=r), :]
        at = slice(j * wide, (j + 1) * wide)
        even_y[at, :] = jnp.where(flip_y, lower, upper)
        odd_y_out[at, :] = jnp.where(flip_y, upper, lower)


CLASSES = (
    (0.0, ((0, 0),)),
    (1.0, ((0, 1), (1, 0))),
    (2.0, ((1, 1),)),
    (4.0, ((2, 0), (0, 2))),
    (5.0, ((2, 1), (1, 2))),
    (8.0, ((2, 2),)),
    (9.0, ((3, 0), (0, 3))),
    (10.0, ((3, 1), (1, 3))),
    (13.0, ((3, 2), (2, 3))),
    (18.0, ((3, 3),)),
)


def weight(radius, square):
    return jnp.maximum(radius - math.sqrt(square), 0.0)


def cover(n, r, radius, out):
    x0, y0 = lax.axis_index("gx") * n, lax.axis_index("gy") * r
    total_x, total_y = n * lax.axis_size("gx"), r * lax.axis_size("gy")
    shape = (r, out.shape[-1])
    y = y0 + rows_of(shape)
    one = jnp.ones(shape, jnp.float32)

    def there(where, total):
        return ((where >= 0) & (where < total)).astype(jnp.float32)

    across = [one] + [there(y - b, total_y) + there(y + b, total_y) for b in range(1, RMAX)]

    def body(x, carry):
        at = pl.ds(pl.multiple_of(x * r, r), r)
        rad = radius[at, :]
        where = jnp.full(shape, x0 + x, jnp.int32)
        along = [one] + [there(where - a, total_x) + there(where + a, total_x) for a in range(1, RMAX)]
        total = None
        for square, members in CLASSES:
            part = sum(across[b] * along[a] for b, a in members)
            part = weight(rad, square) * part
            total = part if total is None else total + part
        out[at, :] = 1.0 / total
        return carry

    lax.fori_loop(0, n, body, 0)


def smooth(n, r, block, u, even, odd, radius, inverse, out, halo, sums):
    flip = odd_y()
    _, _, low, high = edges()
    wide = even.shape[0] // WIDTH
    full = n + 2 * WIDTH
    for j in range(WIDTH):
        at = slice(j * wide, (j + 1) * wide)
        lower = keep(low, jnp.where(flip, even[at, :], odd[at, :]))
        upper = keep(high, jnp.where(flip, odd[at, :], even[at, :]))
        halo[pl.ds(r - WIDTH + j, wide, stride=r), :] = lower
        halo[pl.ds(j, wide, stride=r), :] = upper
    shape = (r, u.shape[-1])
    row = rows_of(shape)

    def fold(k):
        at = pl.ds(pl.multiple_of(k * r, r), r)
        mine, beside = u[at, :], halo[at, :]
        for b in range(1, RMAX):
            upper = pltpu.roll(jnp.where(row < b, beside, mine), r - b, 0)
            lower = pltpu.roll(jnp.where(row >= r - b, beside, mine), b, 0)
            sums[b - 1, at, :] = upper + lower

    def fold_block(i, carry):
        for k in range(block):
            fold(i * block + k)
        return carry

    whole = full // block
    lax.fori_loop(0, whole, fold_block, 0)
    for k in range(whole * block, full):
        fold(k)

    top = math.tanh(SHARPNESS * THRESHOLD)
    bottom = top + math.tanh(SHARPNESS * (1.0 - THRESHOLD))

    def one(x):
        at = pl.ds(pl.multiple_of(x * r, r), r)
        rad = radius[at, :]

        def line(b, a):
            where = pl.ds(pl.multiple_of((x + WIDTH + a) * r, r), r)
            return u[where, :] if b == 0 else sums[b - 1, where, :]

        total = None
        for square, members in CLASSES:
            part = None
            for b, a in members:
                v = line(b, 0) if a == 0 else line(b, a) + line(b, -a)
                part = v if part is None else part + v
            part = weight(rad, square) * part
            total = part if total is None else total + part
        filtered = total * inverse[at, :]
        out[at, :] = (top + jnp.tanh(SHARPNESS * (filtered - THRESHOLD))) / bottom

    def body(i, carry):
        for k in range(block):
            one(i * block + k)
        return carry

    lax.fori_loop(0, n // block, body, 0)


def local(
    adj_electric,
    adj_magnetic,
    polarization,
    pol_rate,
    density,
    forward_rate,
    design_mask,
    partner_rows,
    filter_radius,
):
    n, r, depth = density.shape
    size = n * r
    e, h = adj_electric.reshape(3, size, depth), adj_magnetic.reshape(3, size, depth)
    p, q = polarization.reshape(3, size, depth), pol_rate.reshape(3, size, depth)
    d, m = density.reshape(size, depth), design_mask.reshape(size, depth)
    f = forward_rate.reshape(3 * STEPS, size, depth)
    more = size + 2 * r
    face_x = (SLOTS * r, depth)
    face_y = (5 * n + EXTRA, depth)
    lines = n + 2 * BASE

    pack = functools.partial(pack_x, n, r)
    even, odd = call(pack, [face_x] * 2, [e, h, p, q, d, m])
    odd = send(odd, x_odd)
    even = send(even, x_even)

    inner = functools.partial(step_inner, n, r, 4)
    h1, e1, c1, t1 = call(inner, [(3, more, depth)] * 2 + [(more, depth), (3, size, depth)], [e, h, p, q, d], flops=100 * size * depth)
    ends = functools.partial(step_edges, n, r)
    h1, e1, c1, rows, even_y, odd_y_ = call(
        ends,
        [(3, more, depth)] * 2 + [(more, depth), (2, lines, depth)] + [face_y] * 2,
        [e, h, p, q, d, even, odd, h1, e1, c1],
        aliases={7: 0, 8: 1, 9: 2},
    )
    odd_y_ = send(odd_y_, y_odd)
    even_y = send(even_y, y_even)

    radius = jnp.broadcast_to(filter_radius.astype(jnp.float32)[:, :, None], (n, r, depth)).reshape(size, depth)
    order = jnp.broadcast_to(partner_rows[:, None], (r, depth))
    (inverse,) = call(functools.partial(cover, n, r), [(size, depth)], [radius], flops=100 * size * depth)

    final = functools.partial(step_last, n, r, 4)
    args = [h1, e1, c1, t1, d, rows, even_y, odd_y_, f]
    e2, h2, g, edge = step_call(final, n, r, depth, args)
    other = send(g, mirror)
    edge_m = send(edge, mirror_even)
    edge_e = send(edge, x_even)
    generic = lax.axis_size("gx") != 4
    extra = []
    if generic:
        start = jnp.where(lax.axis_index("gx") % 2 == 1, (n - WIDTH) * r, 0)
        far = lax.dynamic_slice_in_dim(g, start, WIDTH * r, 0)
        extra = [send(far, x_odd), send(far, mirror_odd)]
    full = n + 2 * WIDTH
    wide = -(-full // 8) * 8
    u, even_u, odd_u = scratch_call(
        functools.partial(update, n, r, generic),
        [(full * r, depth), (WIDTH * wide, depth), (WIDTH * wide, depth)],
        [g, other, edge_e, edge_m] + extra + [d, m, even, odd, order],
        [VMEM((wide * r, depth), jnp.float32)],
    )
    odd_u = send(odd_u, y_odd)
    even_u = send(even_u, y_even)
    (out,) = scratch_call(
        functools.partial(smooth, n, r, 4),
        [(size, depth)],
        [u, even_u, odd_u, radius, inverse],
        [VMEM((wide * r, depth), jnp.float32), VMEM((WIDTH, full * r, depth), jnp.float32)],
    )
    return (
        e2.reshape(3, n, r, depth),
        h2.reshape(3, n, r, depth),
        out.reshape(n, r, depth),
    )


def scratch_call(kernel, outs, args, scratch):
    args = [pltpu.with_memory_space_constraint(a, VMEM) for a in args]
    spec = pl.BlockSpec(memory_space=VMEM)
    return pl.pallas_call(
        kernel,
        out_shape=tuple(VMEM(s, jnp.float32) for s in outs),
        in_specs=[spec] * len(args),
        out_specs=tuple([spec] * len(outs)),
        scratch_shapes=scratch,
        compiler_params=pltpu.CompilerParams(vmem_limit_bytes=16 * 2**20),
    )(*args)


def step_call(kernel, n, r, depth, args):
    more = (3, (n + 2) * r, depth)
    scratch = [VMEM(more, jnp.float32)] * 2 + [VMEM((10, n + 2 * BASE, depth), jnp.float32), VMEM((2, r, depth), jnp.float32)]
    size = (3, n * r, depth)
    return scratch_call(kernel, [size, size, (n * r, depth), (WIDTH * r, depth)], args, scratch)


def solution(mesh):
    in_specs = (
        P(None, "gx", "gy", None),
        P(None, "gx", "gy", None),
        P(None, "gx", "gy", None),
        P(None, "gx", "gy", None),
        P("gx", "gy", None),
        P(None, None, "gx", "gy", None),
        P("gx", "gy", None),
        P("gy"),
        P("gx", "gy"),
    )
    out_specs = (P(None, "gx", "gy", None), P(None, "gx", "gy", None), P("gx", "gy", None))
    return jax.shard_map(local, mesh=mesh, in_specs=in_specs, out_specs=out_specs, check_vma=False)
```

```python
import functools
import math

import jax
import jax.numpy as jnp
from jax import lax
from jax.experimental import pallas as pl
from jax.experimental.pallas import tpu as pltpu
from jax.sharding import PartitionSpec as P

STEPS = 2
RMAX = 4

COURANT = 0.5
DAMPING = 0.9
OMEGA_SQUARED = 0.3
LORENTZ_STRENGTH = 2.0
EPS_MATERIAL = 4.0
UPDATE_STEP = 0.25
SHARPNESS = 4.0
THRESHOLD = 0.5

AXES = ("gx", "gy")
WIDTH = RMAX - 1
SLOTS = 20
BASE = 8
EXTRA = 8
VMEM = pltpu.VMEM


def x_even(x, y, nx, ny):
    return x ^ 1, y


def x_odd(x, y, nx, ny):
    other = x + 1 if x % 2 else x - 1
    return (other, y) if 0 <= other < nx else (x, y ^ 1)


def y_even(x, y, nx, ny):
    return x, y ^ 1


def y_odd(x, y, nx, ny):
    other = y + 1 if y % 2 else y - 1
    return (x, other) if 0 <= other < ny else (x ^ 1, y)


def mirror(x, y, nx, ny):
    return nx - 1 - x, y


def mirror_even(x, y, nx, ny):
    return nx - 1 - (x ^ 1), y


def mirror_odd(x, y, nx, ny):
    other = x + 1 if x % 2 else x - 1
    return (nx - 1 - other, y) if 0 <= other < nx else (nx - 1 - x, y)


def send(block, rule):
    nx, ny = lax.axis_size("gx"), lax.axis_size("gy")
    route = []
    for x in range(nx):
        for y in range(ny):
            to_x, to_y = rule(x, y, nx, ny)
            route.append((x * ny + y, to_x * ny + to_y))
    return lax.ppermute(block, AXES, route)


def odd_x():
    return lax.rem(lax.axis_index("gx"), 2) == 1


def odd_y():
    return lax.rem(lax.axis_index("gy"), 2) == 1


def edges():
    x, y = lax.axis_index("gx"), lax.axis_index("gy")
    return (x > 0, x < lax.axis_size("gx") - 1, y > 0, y < lax.axis_size("gy") - 1)


def rows_of(shape):
    return lax.broadcasted_iota(jnp.int32, shape, len(shape) - 2)


def lanes_of(shape):
    return lax.broadcasted_iota(jnp.int32, shape, len(shape) - 1)


def ahead_z(v):
    depth = v.shape[-1]
    return jnp.where(lanes_of(v.shape) == depth - 1, 0.0, pltpu.roll(v, depth - 1, v.ndim - 1))


def behind_z(v):
    return jnp.where(lanes_of(v.shape) == 0, 0.0, pltpu.roll(v, 1, v.ndim - 1))


def ahead_y(v, edge=0.0):
    rows = v.shape[-2]
    return jnp.where(rows_of(v.shape) == rows - 1, edge, pltpu.roll(v, rows - 1, v.ndim - 2))


def behind_y(v, edge=0.0):
    return jnp.where(rows_of(v.shape) == 0, edge, pltpu.roll(v, 1, v.ndim - 2))


def keep(flag, v):
    return jnp.where(flag, v, 0.0)


def call(kernel, outs, args, aliases=None, flops=0):
    args = [a if m is pltpu.SMEM else pltpu.with_memory_space_constraint(a, VMEM) for a, m in [(a, VMEM) for a in args]]
    shapes = tuple(VMEM(s, jnp.float32) for s in outs)
    spec = pl.BlockSpec(memory_space=VMEM)
    traffic = 4 * (sum(math.prod(s) for s in outs) + sum(math.prod(a.shape) for a in args))
    return pl.pallas_call(
        kernel,
        out_shape=shapes,
        in_specs=[spec] * len(args),
        out_specs=tuple([spec] * len(outs)),
        input_output_aliases=aliases or {},
        cost_estimate=pl.CostEstimate(flops=flops, bytes_accessed=traffic, transcendentals=0),
        compiler_params=pltpu.CompilerParams(vmem_limit_bytes=16 * 2**20),
    )(*args)


def pack_x(n, r, e, h, p, q, d, m, even_out, odd_out, e_at, h_at, p_at, q_at, d_at, m_at, sems):
    copies = []
    for end in range(2):
        for k, (ref, held, planes) in enumerate(
            ((e, e_at, 2), (h, h_at, 2), (p, p_at, 1), (q, q_at, 1), (d, d_at, WIDTH), (m, m_at, WIDTH))
        ):
            rows = pl.ds((n - planes) * r if end else 0, planes * r)
            src = ref.at[:, rows, :] if len(ref.shape) == 3 else ref.at[rows, :]
            copies.append(pltpu.make_async_copy(src, held.at[end], sems.at[end, k]))
    for copy in copies:
        copy.start()
    for copy in copies:
        copy.wait()
    odd = odd_x()

    def take(ref, planes, k, c=None):
        low, high = slice(k * r, (k + 1) * r), slice((planes - 1 - k) * r, (planes - k) * r)
        if c is None:
            return ref[0, low, :], ref[1, high, :]
        return ref[0, c, low, :], ref[1, c, high, :]

    def put(slot, pair):
        at = slice(slot * r, (slot + 1) * r)
        even_out[at, :] = jnp.where(odd, pair[0], pair[1])
        odd_out[at, :] = jnp.where(odd, pair[1], pair[0])

    for c in range(3):
        put(c, take(e_at, 2, 0, c))
        put(3 + c, take(h_at, 2, 0, c))
        put(6 + c, [DAMPING * b - OMEGA_SQUARED * a for a, b in zip(take(p_at, 1, 0, c), take(q_at, 1, 0, c))])
        put(10 + c, take(e_at, 2, 1, c))
    put(9, take(d_at, WIDTH, 0))
    put(13, take(h_at, 2, 1, 1))
    put(14, take(h_at, 2, 1, 2))
    put(15, take(d_at, WIDTH, 1))
    put(16, take(d_at, WIDTH, 2))
    for k in range(WIDTH):
        put(17 + k, [v.astype(jnp.float32) for v in take(m_at, WIDTH, k)])


def new_h(h, e, e_next, edge_x=0.0, edge_z=0.0):
    ex, ey, ez = e
    return (
        h[0] - COURANT * ((ahead_y(ez, edge_z) - ez) - (ahead_z(ey) - ey)),
        h[1] - COURANT * ((ahead_z(ex) - ex) - (e_next[2] - ez)),
        h[2] - COURANT * ((e_next[1] - ey) - (ahead_y(ex, edge_x) - ex)),
    )


def curl_h(h, h_last, edge_x=0.0, edge_z=0.0):
    hx, hy, hz = h
    return (
        (hz - behind_y(hz, edge_z)) - (hy - behind_z(hy)),
        (hx - behind_z(hx)) - (hz - h_last[2]),
        (hy - h_last[1]) - (hx - behind_y(hx, edge_x)),
    )


def half_over_eps(d):
    return COURANT / (1.0 + (EPS_MATERIAL - 1.0) * d)


def step_inner(n, r, block, e, h, p, q, d, h_out, e_out, c_out, t_out):
    def plane(ref, x, c=None):
        at = pl.ds(pl.multiple_of(x * r, r), r)
        return ref[at, :] if c is None else ref[c, at, :]

    def put(ref, x, v, c=None):
        at = pl.ds(pl.multiple_of(x * r, r), r)
        if c is None:
            ref[at, :] = v
        else:
            ref[c, at, :] = v

    def one(x, last):
        now = [plane(e, x, c) for c in range(3)]
        nxt = [plane(e, jnp.minimum(x + 1, n - 1), c) for c in range(3)]
        mine = new_h([plane(h, x, c) for c in range(3)], now, nxt)
        dd = plane(d, x)
        half = half_over_eps(dd)
        put(c_out, x + 1, half)
        curl = curl_h(mine, last)
        for c in range(3):
            old = plane(p, x, c)
            rate = DAMPING * plane(q, x, c) - OMEGA_SQUARED * old + (OMEGA_SQUARED * LORENTZ_STRENGTH) * dd * now[c]
            put(t_out, x, (DAMPING - OMEGA_SQUARED) * rate - OMEGA_SQUARED * old, c)
            put(h_out, x + 1, mine[c], c)
            put(e_out, x + 1, now[c] + half * (curl[c] - 2.0 * rate), c)
        return mine

    def body(i, last):
        for k in range(block):
            last = one(i * block + k, last)
        return last

    zero = jnp.zeros((r, e.shape[-1]), jnp.float32)
    lax.fori_loop(0, n // block, body, (zero, zero, zero))


def step_edges(n, r, e, h, p, q, d, even, odd, h_in, e_in, c_in, h_out, e_out, c_out, rows_out, even_y, odd_y_out):
    del h_in, e_in, c_in
    flip = odd_x()
    below, above, _, _ = edges()

    def lo(slot):
        at = slice(slot * r, (slot + 1) * r)
        return keep(below, jnp.where(flip, even[at, :], odd[at, :]))

    def hi(slot):
        at = slice(slot * r, (slot + 1) * r)
        return keep(above, jnp.where(flip, odd[at, :], even[at, :]))

    def own(ref, x):
        return [ref[c, x * r : (x + 1) * r, :] for c in range(3)]

    def at(x):
        return slice((x + 1) * r, (x + 2) * r)

    e_m2, e_m1 = [lo(10), lo(11), lo(12)], [lo(0), lo(1), lo(2)]
    e_n, e_n1 = [hi(0), hi(1), hi(2)], [hi(10), hi(11), hi(12)]
    e_0, e_l = own(e, 0), own(e, n - 1)
    h_m2 = new_h([lo(13), lo(13), lo(14)], e_m2, e_m1)
    h_m1 = [keep(below, v) for v in new_h([lo(3), lo(4), lo(5)], e_m1, e_0)]
    h_l = new_h(own(h, n - 1), e_l, e_n)
    h_n = new_h([hi(3), hi(4), hi(5)], e_n, e_n1)
    h_0 = [h_out[c, at(0), :] for c in range(3)]
    h_l1 = [h_out[c, at(n - 2), :] for c in range(3)]

    def new_e(x, electric, magnetic, last, drift, density, flag=None):
        half = half_over_eps(density)
        if flag is not None:
            half = keep(flag, half)
            c_out[at(x), :] = half
        curl = curl_h(magnetic, last)
        for c in range(3):
            rate = drift[c] + (OMEGA_SQUARED * LORENTZ_STRENGTH) * density * electric[c]
            e_out[c, at(x), :] = electric[c] + half * (curl[c] - 2.0 * rate)

    def drift(x):
        return [DAMPING * b - OMEGA_SQUARED * a for a, b in zip(own(p, x), own(q, x))]

    for c in range(3):
        h_out[c, at(-1), :] = h_m1[c]
        h_out[c, at(n - 1), :] = h_l[c]
        h_out[c, at(n), :] = h_n[c]
    new_e(-1, e_m1, h_m1, h_m2, [lo(6), lo(7), lo(8)], lo(9), below)
    new_e(0, e_0, h_0, h_m1, drift(0), d[:r, :])
    new_e(n - 1, e_l, h_l, h_l1, drift(n - 1), d[(n - 1) * r :, :])
    new_e(n, e_n, h_n, h_l, [hi(6), hi(7), hi(8)], hi(9), above)

    for k, c in enumerate((0, 2)):
        rows_out[k, BASE - 1 : BASE, :] = e_m1[c][:1]
        rows_out[k, BASE : BASE + n, :] = e[c, pl.ds(0, n, stride=r), :]
        rows_out[k, BASE + n : BASE + n + 1, :] = e_n[c][:1]

    def row(ref, y, first, c=None):
        start = (first + 1) * r + y
        if c is None:
            return ref[pl.ds(start, n, stride=r), :]
        return ref[c, pl.ds(start, n, stride=r), :]

    last = r - 1
    g_x, g_z = row(h_out, last, 0, 0), row(h_out, last, 0, 2)
    a_x, a_y, a_y1, a_z = (row(e_out, last, 0, 0), row(e_out, last, 0, 1), row(e_out, last, 1, 1), row(e_out, last, 0, 2))
    up = [
        g_x,
        g_z,
        g_x + COURANT * a_z + COURANT * (ahead_z(a_y) - a_y),
        g_z - COURANT * (a_y1 - a_y) - COURANT * a_x,
        row(c_out, last, 0),
    ]
    down = [row(e_out, 0, 0, 0), row(e_out, 0, 0, 2), row(c_out, 0, 0), rows_out[0, BASE : BASE + n, :], rows_out[1, BASE : BASE + n, :]]
    flip_y = odd_y()
    for k in range(5):
        even_y[k * n : (k + 1) * n, :] = jnp.where(flip_y, down[k], up[k])
        odd_y_out[k * n : (k + 1) * n, :] = jnp.where(flip_y, up[k], down[k])
    up_more = [
        h_m1[0][last:],
        h_n[0][last:],
        h_m1[2][last:],
        c_out[(n + 1) * r + last : (n + 1) * r + last + 1, :],
    ]
    down_more = [
        e_out[0, 0:1, :],
        c_out[0:1, :],
        e_m2[0][:1],
        e_m1[0][:1],
        e_m1[2][:1],
        e_n[0][:1],
        e_n[2][:1],
    ]
    zero = jnp.zeros_like(up_more[0])
    for k in range(EXTRA):
        u = up_more[k] if k < len(up_more) else zero
        v = down_more[k] if k < len(down_more) else zero
        even_y[5 * n + k : 5 * n + k + 1, :] = jnp.where(flip_y, v, u)
        odd_y_out[5 * n + k : 5 * n + k + 1, :] = jnp.where(flip_y, u, v)


def step_last(n, r, block, h, e, c_ref, t, d, rows, even, odd, f, e_out, h_out, g_out, edge_out, hs, es, fix, h_edge):
    flip = odd_y()
    below, above, low, high = edges()
    hxm, hzm, dx, dz, ry, exp_, ezp, hxm2, hzm2, wm = range(10)
    last = r - 1

    def up(k, size=None):
        start, size = (k * n, n) if size is None else (5 * n + k, 1)
        return keep(low, jnp.where(flip, even[start : start + size, :], odd[start : start + size, :]))

    def down(k, size=None):
        start, size = (k * n, n) if size is None else (5 * n + k, 1)
        return keep(high, jnp.where(flip, odd[start : start + size, :], even[start : start + size, :]))

    def put(which, v, x=0):
        fix[which, BASE + x : BASE + x + v.shape[0], :] = v

    def get(which, x=0, size=n):
        return fix[which, BASE + x : BASE + x + size, :]

    def row_e(k, x=0, size=n):
        return rows[k, BASE + x : BASE + x + size, :]

    def strided(ref, y, c, x=0):
        return ref[c, pl.ds((x + 1) * r + y, n, stride=r), :]

    put(hxm, up(0) - COURANT * keep(low, row_e(1)))
    put(hxm, up(0, 1) - COURANT * keep(low, row_e(1, -1, 1)), -1)
    put(hxm, up(1, 1) - COURANT * keep(low, row_e(1, n, 1)), n)
    put(hzm, up(1) + COURANT * keep(low, row_e(0)))
    put(hzm, up(2, 1) + COURANT * keep(low, row_e(0, -1, 1)), -1)
    put(hzm, jnp.zeros((1, hs.shape[-1]), jnp.float32), n)
    put(dz, COURANT * down(3))
    put(dz, COURANT * down(2, 1), -2)
    put(dz, COURANT * down(3, 1), -1)
    put(dz, COURANT * down(5, 1), n)
    put(dx, -COURANT * down(4))
    put(dx, -COURANT * down(4, 1), -1)
    put(dx, -COURANT * down(6, 1), n)
    for x, size in ((0, n), (-1, 1), (n, 1)):
        delta = get(dx, x, size)
        put(ry, delta - behind_z(delta) - get(dz, x, size) + get(dz, x - 1, size), x)

    shape = (r, hs.shape[-1])
    first_row, last_row = rows_of(shape) == 0, rows_of(shape) == last

    def spread(which, x):
        return fix[which, pl.ds(BASE + x, 1), :]

    def amend(x):
        at = pl.ds(pl.multiple_of((x + 1) * r, r), r)
        half = c_ref[at, :]
        d_x, d_z = jnp.where(last_row, spread(dx, x), 0.0), jnp.where(last_row, spread(dz, x), 0.0)
        hs[0, at, :] = h[0, at, :] + d_x
        hs[1, at, :] = h[1, at, :]
        hs[2, at, :] = h[2, at, :] + d_z
        es[0, at, :] = e[0, at, :] + half * jnp.where(first_row, -spread(hzm, x), d_z)
        es[1, at, :] = e[1, at, :] + half * jnp.where(last_row, spread(ry, x), 0.0)
        es[2, at, :] = e[2, at, :] + half * jnp.where(first_row, spread(hxm, x), -d_x)

    def amend_block(i, carry):
        for k in range(block):
            amend(i * block + k)
        return carry

    amend(-1)
    amend(n)
    lax.fori_loop(0, n // block, amend_block, 0)

    half = down(2)
    put(exp_, down(0) - half * strided(hs, last, 2))
    put(exp_, down(0, 1) - down(1, 1) * hs[2, last : last + 1, :], -1)
    put(ezp, down(1) + half * strided(hs, last, 0))
    half = up(4)

    def gain(x, size, factor):
        delta = -COURANT * row_e(1, x, size)
        step = COURANT * (row_e(0, x, size) - row_e(0, x - 1, size))
        return factor * (delta - behind_z(delta) - step)

    put(wm, gain(0, n, half))
    put(wm, gain(n, 1, up(3, 1)), n)
    delta_x, delta_z = -COURANT * row_e(1), COURANT * row_e(0)
    change = get(wm)
    put(
        hxm2,
        keep(
            low,
            up(2) + delta_x - COURANT * half * delta_x + COURANT * (ahead_z(change) - change) - COURANT * strided(es, 0, 2),
        ),
    )
    put(
        hzm2,
        keep(
            low,
            up(3) + delta_z - COURANT * (get(wm, 1) - change) - COURANT * half * delta_z + COURANT * strided(es, 0, 0),
        ),
    )

    def fields(ref, x):
        at = pl.ds(pl.multiple_of((x + 1) * r, r), r)
        return [ref[c, at, :] for c in range(3)]

    def second_h(x):
        return new_h(fields(hs, x), fields(es, x), fields(es, x + 1), spread(exp_, x), spread(ezp, x))

    def one(x, last_h):
        now = fields(es, x)
        mine = second_h(x)
        at = pl.ds(pl.multiple_of(x * r, r), r)
        half = c_ref[pl.ds(pl.multiple_of((x + 1) * r, r), r), :]
        dd = d[at, :]
        curl = curl_h(mine, last_h, spread(hxm2, x), spread(hzm2, x))
        total = None
        for c in range(3):
            rate = t[c, at, :] + (OMEGA_SQUARED * LORENTZ_STRENGTH) * dd * now[c]
            after = now[c] + half * (curl[c] - 2.0 * rate)
            e_out[c, at, :] = after
            h_out[c, at, :] = mine[c]
            part = now[c] * f[c, at, :] + after * f[3 + c, at, :]
            total = part if total is None else total + part
        g_out[at, :] = total
        return mine

    def body(i, last_h):
        for k in range(block):
            last_h = one(i * block + k, last_h)
        return last_h

    start = tuple(keep(below, v) for v in second_h(-1))
    lax.fori_loop(0, n // block, body, start)
    first = jnp.where(odd_x(), 0, n - WIDTH)
    edge_out[...] = g_out[pl.ds(pl.multiple_of(first * r, r), WIDTH * r), :]


def update(n, r, generic, *refs):
    if generic:
        g, other, edge, edge_m, far, far_m, d, m, even, odd, order, u_out, even_y, odd_y_out, u_pad = refs
    else:
        g, other, edge, edge_m, d, m, even, odd, order, u_out, even_y, odd_y_out, u_pad = refs
    flip = odd_x()
    below, above, _, _ = edges()
    perm = order[...]

    def paired(v):
        return jnp.take_along_axis(v, perm, axis=0, mode="promise_in_bounds")

    def plane(ref, x):
        return ref[pl.ds(pl.multiple_of(x * r, r), r), :]

    def put(k, v):
        at = pl.ds(pl.multiple_of(k * r, r), r)
        u_out[at, :] = v
        u_pad[at, :] = v

    scale = 0.5 * UPDATE_STEP
    for x in range(n):
        put(x + WIDTH, plane(d, x) - scale * plane(m, x).astype(jnp.float32) * (plane(g, x) + paired(plane(other, n - 1 - x))))
    slots = (9, 15, 16)
    for j in range(WIDTH):
        high, low = n + WIDTH + j, WIDTH - 1 - j
        back, forth = jnp.where(flip, j, WIDTH - 1 - j), jnp.where(flip, WIDTH - 1 - j, j)
        u = plane(even, slots[j]) - scale * plane(even, 17 + j) * (plane(edge, forth) + paired(plane(edge_m, back)))
        put(jnp.where(flip, low, high), u)
        if generic:
            near, mirrored = plane(far, back), plane(far_m, forth)
        else:
            near = plane(other, jnp.where(flip, j, n - 1 - j))
            mirrored = plane(g, jnp.where(flip, n - 1 - j, j))
        u = plane(odd, slots[j]) - scale * plane(odd, 17 + j) * (near + paired(mirrored))
        put(jnp.where(flip, high, low), keep(jnp.where(flip, above, below), u))
    flip_y = odd_y()
    wide = u_pad.shape[0] // r
    for j in range(WIDTH):
        upper = u_pad[pl.ds(r - WIDTH + j, wide, stride=r), :]
        lower = u_pad[pl.ds(j, wide, stride=r), :]
        at = slice(j * wide, (j + 1) * wide)
        even_y[at, :] = jnp.where(flip_y, lower, upper)
        odd_y_out[at, :] = jnp.where(flip_y, upper, lower)


CLASSES = (
    (0.0, ((0, 0),)),
    (1.0, ((0, 1), (1, 0))),
    (2.0, ((1, 1),)),
    (4.0, ((2, 0), (0, 2))),
    (5.0, ((2, 1), (1, 2))),
    (8.0, ((2, 2),)),
    (9.0, ((3, 0), (0, 3))),
    (10.0, ((3, 1), (1, 3))),
    (13.0, ((3, 2), (2, 3))),
    (18.0, ((3, 3),)),
)


def weight(radius, square):
    return jnp.maximum(radius - math.sqrt(square), 0.0)


def cover(n, r, radius, out):
    x0, y0 = lax.axis_index("gx") * n, lax.axis_index("gy") * r
    total_x, total_y = n * lax.axis_size("gx"), r * lax.axis_size("gy")
    shape = (r, out.shape[-1])
    y = y0 + rows_of(shape)
    one = jnp.ones(shape, jnp.float32)

    def there(where, total):
        return ((where >= 0) & (where < total)).astype(jnp.float32)

    across = [one] + [there(y - b, total_y) + there(y + b, total_y) for b in range(1, RMAX)]

    def body(x, carry):
        at = pl.ds(pl.multiple_of(x * r, r), r)
        rad = radius[at, :]
        where = jnp.full(shape, x0 + x, jnp.int32)
        along = [one] + [there(where - a, total_x) + there(where + a, total_x) for a in range(1, RMAX)]
        total = None
        for square, members in CLASSES:
            part = sum(across[b] * along[a] for b, a in members)
            part = weight(rad, square) * part
            total = part if total is None else total + part
        out[at, :] = 1.0 / total
        return carry

    lax.fori_loop(0, n, body, 0)


def smooth(n, r, block, u, even, odd, radius, inverse, out, halo, sums):
    flip = odd_y()
    _, _, low, high = edges()
    wide = even.shape[0] // WIDTH
    full = n + 2 * WIDTH
    for j in range(WIDTH):
        at = slice(j * wide, (j + 1) * wide)
        lower = keep(low, jnp.where(flip, even[at, :], odd[at, :]))
        upper = keep(high, jnp.where(flip, odd[at, :], even[at, :]))
        halo[pl.ds(r - WIDTH + j, wide, stride=r), :] = lower
        halo[pl.ds(j, wide, stride=r), :] = upper
    shape = (r, u.shape[-1])
    row = rows_of(shape)

    def fold(k):
        at = pl.ds(pl.multiple_of(k * r, r), r)
        mine, beside = u[at, :], halo[at, :]
        for b in range(1, RMAX):
            upper = pltpu.roll(jnp.where(row < b, beside, mine), r - b, 0)
            lower = pltpu.roll(jnp.where(row >= r - b, beside, mine), b, 0)
            sums[b - 1, at, :] = upper + lower

    def fold_block(i, carry):
        for k in range(block):
            fold(i * block + k)
        return carry

    whole = full // block
    lax.fori_loop(0, whole, fold_block, 0)
    for k in range(whole * block, full):
        fold(k)

    top = math.tanh(SHARPNESS * THRESHOLD)
    bottom = top + math.tanh(SHARPNESS * (1.0 - THRESHOLD))

    def one(x):
        at = pl.ds(pl.multiple_of(x * r, r), r)
        rad = radius[at, :]

        def line(b, a):
            where = pl.ds(pl.multiple_of((x + WIDTH + a) * r, r), r)
            return u[where, :] if b == 0 else sums[b - 1, where, :]

        total = None
        for square, members in CLASSES:
            part = None
            for b, a in members:
                v = line(b, 0) if a == 0 else line(b, a) + line(b, -a)
                part = v if part is None else part + v
            part = weight(rad, square) * part
            total = part if total is None else total + part
        filtered = total * inverse[at, :]
        out[at, :] = (top + jnp.tanh(SHARPNESS * (filtered - THRESHOLD))) / bottom

    def body(i, carry):
        for k in range(block):
            one(i * block + k)
        return carry

    lax.fori_loop(0, n // block, body, 0)


def local(
    adj_electric,
    adj_magnetic,
    polarization,
    pol_rate,
    density,
    forward_rate,
    design_mask,
    partner_rows,
    filter_radius,
):
    n, r, depth = density.shape
    size = n * r
    e, h = adj_electric.reshape(3, size, depth), adj_magnetic.reshape(3, size, depth)
    p, q = polarization.reshape(3, size, depth), pol_rate.reshape(3, size, depth)
    d, m = density.reshape(size, depth), design_mask.reshape(size, depth)
    f = forward_rate.reshape(3 * STEPS, size, depth)
    more = size + 2 * r
    face_x = (SLOTS * r, depth)
    face_y = (5 * n + EXTRA, depth)
    lines = n + 2 * BASE

    f32 = jnp.float32
    even, odd = pl.pallas_call(
        functools.partial(pack_x, n, r),
        out_shape=(VMEM(face_x, f32), VMEM(face_x, f32)),
        in_specs=[pl.BlockSpec(memory_space=pl.ANY)] * 6,
        out_specs=(pl.BlockSpec(memory_space=VMEM), pl.BlockSpec(memory_space=VMEM)),
        scratch_shapes=[
            VMEM((2, 3, 2 * r, depth), f32),
            VMEM((2, 3, 2 * r, depth), f32),
            VMEM((2, 3, r, depth), f32),
            VMEM((2, 3, r, depth), f32),
            VMEM((2, WIDTH * r, depth), f32),
            VMEM((2, WIDTH * r, depth), jnp.int32),
            pltpu.SemaphoreType.DMA((2, 6)),
        ],
    )(e, h, p, q, d, m)
    even = send(even, x_even)
    odd = send(odd, x_odd)

    inner = functools.partial(step_inner, n, r, 16)
    h1, e1, c1, t1 = call(inner, [(3, more, depth)] * 2 + [(more, depth), (3, size, depth)], [e, h, p, q, d], flops=100 * size * depth)
    ends = functools.partial(step_edges, n, r)
    h1, e1, c1, rows, even_y, odd_y_ = call(
        ends,
        [(3, more, depth)] * 2 + [(more, depth), (2, lines, depth)] + [face_y] * 2,
        [e, h, p, q, d, even, odd, h1, e1, c1],
        aliases={7: 0, 8: 1, 9: 2},
    )
    odd_y_ = send(odd_y_, y_odd)
    even_y = send(even_y, y_even)

    radius = jnp.broadcast_to(filter_radius.astype(jnp.float32)[:, :, None], (n, r, depth)).reshape(size, depth)
    order = jnp.broadcast_to(partner_rows[:, None], (r, depth))
    (inverse,) = call(functools.partial(cover, n, r), [(size, depth)], [radius], flops=100 * size * depth)

    final = functools.partial(step_last, n, r, 16)
    args = [h1, e1, c1, t1, d, rows, even_y, odd_y_, f]
    e2, h2, g, edge = step_call(final, n, r, depth, args)
    edge_e = send(edge, x_even)
    edge_m = send(edge, mirror_even)
    other = send(g, mirror)
    generic = lax.axis_size("gx") != 4
    extra = []
    if generic:
        start = jnp.where(lax.axis_index("gx") % 2 == 1, (n - WIDTH) * r, 0)
        far = lax.dynamic_slice_in_dim(g, start, WIDTH * r, 0)
        extra = [send(far, x_odd), send(far, mirror_odd)]
    full = n + 2 * WIDTH
    wide = -(-full // 8) * 8
    u, even_u, odd_u = scratch_call(
        functools.partial(update, n, r, generic),
        [(full * r, depth), (WIDTH * wide, depth), (WIDTH * wide, depth)],
        [g, other, edge_e, edge_m] + extra + [d, m, even, odd, order],
        [VMEM((wide * r, depth), jnp.float32)],
    )
    odd_u = send(odd_u, y_odd)
    even_u = send(even_u, y_even)
    (out,) = scratch_call(
        functools.partial(smooth, n, r, 16),
        [(size, depth)],
        [u, even_u, odd_u, radius, inverse],
        [VMEM((wide * r, depth), jnp.float32), VMEM((WIDTH, full * r, depth), jnp.float32)],
    )
    return (
        e2.reshape(3, n, r, depth),
        h2.reshape(3, n, r, depth),
        out.reshape(n, r, depth),
    )


def scratch_call(kernel, outs, args, scratch):
    args = [pltpu.with_memory_space_constraint(a, VMEM) for a in args]
    spec = pl.BlockSpec(memory_space=VMEM)
    return pl.pallas_call(
        kernel,
        out_shape=tuple(VMEM(s, jnp.float32) for s in outs),
        in_specs=[spec] * len(args),
        out_specs=tuple([spec] * len(outs)),
        scratch_shapes=scratch,
        compiler_params=pltpu.CompilerParams(vmem_limit_bytes=16 * 2**20),
    )(*args)


def step_call(kernel, n, r, depth, args):
    more = (3, (n + 2) * r, depth)
    scratch = [VMEM(more, jnp.float32)] * 2 + [VMEM((10, n + 2 * BASE, depth), jnp.float32), VMEM((2, r, depth), jnp.float32)]
    size = (3, n * r, depth)
    return scratch_call(kernel, [size, size, (n * r, depth), (WIDTH * r, depth)], args, scratch)


def solution(mesh):
    in_specs = (
        P(None, "gx", "gy", None),
        P(None, "gx", "gy", None),
        P(None, "gx", "gy", None),
        P(None, "gx", "gy", None),
        P("gx", "gy", None),
        P(None, None, "gx", "gy", None),
        P("gx", "gy", None),
        P("gy"),
        P("gx", "gy"),
    )
    out_specs = (P(None, "gx", "gy", None), P(None, "gx", "gy", None), P("gx", "gy", None))
    return jax.shard_map(local, mesh=mesh, in_specs=in_specs, out_specs=out_specs, check_vma=False)
```

```python
import functools
import math

import jax
import jax.numpy as jnp
from jax import lax
from jax.experimental import pallas as pl
from jax.experimental.pallas import tpu as pltpu
from jax.sharding import PartitionSpec as P

STEPS = 2
RMAX = 4

COURANT = 0.5
DAMPING = 0.9
OMEGA_SQUARED = 0.3
LORENTZ_STRENGTH = 2.0
EPS_MATERIAL = 4.0
UPDATE_STEP = 0.25
SHARPNESS = 4.0
THRESHOLD = 0.5

AXES = ("gx", "gy")
WIDTH = RMAX - 1
SLOTS = 20
BASE = 8
REACH = STEPS
VMEM = pltpu.VMEM


def late_rows(n):
    up = ((0, -1), (0, n), (1, -1), (1, n - 1), (2, 0), (2, n - 1), (3, 0), (3, n - 2), (3, n - 1), (4, n))
    down = ((0, -1), (0, n - 1), (1, 0), (1, n - 1), (2, -1), (3, -2), (3, -1), (3, n), (4, -1), (4, n))
    return up, down


LATE = 16


def x_even(x, y, nx, ny):
    return x ^ 1, y


def x_odd(x, y, nx, ny):
    other = x + 1 if x % 2 else x - 1
    return (other, y) if 0 <= other < nx else (x, y ^ 1)


def y_even(x, y, nx, ny):
    return x, y ^ 1


def y_odd(x, y, nx, ny):
    other = y + 1 if y % 2 else y - 1
    return (x, other) if 0 <= other < ny else (x ^ 1, y)


def mirror(x, y, nx, ny):
    return nx - 1 - x, y


def mirror_even(x, y, nx, ny):
    return nx - 1 - (x ^ 1), y


def mirror_odd(x, y, nx, ny):
    other = x + 1 if x % 2 else x - 1
    return (nx - 1 - other, y) if 0 <= other < nx else (nx - 1 - x, y)


def send(block, rule):
    nx, ny = lax.axis_size("gx"), lax.axis_size("gy")
    route = []
    for x in range(nx):
        for y in range(ny):
            to_x, to_y = rule(x, y, nx, ny)
            route.append((x * ny + y, to_x * ny + to_y))
    return lax.ppermute(block, AXES, route)


def odd_x():
    return lax.rem(lax.axis_index("gx"), 2) == 1


def odd_y():
    return lax.rem(lax.axis_index("gy"), 2) == 1


def edges():
    x, y = lax.axis_index("gx"), lax.axis_index("gy")
    return (x > 0, x < lax.axis_size("gx") - 1, y > 0, y < lax.axis_size("gy") - 1)


def rows_of(shape):
    return lax.broadcasted_iota(jnp.int32, shape, len(shape) - 2)


def lanes_of(shape):
    return lax.broadcasted_iota(jnp.int32, shape, len(shape) - 1)


def ahead_z(v):
    depth = v.shape[-1]
    return jnp.where(lanes_of(v.shape) == depth - 1, 0.0, pltpu.roll(v, depth - 1, v.ndim - 1))


def behind_z(v):
    return jnp.where(lanes_of(v.shape) == 0, 0.0, pltpu.roll(v, 1, v.ndim - 1))


def ahead_y(v, edge=0.0):
    rows = v.shape[-2]
    return jnp.where(rows_of(v.shape) == rows - 1, edge, pltpu.roll(v, rows - 1, v.ndim - 2))


def behind_y(v, edge=0.0):
    return jnp.where(rows_of(v.shape) == 0, edge, pltpu.roll(v, 1, v.ndim - 2))


def keep(flag, v):
    return jnp.where(flag, v, 0.0)


def call(kernel, outs, args, aliases=None, flops=0, scratch=()):
    spec = pl.BlockSpec(memory_space=VMEM)
    traffic = 4 * (sum(math.prod(s) for s in outs) + sum(math.prod(a.shape) for a in args))
    return pl.pallas_call(
        kernel,
        out_shape=tuple(VMEM(s, jnp.float32) for s in outs),
        in_specs=[spec] * len(args),
        out_specs=tuple([spec] * len(outs)),
        scratch_shapes=scratch,
        input_output_aliases=aliases or {},
        cost_estimate=pl.CostEstimate(flops=flops, bytes_accessed=traffic, transcendentals=0),
        compiler_params=pltpu.CompilerParams(vmem_limit_bytes=16 * 2**20),
    )(*[pltpu.with_memory_space_constraint(a, VMEM) for a in args])


def pack_x(n, r, e, h, p, q, d, m, even_out, odd_out, e_at, h_at, p_at, q_at, d_at, m_at, sems):
    copies = []
    for end in range(2):
        for k, (ref, held, planes) in enumerate(
            ((e, e_at, 2), (h, h_at, 2), (p, p_at, 1), (q, q_at, 1), (d, d_at, WIDTH), (m, m_at, WIDTH))
        ):
            rows = pl.ds((n - planes) * r if end else 0, planes * r)
            src = ref.at[:, rows, :] if len(ref.shape) == 3 else ref.at[rows, :]
            copies.append(pltpu.make_async_copy(src, held.at[end], sems.at[end, k]))
    for copy in copies:
        copy.start()
    for copy in copies:
        copy.wait()
    odd = odd_x()

    def take(ref, planes, k, c=None):
        low, high = slice(k * r, (k + 1) * r), slice((planes - 1 - k) * r, (planes - k) * r)
        if c is None:
            return ref[0, low, :], ref[1, high, :]
        return ref[0, c, low, :], ref[1, c, high, :]

    def put(slot, pair):
        at = slice(slot * r, (slot + 1) * r)
        even_out[at, :] = jnp.where(odd, pair[0], pair[1])
        odd_out[at, :] = jnp.where(odd, pair[1], pair[0])

    for c in range(3):
        put(c, take(e_at, 2, 0, c))
        put(3 + c, take(h_at, 2, 0, c))
        put(6 + c, [DAMPING * b - OMEGA_SQUARED * a for a, b in zip(take(p_at, 1, 0, c), take(q_at, 1, 0, c))])
        put(10 + c, take(e_at, 2, 1, c))
    put(9, take(d_at, WIDTH, 0))
    put(13, take(h_at, 2, 1, 1))
    put(14, take(h_at, 2, 1, 2))
    put(15, take(d_at, WIDTH, 1))
    put(16, take(d_at, WIDTH, 2))
    for k in range(WIDTH):
        put(17 + k, [v.astype(jnp.float32) for v in take(m_at, WIDTH, k)])


def new_h(h, e, e_next, edge_x=0.0, edge_z=0.0):
    ex, ey, ez = e
    return (
        h[0] - COURANT * ((ahead_y(ez, edge_z) - ez) - (ahead_z(ey) - ey)),
        h[1] - COURANT * ((ahead_z(ex) - ex) - (e_next[2] - ez)),
        h[2] - COURANT * ((e_next[1] - ey) - (ahead_y(ex, edge_x) - ex)),
    )


def curl_h(h, h_last, edge_x=0.0, edge_z=0.0):
    hx, hy, hz = h
    return (
        (hz - behind_y(hz, edge_z)) - (hy - behind_z(hy)),
        (hx - behind_z(hx)) - (hz - h_last[2]),
        (hy - h_last[1]) - (hx - behind_y(hx, edge_x)),
    )


def half_over_eps(d):
    return COURANT / (1.0 + (EPS_MATERIAL - 1.0) * d)


def step_inner(n, r, block, e, h, p, q, d, h_out, e_out, c_out, t_out, even_y, odd_y_out):
    def plane(ref, x, c=None):
        at = pl.ds(pl.multiple_of(x * r, r), r)
        return ref[at, :] if c is None else ref[c, at, :]

    def put(ref, x, v, c=None):
        at = pl.ds(pl.multiple_of(x * r, r), r)
        if c is None:
            ref[at, :] = v
        else:
            ref[c, at, :] = v

    def one(x, last):
        now = [plane(e, x, c) for c in range(3)]
        nxt = [plane(e, jnp.minimum(x + 1, n - 1), c) for c in range(3)]
        mine = new_h([plane(h, x, c) for c in range(3)], now, nxt)
        dd = plane(d, x)
        half = half_over_eps(dd)
        put(c_out, x + 1, half)
        curl = curl_h(mine, last)
        for c in range(3):
            old = plane(p, x, c)
            rate = DAMPING * plane(q, x, c) - OMEGA_SQUARED * old + (OMEGA_SQUARED * LORENTZ_STRENGTH) * dd * now[c]
            put(t_out, x, (DAMPING - OMEGA_SQUARED) * rate - OMEGA_SQUARED * old, c)
            put(h_out, x + 1, mine[c], c)
            put(e_out, x + 1, now[c] + half * (curl[c] - 2.0 * rate), c)
        return mine

    def body(i, last):
        for k in range(block):
            last = one(i * block + k, last)
        return last

    zero = jnp.zeros((r, e.shape[-1]), jnp.float32)
    for c in range(3):
        put(h_out, n + 1, zero, c)
        put(e_out, n + 1, zero, c)
    lax.fori_loop(0, n // block, body, (zero, zero, zero))
    flip_y = odd_y()
    for k, (u, v) in enumerate(zip(*faces(n, r, n, 0, e, h_out, e_out, c_out))):
        even_y[k * n : (k + 1) * n, :] = jnp.where(flip_y, v, u)
        odd_y_out[k * n : (k + 1) * n, :] = jnp.where(flip_y, u, v)


def faces(n, r, size, x, e, h_out, e_out, c_out):
    def row(ref, y, first, c=None):
        at = pl.ds((first + 1) * r + y, size, stride=r)
        return ref[at, :] if c is None else ref[c, at, :]

    last = r - 1
    g_x, g_z = row(h_out, last, x, 0), row(h_out, last, x, 2)
    a_x, a_y, a_z = row(e_out, last, x, 0), row(e_out, last, x, 1), row(e_out, last, x, 2)
    a_y1 = row(e_out, last, x + 1, 1)
    up = (
        g_x,
        g_z,
        g_x + COURANT * a_z + COURANT * (ahead_z(a_y) - a_y),
        g_z - COURANT * (a_y1 - a_y) - COURANT * a_x,
        row(c_out, last, x),
    )
    down = (
        row(e_out, 0, x, 0),
        row(e_out, 0, x, 2),
        row(c_out, 0, x),
        e[0, pl.ds(x * r, size, stride=r), :],
        e[2, pl.ds(x * r, size, stride=r), :],
    )
    return up, down


def step_edges(n, r, e, h, p, q, d, even, odd, h_in, e_in, c_in, h_out, e_out, c_out, rows_out, even_y, odd_y_out):
    del h_in, e_in, c_in
    flip = odd_x()
    below, above, _, _ = edges()

    def lo(slot):
        at = slice(slot * r, (slot + 1) * r)
        return keep(below, jnp.where(flip, even[at, :], odd[at, :]))

    def hi(slot):
        at = slice(slot * r, (slot + 1) * r)
        return keep(above, jnp.where(flip, odd[at, :], even[at, :]))

    def own(ref, x):
        return [ref[c, x * r : (x + 1) * r, :] for c in range(3)]

    def at(x):
        return slice((x + 1) * r, (x + 2) * r)

    e_m2, e_m1 = [lo(10), lo(11), lo(12)], [lo(0), lo(1), lo(2)]
    e_n, e_n1 = [hi(0), hi(1), hi(2)], [hi(10), hi(11), hi(12)]
    e_0, e_l = own(e, 0), own(e, n - 1)
    h_m2 = new_h([lo(13), lo(13), lo(14)], e_m2, e_m1)
    h_m1 = [keep(below, v) for v in new_h([lo(3), lo(4), lo(5)], e_m1, e_0)]
    h_l = new_h(own(h, n - 1), e_l, e_n)
    h_n = new_h([hi(3), hi(4), hi(5)], e_n, e_n1)
    h_0 = [h_out[c, at(0), :] for c in range(3)]
    h_l1 = [h_out[c, at(n - 2), :] for c in range(3)]

    def new_e(x, electric, magnetic, last, drift, density, flag=None):
        half = half_over_eps(density)
        if flag is not None:
            half = keep(flag, half)
            c_out[at(x), :] = half
        curl = curl_h(magnetic, last)
        for c in range(3):
            rate = drift[c] + (OMEGA_SQUARED * LORENTZ_STRENGTH) * density * electric[c]
            e_out[c, at(x), :] = electric[c] + half * (curl[c] - 2.0 * rate)

    def drift(x):
        return [DAMPING * b - OMEGA_SQUARED * a for a, b in zip(own(p, x), own(q, x))]

    for c in range(3):
        h_out[c, at(-1), :] = h_m1[c]
        h_out[c, at(n - 1), :] = h_l[c]
        h_out[c, at(n), :] = h_n[c]
    new_e(-1, e_m1, h_m1, h_m2, [lo(6), lo(7), lo(8)], lo(9), below)
    new_e(0, e_0, h_0, h_m1, drift(0), d[:r, :])
    new_e(n - 1, e_l, h_l, h_l1, drift(n - 1), d[(n - 1) * r :, :])
    new_e(n, e_n, h_n, h_l, [hi(6), hi(7), hi(8)], hi(9), above)

    for k, c in enumerate((0, 2)):
        rows_out[k, BASE - 1 : BASE, :] = e_m1[c][:1]
        rows_out[k, BASE : BASE + n, :] = e[c, pl.ds(0, n, stride=r), :]
        rows_out[k, BASE + n : BASE + n + 1, :] = e_n[c][:1]

    def up(field, x):
        def at_last(ref, c, x):
            start = (x + 1) * r + r - 1
            return ref[c, start : start + 1, :]

        g_x, g_z = at_last(h_out, 0, x), at_last(h_out, 2, x)
        if field == 0:
            return g_x
        if field == 1:
            return g_z
        if field == 4:
            return c_out[(x + 2) * r - 1 : (x + 2) * r, :]
        a_y = at_last(e_out, 1, x)
        if field == 2:
            return g_x + COURANT * at_last(e_out, 2, x) + COURANT * (ahead_z(a_y) - a_y)
        return g_z - COURANT * (at_last(e_out, 1, x + 1) - a_y) - COURANT * at_last(e_out, 0, x)

    def down(field, x):
        start = (x + 1) * r
        if field < 2:
            return e_out[2 * field, start : start + 1, :]
        if field == 2:
            return c_out[start : start + 1, :]
        return {-2: e_m2, -1: e_m1, n: e_n}[x][2 * (field - 3)][:1]

    flip_y = odd_y()
    zero = jnp.zeros((1, e.shape[-1]), jnp.float32)
    upward, downward = late_rows(n)
    for k in range(LATE):
        u = up(*upward[k]) if k < len(upward) else zero
        v = down(*downward[k]) if k < len(downward) else zero
        even_y[k : k + 1, :] = jnp.where(flip_y, v, u)
        odd_y_out[k : k + 1, :] = jnp.where(flip_y, u, v)


def step_mid(n, r, block, h, e, c_ref, t, d, f, out, g):
    below, _, _, _ = edges()

    def fields(ref, x):
        at = pl.ds(pl.multiple_of((x + 1) * r, r), r)
        return [ref[c, at, :] for c in range(3)]

    def one(x, last_h):
        now = fields(e, x)
        mine = new_h(fields(h, x), now, fields(e, x + 1))
        at = pl.ds(pl.multiple_of(x * r, r), r)
        half = c_ref[pl.ds(pl.multiple_of((x + 1) * r, r), r), :]
        dd = d[at, :]
        curl = curl_h(mine, last_h)
        total = None
        for c in range(3):
            rate = t[c, at, :] + (OMEGA_SQUARED * LORENTZ_STRENGTH) * dd * now[c]
            after = now[c] + half * (curl[c] - 2.0 * rate)
            part = now[c] * f[c, at, :] + after * f[3 + c, at, :]
            total = part if total is None else total + part
        g[at, :] = total
        return mine

    def body(i, last_h):
        for k in range(block):
            last_h = one(i * block + k, last_h)
        return last_h

    start = tuple(keep(below, v) for v in new_h(fields(h, -1), fields(e, -1), fields(e, 0)))
    lax.fori_loop(0, n // block, body, start)
    for j in range(REACH, r - REACH):
        out[(j - REACH) * n : (j - REACH + 1) * n, :] = g[pl.ds(j, n, stride=r), :]


def step_last(
    n, r, block, h, e, c_ref, t, d, rows, even, odd, even_late, odd_late, f, e_out, h_out, g_out, rim_out, edge_out, face, fix
):
    flip = odd_y()
    below, above, low, high = edges()
    hxm, hzm, dx, dz, ry, exp_, ezp, hxm2, hzm2, wm = range(10)
    last = r - 1
    upward, downward = late_rows(n)
    for k in range(5):
        at = slice(k * n, (k + 1) * n)
        face[0, k, BASE : BASE + n, :] = jnp.where(flip, even[at, :], odd[at, :])
        face[1, k, BASE : BASE + n, :] = jnp.where(flip, odd[at, :], even[at, :])
    for k, ((field_u, x_u), (field_v, x_v)) in enumerate(zip(upward, downward)):
        at = slice(k, k + 1)
        face[0, field_u, BASE + x_u : BASE + x_u + 1, :] = jnp.where(flip, even_late[at, :], odd_late[at, :])
        face[1, field_v, BASE + x_v : BASE + x_v + 1, :] = jnp.where(flip, odd_late[at, :], even_late[at, :])

    def up(k, x=0, size=n):
        return keep(low, face[0, k, BASE + x : BASE + x + size, :])

    def down(k, x=0, size=n):
        return keep(high, face[1, k, BASE + x : BASE + x + size, :])

    def put(which, v, x=0):
        fix[which, BASE + x : BASE + x + v.shape[0], :] = v

    def get(which, x=0, size=n):
        return fix[which, BASE + x : BASE + x + size, :]

    def row_e(k, x=0, size=n):
        return rows[k, BASE + x : BASE + x + size, :]

    def strided(ref, y, c, x=0):
        return ref[c, pl.ds((x + 1) * r + y, n, stride=r), :]

    for x, size in ((0, n), (-1, 1), (n, 1)):
        put(hxm, keep(low, up(0, x, size) - COURANT * row_e(1, x, size)), x)
        put(dx, -COURANT * down(4, x, size), x)
        put(dz, COURANT * down(3, x, size), x)
    put(dz, COURANT * down(3, -2, 1), -2)
    for x, size in ((0, n), (-1, 1)):
        put(hzm, keep(low, up(1, x, size) + COURANT * row_e(0, x, size)), x)
    put(hzm, jnp.zeros((1, h.shape[-1]), jnp.float32), n)
    for x, size in ((0, n), (-1, 1), (n, 1)):
        delta = get(dx, x, size)
        put(ry, delta - behind_z(delta) - get(dz, x, size) + get(dz, x - 1, size), x)

    half = down(2)
    put(exp_, down(0) - half * (strided(h, last, 2) + get(dz)))
    put(exp_, down(0, -1, 1) - down(2, -1, 1) * (h[2, last : last + 1, :] + get(dz, -1, 1)), -1)
    put(ezp, down(1) + half * (strided(h, last, 0) + get(dx)))
    half = up(4)

    def gain(x, size, factor):
        delta = -COURANT * row_e(1, x, size)
        step = COURANT * (row_e(0, x, size) - row_e(0, x - 1, size))
        return factor * (delta - behind_z(delta) - step)

    put(wm, gain(0, n, half))
    put(wm, gain(n, 1, up(4, n, 1)), n)
    delta_x, delta_z = -COURANT * row_e(1), COURANT * row_e(0)
    change = get(wm)
    here = c_ref[pl.ds(r, n, stride=r), :]
    first_z = strided(e, 0, 2) + here * get(hxm)
    first_x = strided(e, 0, 0) - here * get(hzm)
    add = up(2) + delta_x - COURANT * half * delta_x + COURANT * (ahead_z(change) - change) - COURANT * first_z
    put(hxm2, keep(low, add))
    add = up(3) + delta_z - COURANT * half * delta_z - COURANT * (get(wm, 1) - change) + COURANT * first_x
    put(hzm2, keep(low, add))

    shape = (r, h.shape[-1])
    first_row, last_row = rows_of(shape) == 0, rows_of(shape) == last

    def spread(which, x):
        return fix[which, pl.ds(BASE + x, 1), :]

    def after_one(x):
        at = pl.ds(pl.multiple_of((x + 1) * r, r), r)
        half = c_ref[at, :]
        d_x, d_z = jnp.where(last_row, spread(dx, x), 0.0), jnp.where(last_row, spread(dz, x), 0.0)
        magnetic = (h[0, at, :] + d_x, h[1, at, :], h[2, at, :] + d_z)
        electric = (
            e[0, at, :] + half * jnp.where(first_row, -spread(hzm, x), d_z),
            e[1, at, :] + half * jnp.where(last_row, spread(ry, x), 0.0),
            e[2, at, :] + half * jnp.where(first_row, spread(hxm, x), -d_x),
        )
        return magnetic, electric

    def second_h(x, magnetic, now, ahead):
        return new_h(magnetic, now, ahead, spread(exp_, x), spread(ezp, x))

    def one(x, carry):
        last_h, magnetic, now = carry
        next_magnetic, ahead = after_one(x + 1)
        mine = second_h(x, magnetic, now, ahead)
        at = pl.ds(pl.multiple_of(x * r, r), r)
        half = c_ref[pl.ds(pl.multiple_of((x + 1) * r, r), r), :]
        dd = d[at, :]
        curl = curl_h(mine, last_h, spread(hxm2, x), spread(hzm2, x))
        total = None
        for c in range(3):
            rate = t[c, at, :] + (OMEGA_SQUARED * LORENTZ_STRENGTH) * dd * now[c]
            after = now[c] + half * (curl[c] - 2.0 * rate)
            e_out[c, at, :] = after
            h_out[c, at, :] = mine[c]
            part = now[c] * f[c, at, :] + after * f[3 + c, at, :]
            total = part if total is None else total + part
        g_out[at, :] = total
        return mine, next_magnetic, ahead

    def body(i, carry):
        for k in range(block):
            carry = one(i * block + k, carry)
        return carry

    magnetic, now = after_one(-1)
    next_magnetic, ahead = after_one(0)
    start = tuple(keep(below, v) for v in second_h(-1, magnetic, now, ahead))
    lax.fori_loop(0, n // block, body, (start, next_magnetic, ahead))
    for k, j in enumerate(rim_rows(r)):
        rim_out[k * n : (k + 1) * n, :] = g_out[pl.ds(j, n, stride=r), :]
    first = jnp.where(odd_x(), 0, n - WIDTH)
    edge_out[...] = g_out[pl.ds(pl.multiple_of(first * r, r), WIDTH * r), :]


def rim_rows(r):
    return [j for j in range(r) if not REACH <= j < r - REACH]


def update(n, r, generic, *refs):
    if generic:
        g, mid, rim, edge, edge_m, far, far_m, d, m, even, odd, order, u_out, even_y, odd_y_out, u_pad, other = refs
    else:
        g, mid, rim, edge, edge_m, d, m, even, odd, order, u_out, even_y, odd_y_out, u_pad, other = refs
    for k, j in enumerate(range(REACH, r - REACH)):
        other[pl.ds(j, n, stride=r), :] = mid[k * n : (k + 1) * n, :]
    for k, j in enumerate(rim_rows(r)):
        other[pl.ds(j, n, stride=r), :] = rim[k * n : (k + 1) * n, :]
    flip = odd_x()
    below, above, _, _ = edges()
    perm = order[...]

    def paired(v):
        return jnp.take_along_axis(v, perm, axis=0, mode="promise_in_bounds")

    def plane(ref, x):
        return ref[pl.ds(pl.multiple_of(x * r, r), r), :]

    def put(k, v):
        at = pl.ds(pl.multiple_of(k * r, r), r)
        u_out[at, :] = v
        u_pad[at, :] = v

    scale = 0.5 * UPDATE_STEP
    for x in range(n):
        put(x + WIDTH, plane(d, x) - scale * plane(m, x).astype(jnp.float32) * (plane(g, x) + paired(plane(other, n - 1 - x))))
    slots = (9, 15, 16)
    for j in range(WIDTH):
        high, low = n + WIDTH + j, WIDTH - 1 - j
        back, forth = jnp.where(flip, j, WIDTH - 1 - j), jnp.where(flip, WIDTH - 1 - j, j)
        u = plane(even, slots[j]) - scale * plane(even, 17 + j) * (plane(edge, forth) + paired(plane(edge_m, back)))
        put(jnp.where(flip, low, high), u)
        if generic:
            near, mirrored = plane(far, back), plane(far_m, forth)
        else:
            near = plane(other, jnp.where(flip, j, n - 1 - j))
            mirrored = plane(g, jnp.where(flip, n - 1 - j, j))
        u = plane(odd, slots[j]) - scale * plane(odd, 17 + j) * (near + paired(mirrored))
        put(jnp.where(flip, high, low), keep(jnp.where(flip, above, below), u))
    flip_y = odd_y()
    wide = u_pad.shape[0] // r
    for j in range(WIDTH):
        upper = u_pad[pl.ds(r - WIDTH + j, wide, stride=r), :]
        lower = u_pad[pl.ds(j, wide, stride=r), :]
        at = slice(j * wide, (j + 1) * wide)
        even_y[at, :] = jnp.where(flip_y, lower, upper)
        odd_y_out[at, :] = jnp.where(flip_y, upper, lower)


CLASSES = (
    (0.0, ((0, 0),)),
    (1.0, ((0, 1), (1, 0))),
    (2.0, ((1, 1),)),
    (4.0, ((2, 0), (0, 2))),
    (5.0, ((2, 1), (1, 2))),
    (8.0, ((2, 2),)),
    (9.0, ((3, 0), (0, 3))),
    (10.0, ((3, 1), (1, 3))),
    (13.0, ((3, 2), (2, 3))),
    (18.0, ((3, 3),)),
)


def weight(radius, square):
    return jnp.maximum(radius - math.sqrt(square), 0.0)


def cover(n, r, block, radius, out):
    x0, y0 = lax.axis_index("gx") * n, lax.axis_index("gy") * r
    total_x, total_y = n * lax.axis_size("gx"), r * lax.axis_size("gy")
    shape = (r, out.shape[-1])
    y = y0 + rows_of(shape)
    ones = jnp.ones(shape, jnp.float32)

    def there(where, total):
        return ((where >= 0) & (where < total)).astype(jnp.float32)

    across = [ones] + [there(y - b, total_y) + there(y + b, total_y) for b in range(1, RMAX)]

    def one(x):
        at = pl.ds(pl.multiple_of(x * r, r), r)
        rad = radius[at, :]
        where = jnp.full(shape, x0 + x, jnp.int32)
        along = [ones] + [there(where - a, total_x) + there(where + a, total_x) for a in range(1, RMAX)]
        total = None
        for square, members in CLASSES:
            part = sum(across[b] * along[a] for b, a in members)
            part = weight(rad, square) * part
            total = part if total is None else total + part
        out[at, :] = 1.0 / total

    def body(i, carry):
        for k in range(block):
            one(i * block + k)
        return carry

    lax.fori_loop(0, n // block, body, 0)


def smooth(n, r, block, u, even, odd, radius, inverse, out, halo, sums):
    flip = odd_y()
    _, _, low, high = edges()
    wide = even.shape[0] // WIDTH
    full = n + 2 * WIDTH
    for j in range(WIDTH):
        at = slice(j * wide, (j + 1) * wide)
        lower = keep(low, jnp.where(flip, even[at, :], odd[at, :]))
        upper = keep(high, jnp.where(flip, odd[at, :], even[at, :]))
        halo[pl.ds(r - WIDTH + j, wide, stride=r), :] = lower
        halo[pl.ds(j, wide, stride=r), :] = upper
    shape = (r, u.shape[-1])
    row = rows_of(shape)

    def fold(k):
        at = pl.ds(pl.multiple_of(k * r, r), r)
        mine, beside = u[at, :], halo[at, :]
        for b in range(1, RMAX):
            upper = pltpu.roll(jnp.where(row < b, beside, mine), r - b, 0)
            lower = pltpu.roll(jnp.where(row >= r - b, beside, mine), b, 0)
            sums[b - 1, at, :] = upper + lower

    def fold_block(i, carry):
        for k in range(block):
            fold(i * block + k)
        return carry

    whole = full // block
    lax.fori_loop(0, whole, fold_block, 0)
    for k in range(whole * block, full):
        fold(k)

    top = math.tanh(SHARPNESS * THRESHOLD)
    bottom = top + math.tanh(SHARPNESS * (1.0 - THRESHOLD))

    def one(x):
        at = pl.ds(pl.multiple_of(x * r, r), r)
        rad = radius[at, :]

        def line(b, a):
            where = pl.ds(pl.multiple_of((x + WIDTH + a) * r, r), r)
            return u[where, :] if b == 0 else sums[b - 1, where, :]

        total = None
        for square, members in CLASSES:
            part = None
            for b, a in members:
                v = line(b, 0) if a == 0 else line(b, a) + line(b, -a)
                part = v if part is None else part + v
            part = weight(rad, square) * part
            total = part if total is None else total + part
        filtered = total * inverse[at, :]
        out[at, :] = (top + jnp.tanh(SHARPNESS * (filtered - THRESHOLD))) / bottom

    def body(i, carry):
        for k in range(block):
            one(i * block + k)
        return carry

    lax.fori_loop(0, n // block, body, 0)


def local(
    adj_electric,
    adj_magnetic,
    polarization,
    pol_rate,
    density,
    forward_rate,
    design_mask,
    partner_rows,
    filter_radius,
):
    n, r, depth = density.shape
    size = n * r
    e, h = adj_electric.reshape(3, size, depth), adj_magnetic.reshape(3, size, depth)
    p, q = polarization.reshape(3, size, depth), pol_rate.reshape(3, size, depth)
    d, m = density.reshape(size, depth), design_mask.reshape(size, depth)
    f = forward_rate.reshape(3 * STEPS, size, depth)
    more = size + 2 * r
    face_x = (SLOTS * r, depth)
    face_y = (5 * n, depth)
    lines = n + 2 * BASE

    f32 = jnp.float32
    even, odd = pl.pallas_call(
        functools.partial(pack_x, n, r),
        out_shape=(VMEM(face_x, f32), VMEM(face_x, f32)),
        in_specs=[pl.BlockSpec(memory_space=pl.ANY)] * 6,
        out_specs=(pl.BlockSpec(memory_space=VMEM), pl.BlockSpec(memory_space=VMEM)),
        scratch_shapes=[
            VMEM((2, 3, 2 * r, depth), f32),
            VMEM((2, 3, 2 * r, depth), f32),
            VMEM((2, 3, r, depth), f32),
            VMEM((2, 3, r, depth), f32),
            VMEM((2, WIDTH * r, depth), f32),
            VMEM((2, WIDTH * r, depth), jnp.int32),
            pltpu.SemaphoreType.DMA((2, 6)),
        ],
    )(e, h, p, q, d, m)
    even = send(even, x_even)
    odd = send(odd, x_odd)

    inner = functools.partial(step_inner, n, r, 16)
    h1, e1, c1, t1, even_y, odd_y_ = call(
        inner,
        [(3, more, depth)] * 2 + [(more, depth), (3, size, depth)] + [face_y] * 2,
        [e, h, p, q, d],
        flops=100 * size * depth,
    )
    odd_y_ = send(odd_y_, y_odd)
    even_y = send(even_y, y_even)
    ends = functools.partial(step_edges, n, r)
    h1, e1, c1, rows, even_late, odd_late = call(
        ends,
        [(3, more, depth)] * 2 + [(more, depth), (2, lines, depth)] + [(LATE, depth)] * 2,
        [e, h, p, q, d, even, odd, h1, e1, c1],
        aliases={7: 0, 8: 1, 9: 2},
    )
    odd_late = send(odd_late, y_odd)
    even_late = send(even_late, y_even)
    (mid,) = call(
        functools.partial(step_mid, n, r, 16),
        [((r - 2 * REACH) * n, depth)],
        [h1, e1, c1, t1, d, f],
        flops=100 * size * depth,
        scratch=[VMEM((size, depth), jnp.float32)],
    )
    mid = send(mid, mirror)

    radius = jnp.broadcast_to(filter_radius.astype(jnp.float32)[:, :, None], (n, r, depth)).reshape(size, depth)
    order = jnp.broadcast_to(partner_rows[:, None], (r, depth))
    (inverse,) = call(functools.partial(cover, n, r, 16), [(size, depth)], [radius], flops=100 * size * depth)

    e2, h2, g, rim, edge = call(
        functools.partial(step_last, n, r, 16),
        [(3, size, depth)] * 2 + [(size, depth), (2 * REACH * n, depth), (WIDTH * r, depth)],
        [h1, e1, c1, t1, d, rows, even_y, odd_y_, even_late, odd_late, f],
        flops=150 * size * depth,
        scratch=[VMEM((2, 5, lines, depth), jnp.float32), VMEM((10, lines, depth), jnp.float32)],
    )
    rim = send(rim, mirror)
    edge_m = send(edge, mirror_even)
    edge_e = send(edge, x_even)
    generic = lax.axis_size("gx") != 4
    extra = []
    if generic:
        start = jnp.where(lax.axis_index("gx") % 2 == 1, (n - WIDTH) * r, 0)
        far = lax.dynamic_slice_in_dim(g, start, WIDTH * r, 0)
        extra = [send(far, x_odd), send(far, mirror_odd)]
    full = n + 2 * WIDTH
    wide = -(-full // 8) * 8
    u, even_u, odd_u = call(
        functools.partial(update, n, r, generic),
        [(full * r, depth), (WIDTH * wide, depth), (WIDTH * wide, depth)],
        [g, mid, rim, edge_e, edge_m] + extra + [d, m, even, odd, order],
        scratch=[VMEM((wide * r, depth), jnp.float32), VMEM((size, depth), jnp.float32)],
    )
    odd_u = send(odd_u, y_odd)
    even_u = send(even_u, y_even)
    (out,) = call(
        functools.partial(smooth, n, r, 16),
        [(size, depth)],
        [u, even_u, odd_u, radius, inverse],
        scratch=[VMEM((wide * r, depth), jnp.float32), VMEM((WIDTH, full * r, depth), jnp.float32)],
    )
    return (
        e2.reshape(3, n, r, depth),
        h2.reshape(3, n, r, depth),
        out.reshape(n, r, depth),
    )


def solution(mesh):
    in_specs = (
        P(None, "gx", "gy", None),
        P(None, "gx", "gy", None),
        P(None, "gx", "gy", None),
        P(None, "gx", "gy", None),
        P("gx", "gy", None),
        P(None, None, "gx", "gy", None),
        P("gx", "gy", None),
        P("gy"),
        P("gx", "gy"),
    )
    out_specs = (P(None, "gx", "gy", None), P(None, "gx", "gy", None), P("gx", "gy", None))
    return jax.shard_map(local, mesh=mesh, in_specs=in_specs, out_specs=out_specs, check_vma=False)
```

```python
import functools
import math

import jax
import jax.numpy as jnp
from jax import lax
from jax.experimental import pallas as pl
from jax.experimental.pallas import tpu as pltpu
from jax.sharding import PartitionSpec as P

STEPS = 2
RMAX = 4

COURANT = 0.5
DAMPING = 0.9
OMEGA_SQUARED = 0.3
LORENTZ_STRENGTH = 2.0
EPS_MATERIAL = 4.0
UPDATE_STEP = 0.25
SHARPNESS = 4.0
THRESHOLD = 0.5

AXES = ("gx", "gy")
WIDTH = RMAX - 1
SLOTS = 20
BASE = 8
REACH = STEPS
VMEM = pltpu.VMEM


def late_rows(n):
    up = ((0, -1), (0, n), (1, -1), (1, n - 1), (2, 0), (2, n - 1), (3, 0), (3, n - 2), (3, n - 1), (4, n))
    down = ((0, -1), (0, n - 1), (1, 0), (1, n - 1), (2, -1), (3, -2), (3, -1), (3, n), (4, -1), (4, n))
    return up, down


LATE = 16


def x_even(x, y, nx, ny):
    return x ^ 1, y


def x_odd(x, y, nx, ny):
    other = x + 1 if x % 2 else x - 1
    return (other, y) if 0 <= other < nx else (x, y ^ 1)


def y_even(x, y, nx, ny):
    return x, y ^ 1


def y_odd(x, y, nx, ny):
    other = y + 1 if y % 2 else y - 1
    return (x, other) if 0 <= other < ny else (x ^ 1, y)


def mirror(x, y, nx, ny):
    return nx - 1 - x, y


def mirror_even(x, y, nx, ny):
    return nx - 1 - (x ^ 1), y


def mirror_odd(x, y, nx, ny):
    other = x + 1 if x % 2 else x - 1
    return (nx - 1 - other, y) if 0 <= other < nx else (nx - 1 - x, y)


def send(block, rule):
    nx, ny = lax.axis_size("gx"), lax.axis_size("gy")
    route = []
    for x in range(nx):
        for y in range(ny):
            to_x, to_y = rule(x, y, nx, ny)
            route.append((x * ny + y, to_x * ny + to_y))
    return lax.ppermute(block, AXES, route)


def odd_x():
    return lax.rem(lax.axis_index("gx"), 2) == 1


def odd_y():
    return lax.rem(lax.axis_index("gy"), 2) == 1


def edges():
    x, y = lax.axis_index("gx"), lax.axis_index("gy")
    return (x > 0, x < lax.axis_size("gx") - 1, y > 0, y < lax.axis_size("gy") - 1)


def rows_of(shape):
    return lax.broadcasted_iota(jnp.int32, shape, len(shape) - 2)


def lanes_of(shape):
    return lax.broadcasted_iota(jnp.int32, shape, len(shape) - 1)


def ahead_z(v):
    depth = v.shape[-1]
    return jnp.where(lanes_of(v.shape) == depth - 1, 0.0, pltpu.roll(v, depth - 1, v.ndim - 1))


def behind_z(v):
    return jnp.where(lanes_of(v.shape) == 0, 0.0, pltpu.roll(v, 1, v.ndim - 1))


def ahead_y(v, edge=0.0):
    rows = v.shape[-2]
    return jnp.where(rows_of(v.shape) == rows - 1, edge, pltpu.roll(v, rows - 1, v.ndim - 2))


def behind_y(v, edge=0.0):
    return jnp.where(rows_of(v.shape) == 0, edge, pltpu.roll(v, 1, v.ndim - 2))


def keep(flag, v):
    return jnp.where(flag, v, 0.0)


def call(kernel, outs, args, aliases=None, flops=0, scratch=()):
    spec = pl.BlockSpec(memory_space=VMEM)
    traffic = 4 * (sum(math.prod(s) for s in outs) + sum(math.prod(a.shape) for a in args))
    return pl.pallas_call(
        kernel,
        out_shape=tuple(VMEM(s, jnp.float32) for s in outs),
        in_specs=[spec] * len(args),
        out_specs=tuple([spec] * len(outs)),
        scratch_shapes=scratch,
        input_output_aliases=aliases or {},
        cost_estimate=pl.CostEstimate(flops=flops, bytes_accessed=traffic, transcendentals=0),
        compiler_params=pltpu.CompilerParams(vmem_limit_bytes=16 * 2**20),
    )(*[pltpu.with_memory_space_constraint(a, VMEM) for a in args])


def pack_x(n, r, e, h, p, q, d, m, even_out, odd_out, e_at, h_at, p_at, q_at, d_at, m_at, sems):
    copies = []
    for end in range(2):
        for k, (ref, held, planes) in enumerate(
            ((e, e_at, 2), (h, h_at, 2), (p, p_at, 1), (q, q_at, 1), (d, d_at, WIDTH), (m, m_at, WIDTH))
        ):
            rows = pl.ds((n - planes) * r if end else 0, planes * r)
            src = ref.at[:, rows, :] if len(ref.shape) == 3 else ref.at[rows, :]
            copies.append(pltpu.make_async_copy(src, held.at[end], sems.at[end, k]))
    for copy in copies:
        copy.start()
    for copy in copies:
        copy.wait()
    odd = odd_x()

    def take(ref, planes, k, c=None):
        low, high = slice(k * r, (k + 1) * r), slice((planes - 1 - k) * r, (planes - k) * r)
        if c is None:
            return ref[0, low, :], ref[1, high, :]
        return ref[0, c, low, :], ref[1, c, high, :]

    def put(slot, pair):
        at = slice(slot * r, (slot + 1) * r)
        even_out[at, :] = jnp.where(odd, pair[0], pair[1])
        odd_out[at, :] = jnp.where(odd, pair[1], pair[0])

    for c in range(3):
        put(c, take(e_at, 2, 0, c))
        put(3 + c, take(h_at, 2, 0, c))
        put(6 + c, [DAMPING * b - OMEGA_SQUARED * a for a, b in zip(take(p_at, 1, 0, c), take(q_at, 1, 0, c))])
        put(10 + c, take(e_at, 2, 1, c))
    put(9, take(d_at, WIDTH, 0))
    put(13, take(h_at, 2, 1, 1))
    put(14, take(h_at, 2, 1, 2))
    put(15, take(d_at, WIDTH, 1))
    put(16, take(d_at, WIDTH, 2))
    for k in range(WIDTH):
        put(17 + k, [v.astype(jnp.float32) for v in take(m_at, WIDTH, k)])


def new_h(h, e, e_next, edge_x=0.0, edge_z=0.0):
    ex, ey, ez = e
    return (
        h[0] - COURANT * ((ahead_y(ez, edge_z) - ez) - (ahead_z(ey) - ey)),
        h[1] - COURANT * ((ahead_z(ex) - ex) - (e_next[2] - ez)),
        h[2] - COURANT * ((e_next[1] - ey) - (ahead_y(ex, edge_x) - ex)),
    )


def curl_h(h, h_last, edge_x=0.0, edge_z=0.0):
    hx, hy, hz = h
    return (
        (hz - behind_y(hz, edge_z)) - (hy - behind_z(hy)),
        (hx - behind_z(hx)) - (hz - h_last[2]),
        (hy - h_last[1]) - (hx - behind_y(hx, edge_x)),
    )


def half_over_eps(d):
    return COURANT / (1.0 + (EPS_MATERIAL - 1.0) * d)


def step_inner(n, r, block, e, h, p, q, d, h_out, e_out, c_out, t_out, even_y, odd_y_out):
    def plane(ref, x, c=None):
        at = pl.ds(pl.multiple_of(x * r, r), r)
        return ref[at, :] if c is None else ref[c, at, :]

    def put(ref, x, v, c=None):
        at = pl.ds(pl.multiple_of(x * r, r), r)
        if c is None:
            ref[at, :] = v
        else:
            ref[c, at, :] = v

    def one(x, last):
        now = [plane(e, x, c) for c in range(3)]
        nxt = [plane(e, jnp.minimum(x + 1, n - 1), c) for c in range(3)]
        mine = new_h([plane(h, x, c) for c in range(3)], now, nxt)
        dd = plane(d, x)
        half = half_over_eps(dd)
        put(c_out, x + 1, half)
        curl = curl_h(mine, last)
        for c in range(3):
            old = plane(p, x, c)
            rate = DAMPING * plane(q, x, c) - OMEGA_SQUARED * old + (OMEGA_SQUARED * LORENTZ_STRENGTH) * dd * now[c]
            put(t_out, x, (DAMPING - OMEGA_SQUARED) * rate - OMEGA_SQUARED * old, c)
            put(h_out, x + 1, mine[c], c)
            put(e_out, x + 1, now[c] + half * (curl[c] - 2.0 * rate), c)
        return mine

    def body(i, last):
        for k in range(block):
            last = one(i * block + k, last)
        return last

    zero = jnp.zeros((r, e.shape[-1]), jnp.float32)
    for c in range(3):
        put(h_out, n + 1, zero, c)
        put(e_out, n + 1, zero, c)
    lax.fori_loop(0, n // block, body, (zero, zero, zero))
    flip_y = odd_y()
    for k, (u, v) in enumerate(zip(*faces(n, r, n, 0, e, h_out, e_out, c_out))):
        even_y[k * n : (k + 1) * n, :] = jnp.where(flip_y, v, u)
        odd_y_out[k * n : (k + 1) * n, :] = jnp.where(flip_y, u, v)


def faces(n, r, size, x, e, h_out, e_out, c_out):
    def row(ref, y, first, c=None):
        at = pl.ds((first + 1) * r + y, size, stride=r)
        return ref[at, :] if c is None else ref[c, at, :]

    last = r - 1
    g_x, g_z = row(h_out, last, x, 0), row(h_out, last, x, 2)
    a_x, a_y, a_z = row(e_out, last, x, 0), row(e_out, last, x, 1), row(e_out, last, x, 2)
    a_y1 = row(e_out, last, x + 1, 1)
    up = (
        g_x,
        g_z,
        g_x + COURANT * a_z + COURANT * (ahead_z(a_y) - a_y),
        g_z - COURANT * (a_y1 - a_y) - COURANT * a_x,
        row(c_out, last, x),
    )
    down = (
        row(e_out, 0, x, 0),
        row(e_out, 0, x, 2),
        row(c_out, 0, x),
        e[0, pl.ds(x * r, size, stride=r), :],
        e[2, pl.ds(x * r, size, stride=r), :],
    )
    return up, down


def step_edges(n, r, e, h, p, q, d, even, odd, h_in, e_in, c_in, h_out, e_out, c_out, rows_out, even_y, odd_y_out):
    del h_in, e_in, c_in
    flip = odd_x()
    below, above, _, _ = edges()

    def lo(slot):
        at = slice(slot * r, (slot + 1) * r)
        return keep(below, jnp.where(flip, even[at, :], odd[at, :]))

    def hi(slot):
        at = slice(slot * r, (slot + 1) * r)
        return keep(above, jnp.where(flip, odd[at, :], even[at, :]))

    def own(ref, x):
        return [ref[c, x * r : (x + 1) * r, :] for c in range(3)]

    def at(x):
        return slice((x + 1) * r, (x + 2) * r)

    e_m2, e_m1 = [lo(10), lo(11), lo(12)], [lo(0), lo(1), lo(2)]
    e_n, e_n1 = [hi(0), hi(1), hi(2)], [hi(10), hi(11), hi(12)]
    e_0, e_l = own(e, 0), own(e, n - 1)
    h_m2 = new_h([lo(13), lo(13), lo(14)], e_m2, e_m1)
    h_m1 = [keep(below, v) for v in new_h([lo(3), lo(4), lo(5)], e_m1, e_0)]
    h_l = new_h(own(h, n - 1), e_l, e_n)
    h_n = new_h([hi(3), hi(4), hi(5)], e_n, e_n1)
    h_0 = [h_out[c, at(0), :] for c in range(3)]
    h_l1 = [h_out[c, at(n - 2), :] for c in range(3)]

    def new_e(x, electric, magnetic, last, drift, density, flag=None):
        half = half_over_eps(density)
        if flag is not None:
            half = keep(flag, half)
            c_out[at(x), :] = half
        curl = curl_h(magnetic, last)
        for c in range(3):
            rate = drift[c] + (OMEGA_SQUARED * LORENTZ_STRENGTH) * density * electric[c]
            e_out[c, at(x), :] = electric[c] + half * (curl[c] - 2.0 * rate)

    def drift(x):
        return [DAMPING * b - OMEGA_SQUARED * a for a, b in zip(own(p, x), own(q, x))]

    for c in range(3):
        h_out[c, at(-1), :] = h_m1[c]
        h_out[c, at(n - 1), :] = h_l[c]
        h_out[c, at(n), :] = h_n[c]
    new_e(-1, e_m1, h_m1, h_m2, [lo(6), lo(7), lo(8)], lo(9), below)
    new_e(0, e_0, h_0, h_m1, drift(0), d[:r, :])
    new_e(n - 1, e_l, h_l, h_l1, drift(n - 1), d[(n - 1) * r :, :])
    new_e(n, e_n, h_n, h_l, [hi(6), hi(7), hi(8)], hi(9), above)

    for k, c in enumerate((0, 2)):
        rows_out[k, BASE - 1 : BASE, :] = e_m1[c][:1]
        rows_out[k, BASE : BASE + n, :] = e[c, pl.ds(0, n, stride=r), :]
        rows_out[k, BASE + n : BASE + n + 1, :] = e_n[c][:1]

    def up(field, x):
        def at_last(ref, c, x):
            start = (x + 1) * r + r - 1
            return ref[c, start : start + 1, :]

        g_x, g_z = at_last(h_out, 0, x), at_last(h_out, 2, x)
        if field == 0:
            return g_x
        if field == 1:
            return g_z
        if field == 4:
            return c_out[(x + 2) * r - 1 : (x + 2) * r, :]
        a_y = at_last(e_out, 1, x)
        if field == 2:
            return g_x + COURANT * at_last(e_out, 2, x) + COURANT * (ahead_z(a_y) - a_y)
        return g_z - COURANT * (at_last(e_out, 1, x + 1) - a_y) - COURANT * at_last(e_out, 0, x)

    def down(field, x):
        start = (x + 1) * r
        if field < 2:
            return e_out[2 * field, start : start + 1, :]
        if field == 2:
            return c_out[start : start + 1, :]
        return {-2: e_m2, -1: e_m1, n: e_n}[x][2 * (field - 3)][:1]

    flip_y = odd_y()
    zero = jnp.zeros((1, e.shape[-1]), jnp.float32)
    upward, downward = late_rows(n)
    for k in range(LATE):
        u = up(*upward[k]) if k < len(upward) else zero
        v = down(*downward[k]) if k < len(downward) else zero
        even_y[k : k + 1, :] = jnp.where(flip_y, v, u)
        odd_y_out[k : k + 1, :] = jnp.where(flip_y, u, v)


def step_mid(n, r, block, h, e, c_ref, t, d, f, out, g):
    below, _, _, _ = edges()

    def fields(ref, x):
        at = pl.ds(pl.multiple_of((x + 1) * r, r), r)
        return [ref[c, at, :] for c in range(3)]

    def one(x, last_h):
        now = fields(e, x)
        mine = new_h(fields(h, x), now, fields(e, x + 1))
        at = pl.ds(pl.multiple_of(x * r, r), r)
        half = c_ref[pl.ds(pl.multiple_of((x + 1) * r, r), r), :]
        dd = d[at, :]
        curl = curl_h(mine, last_h)
        total = None
        for c in range(3):
            rate = t[c, at, :] + (OMEGA_SQUARED * LORENTZ_STRENGTH) * dd * now[c]
            after = now[c] + half * (curl[c] - 2.0 * rate)
            part = now[c] * f[c, at, :] + after * f[3 + c, at, :]
            total = part if total is None else total + part
        g[at, :] = total
        return mine

    def body(i, last_h):
        for k in range(block):
            last_h = one(i * block + k, last_h)
        return last_h

    start = tuple(keep(below, v) for v in new_h(fields(h, -1), fields(e, -1), fields(e, 0)))
    lax.fori_loop(0, n // block, body, start)
    for j in range(REACH, r - REACH):
        out[(j - REACH) * n : (j - REACH + 1) * n, :] = g[pl.ds(j, n, stride=r), :]


def step_last(
    n, r, block, h, e, c_ref, t, d, rows, even, odd, odd_late, even_late, f, e_out, h_out, g_out, rim_out, edge_out, face, fix
):
    flip = odd_y()
    below, above, low, high = edges()
    hxm, hzm, dx, dz, ry, exp_, ezp, hxm2, hzm2, wm = range(10)
    last = r - 1
    upward, downward = late_rows(n)
    for k in range(5):
        at = slice(k * n, (k + 1) * n)
        face[0, k, BASE : BASE + n, :] = jnp.where(flip, even[at, :], odd[at, :])
        face[1, k, BASE : BASE + n, :] = jnp.where(flip, odd[at, :], even[at, :])
    for k, ((field_u, x_u), (field_v, x_v)) in enumerate(zip(upward, downward)):
        at = slice(k, k + 1)
        face[0, field_u, BASE + x_u : BASE + x_u + 1, :] = jnp.where(flip, even_late[at, :], odd_late[at, :])
        face[1, field_v, BASE + x_v : BASE + x_v + 1, :] = jnp.where(flip, odd_late[at, :], even_late[at, :])

    def up(k, x=0, size=n):
        return keep(low, face[0, k, BASE + x : BASE + x + size, :])

    def down(k, x=0, size=n):
        return keep(high, face[1, k, BASE + x : BASE + x + size, :])

    def put(which, v, x=0):
        fix[which, BASE + x : BASE + x + v.shape[0], :] = v

    def get(which, x=0, size=n):
        return fix[which, BASE + x : BASE + x + size, :]

    def row_e(k, x=0, size=n):
        return rows[k, BASE + x : BASE + x + size, :]

    def strided(ref, y, c, x=0):
        return ref[c, pl.ds((x + 1) * r + y, n, stride=r), :]

    for x, size in ((0, n), (-1, 1), (n, 1)):
        put(hxm, keep(low, up(0, x, size) - COURANT * row_e(1, x, size)), x)
        put(dx, -COURANT * down(4, x, size), x)
        put(dz, COURANT * down(3, x, size), x)
    put(dz, COURANT * down(3, -2, 1), -2)
    for x, size in ((0, n), (-1, 1)):
        put(hzm, keep(low, up(1, x, size) + COURANT * row_e(0, x, size)), x)
    put(hzm, jnp.zeros((1, h.shape[-1]), jnp.float32), n)
    for x, size in ((0, n), (-1, 1), (n, 1)):
        delta = get(dx, x, size)
        put(ry, delta - behind_z(delta) - get(dz, x, size) + get(dz, x - 1, size), x)

    half = down(2)
    put(exp_, down(0) - half * (strided(h, last, 2) + get(dz)))
    put(exp_, down(0, -1, 1) - down(2, -1, 1) * (h[2, last : last + 1, :] + get(dz, -1, 1)), -1)
    put(ezp, down(1) + half * (strided(h, last, 0) + get(dx)))
    half = up(4)

    def gain(x, size, factor):
        delta = -COURANT * row_e(1, x, size)
        step = COURANT * (row_e(0, x, size) - row_e(0, x - 1, size))
        return factor * (delta - behind_z(delta) - step)

    put(wm, gain(0, n, half))
    put(wm, gain(n, 1, up(4, n, 1)), n)
    delta_x, delta_z = -COURANT * row_e(1), COURANT * row_e(0)
    change = get(wm)
    here = c_ref[pl.ds(r, n, stride=r), :]
    first_z = strided(e, 0, 2) + here * get(hxm)
    first_x = strided(e, 0, 0) - here * get(hzm)
    add = up(2) + delta_x - COURANT * half * delta_x + COURANT * (ahead_z(change) - change) - COURANT * first_z
    put(hxm2, keep(low, add))
    add = up(3) + delta_z - COURANT * half * delta_z - COURANT * (get(wm, 1) - change) + COURANT * first_x
    put(hzm2, keep(low, add))

    shape = (r, h.shape[-1])
    first_row, last_row = rows_of(shape) == 0, rows_of(shape) == last

    def spread(which, x):
        return fix[which, pl.ds(BASE + x, 1), :]

    def after_one(x):
        at = pl.ds(pl.multiple_of((x + 1) * r, r), r)
        half = c_ref[at, :]
        d_x, d_z = jnp.where(last_row, spread(dx, x), 0.0), jnp.where(last_row, spread(dz, x), 0.0)
        magnetic = (h[0, at, :] + d_x, h[1, at, :], h[2, at, :] + d_z)
        electric = (
            e[0, at, :] + half * jnp.where(first_row, -spread(hzm, x), d_z),
            e[1, at, :] + half * jnp.where(last_row, spread(ry, x), 0.0),
            e[2, at, :] + half * jnp.where(first_row, spread(hxm, x), -d_x),
        )
        return magnetic, electric

    def second_h(x, magnetic, now, ahead):
        return new_h(magnetic, now, ahead, spread(exp_, x), spread(ezp, x))

    def one(x, carry):
        last_h, magnetic, now = carry
        next_magnetic, ahead = after_one(x + 1)
        mine = second_h(x, magnetic, now, ahead)
        at = pl.ds(pl.multiple_of(x * r, r), r)
        half = c_ref[pl.ds(pl.multiple_of((x + 1) * r, r), r), :]
        dd = d[at, :]
        curl = curl_h(mine, last_h, spread(hxm2, x), spread(hzm2, x))
        total = None
        for c in range(3):
            rate = t[c, at, :] + (OMEGA_SQUARED * LORENTZ_STRENGTH) * dd * now[c]
            after = now[c] + half * (curl[c] - 2.0 * rate)
            e_out[c, at, :] = after
            h_out[c, at, :] = mine[c]
            part = now[c] * f[c, at, :] + after * f[3 + c, at, :]
            total = part if total is None else total + part
        g_out[at, :] = total
        return mine, next_magnetic, ahead

    def body(i, carry):
        for k in range(block):
            carry = one(i * block + k, carry)
        return carry

    magnetic, now = after_one(-1)
    next_magnetic, ahead = after_one(0)
    start = tuple(keep(below, v) for v in second_h(-1, magnetic, now, ahead))
    lax.fori_loop(0, n // block, body, (start, next_magnetic, ahead))
    for k, j in enumerate(rim_rows(r)):
        rim_out[k * n : (k + 1) * n, :] = g_out[pl.ds(j, n, stride=r), :]
    first = jnp.where(odd_x(), 0, n - WIDTH)
    edge_out[...] = g_out[pl.ds(pl.multiple_of(first * r, r), WIDTH * r), :]


def rim_rows(r):
    return [j for j in range(r) if not REACH <= j < r - REACH]


def update(n, r, generic, *refs):
    if generic:
        g, mid, rim, edge_m, edge, far, far_m, d, m, even, odd, order, u_out, even_y, odd_y_out, u_pad, other = refs
    else:
        g, mid, rim, edge_m, edge, d, m, even, odd, order, u_out, even_y, odd_y_out, u_pad, other = refs
    for k, j in enumerate(range(REACH, r - REACH)):
        other[pl.ds(j, n, stride=r), :] = mid[k * n : (k + 1) * n, :]
    for k, j in enumerate(rim_rows(r)):
        other[pl.ds(j, n, stride=r), :] = rim[k * n : (k + 1) * n, :]
    flip = odd_x()
    below, above, _, _ = edges()
    perm = order[...]

    def paired(v):
        return jnp.take_along_axis(v, perm, axis=0, mode="promise_in_bounds")

    def plane(ref, x):
        return ref[pl.ds(pl.multiple_of(x * r, r), r), :]

    def put(k, v):
        at = pl.ds(pl.multiple_of(k * r, r), r)
        u_out[at, :] = v
        u_pad[at, :] = v

    scale = 0.5 * UPDATE_STEP
    for x in range(n):
        put(x + WIDTH, plane(d, x) - scale * plane(m, x).astype(jnp.float32) * (plane(g, x) + paired(plane(other, n - 1 - x))))
    slots = (9, 15, 16)
    for j in range(WIDTH):
        high, low = n + WIDTH + j, WIDTH - 1 - j
        back, forth = jnp.where(flip, j, WIDTH - 1 - j), jnp.where(flip, WIDTH - 1 - j, j)
        u = plane(even, slots[j]) - scale * plane(even, 17 + j) * (plane(edge, forth) + paired(plane(edge_m, back)))
        put(jnp.where(flip, low, high), u)
        if generic:
            near, mirrored = plane(far, back), plane(far_m, forth)
        else:
            near = plane(other, jnp.where(flip, j, n - 1 - j))
            mirrored = plane(g, jnp.where(flip, n - 1 - j, j))
        u = plane(odd, slots[j]) - scale * plane(odd, 17 + j) * (near + paired(mirrored))
        put(jnp.where(flip, high, low), keep(jnp.where(flip, above, below), u))
    flip_y = odd_y()
    wide = u_pad.shape[0] // r
    for j in range(WIDTH):
        upper = u_pad[pl.ds(r - WIDTH + j, wide, stride=r), :]
        lower = u_pad[pl.ds(j, wide, stride=r), :]
        at = slice(j * wide, (j + 1) * wide)
        even_y[at, :] = jnp.where(flip_y, lower, upper)
        odd_y_out[at, :] = jnp.where(flip_y, upper, lower)


CLASSES = (
    (0.0, ((0, 0),)),
    (1.0, ((0, 1), (1, 0))),
    (2.0, ((1, 1),)),
    (4.0, ((2, 0), (0, 2))),
    (5.0, ((2, 1), (1, 2))),
    (8.0, ((2, 2),)),
    (9.0, ((3, 0), (0, 3))),
    (10.0, ((3, 1), (1, 3))),
    (13.0, ((3, 2), (2, 3))),
    (18.0, ((3, 3),)),
)


def weight(radius, square):
    return jnp.maximum(radius - math.sqrt(square), 0.0)


def cover(n, r, block, radius, out):
    x0, y0 = lax.axis_index("gx") * n, lax.axis_index("gy") * r
    total_x, total_y = n * lax.axis_size("gx"), r * lax.axis_size("gy")
    shape = (r, out.shape[-1])
    y = y0 + rows_of(shape)
    ones = jnp.ones(shape, jnp.float32)

    def there(where, total):
        return ((where >= 0) & (where < total)).astype(jnp.float32)

    across = [ones] + [there(y - b, total_y) + there(y + b, total_y) for b in range(1, RMAX)]

    def one(x):
        at = pl.ds(pl.multiple_of(x * r, r), r)
        rad = radius[at, :]
        where = jnp.full(shape, x0 + x, jnp.int32)
        along = [ones] + [there(where - a, total_x) + there(where + a, total_x) for a in range(1, RMAX)]
        total = None
        for square, members in CLASSES:
            part = sum(across[b] * along[a] for b, a in members)
            part = weight(rad, square) * part
            total = part if total is None else total + part
        out[at, :] = 1.0 / total

    def body(i, carry):
        for k in range(block):
            one(i * block + k)
        return carry

    lax.fori_loop(0, n // block, body, 0)


def smooth(n, r, block, u, even, odd, radius, inverse, out, halo, sums):
    flip = odd_y()
    _, _, low, high = edges()
    wide = even.shape[0] // WIDTH
    full = n + 2 * WIDTH
    for j in range(WIDTH):
        at = slice(j * wide, (j + 1) * wide)
        lower = keep(low, jnp.where(flip, even[at, :], odd[at, :]))
        upper = keep(high, jnp.where(flip, odd[at, :], even[at, :]))
        halo[pl.ds(r - WIDTH + j, wide, stride=r), :] = lower
        halo[pl.ds(j, wide, stride=r), :] = upper
    shape = (r, u.shape[-1])
    row = rows_of(shape)

    def fold(k):
        at = pl.ds(pl.multiple_of(k * r, r), r)
        mine, beside = u[at, :], halo[at, :]
        for b in range(1, RMAX):
            upper = pltpu.roll(jnp.where(row < b, beside, mine), r - b, 0)
            lower = pltpu.roll(jnp.where(row >= r - b, beside, mine), b, 0)
            sums[b - 1, at, :] = upper + lower

    def fold_block(i, carry):
        for k in range(block):
            fold(i * block + k)
        return carry

    whole = full // block
    lax.fori_loop(0, whole, fold_block, 0)
    for k in range(whole * block, full):
        fold(k)

    top = math.tanh(SHARPNESS * THRESHOLD)
    bottom = top + math.tanh(SHARPNESS * (1.0 - THRESHOLD))

    def one(x):
        at = pl.ds(pl.multiple_of(x * r, r), r)
        rad = radius[at, :]

        def line(b, a):
            where = pl.ds(pl.multiple_of((x + WIDTH + a) * r, r), r)
            return u[where, :] if b == 0 else sums[b - 1, where, :]

        total = None
        for square, members in CLASSES:
            part = None
            for b, a in members:
                v = line(b, 0) if a == 0 else line(b, a) + line(b, -a)
                part = v if part is None else part + v
            part = weight(rad, square) * part
            total = part if total is None else total + part
        filtered = total * inverse[at, :]
        out[at, :] = (top + jnp.tanh(SHARPNESS * (filtered - THRESHOLD))) / bottom

    def body(i, carry):
        for k in range(block):
            one(i * block + k)
        return carry

    lax.fori_loop(0, n // block, body, 0)


def local(
    adj_electric,
    adj_magnetic,
    polarization,
    pol_rate,
    density,
    forward_rate,
    design_mask,
    partner_rows,
    filter_radius,
):
    n, r, depth = density.shape
    size = n * r
    e, h = adj_electric.reshape(3, size, depth), adj_magnetic.reshape(3, size, depth)
    p, q = polarization.reshape(3, size, depth), pol_rate.reshape(3, size, depth)
    d, m = density.reshape(size, depth), design_mask.reshape(size, depth)
    f = forward_rate.reshape(3 * STEPS, size, depth)
    more = size + 2 * r
    face_x = (SLOTS * r, depth)
    face_y = (5 * n, depth)
    lines = n + 2 * BASE

    f32 = jnp.float32
    even, odd = pl.pallas_call(
        functools.partial(pack_x, n, r),
        out_shape=(VMEM(face_x, f32), VMEM(face_x, f32)),
        in_specs=[pl.BlockSpec(memory_space=pl.ANY)] * 6,
        out_specs=(pl.BlockSpec(memory_space=VMEM), pl.BlockSpec(memory_space=VMEM)),
        scratch_shapes=[
            VMEM((2, 3, 2 * r, depth), f32),
            VMEM((2, 3, 2 * r, depth), f32),
            VMEM((2, 3, r, depth), f32),
            VMEM((2, 3, r, depth), f32),
            VMEM((2, WIDTH * r, depth), f32),
            VMEM((2, WIDTH * r, depth), jnp.int32),
            pltpu.SemaphoreType.DMA((2, 6)),
        ],
    )(e, h, p, q, d, m)
    even = send(even, x_even)
    odd = send(odd, x_odd)

    inner = functools.partial(step_inner, n, r, 16)
    h1, e1, c1, t1, even_y, odd_y_ = call(
        inner,
        [(3, more, depth)] * 2 + [(more, depth), (3, size, depth)] + [face_y] * 2,
        [e, h, p, q, d],
        flops=100 * size * depth,
    )
    odd_y_ = send(odd_y_, y_odd)
    even_y = send(even_y, y_even)
    ends = functools.partial(step_edges, n, r)
    h1, e1, c1, rows, even_late, odd_late = call(
        ends,
        [(3, more, depth)] * 2 + [(more, depth), (2, lines, depth)] + [(LATE, depth)] * 2,
        [e, h, p, q, d, even, odd, h1, e1, c1],
        aliases={7: 0, 8: 1, 9: 2},
    )
    odd_late = send(odd_late, y_odd)
    even_late = send(even_late, y_even)
    (mid,) = call(
        functools.partial(step_mid, n, r, 16),
        [((r - 2 * REACH) * n, depth)],
        [h1, e1, c1, t1, d, f],
        flops=100 * size * depth,
        scratch=[VMEM((size, depth), jnp.float32)],
    )
    mid = send(mid, mirror)

    radius = jnp.broadcast_to(filter_radius.astype(jnp.float32)[:, :, None], (n, r, depth)).reshape(size, depth)
    order = jnp.broadcast_to(partner_rows[:, None], (r, depth))
    (inverse,) = call(functools.partial(cover, n, r, 16), [(size, depth)], [radius], flops=100 * size * depth)

    e2, h2, g, rim, edge = call(
        functools.partial(step_last, n, r, 16),
        [(3, size, depth)] * 2 + [(size, depth), (2 * REACH * n, depth), (WIDTH * r, depth)],
        [h1, e1, c1, t1, d, rows, even_y, odd_y_, odd_late, even_late, f],
        flops=150 * size * depth,
        scratch=[VMEM((2, 5, lines, depth), jnp.float32), VMEM((10, lines, depth), jnp.float32)],
    )
    rim = send(rim, mirror)
    edge_m = send(edge, mirror_even)
    edge_e = send(edge, x_even)
    generic = lax.axis_size("gx") != 4
    extra = []
    if generic:
        start = jnp.where(lax.axis_index("gx") % 2 == 1, (n - WIDTH) * r, 0)
        far = lax.dynamic_slice_in_dim(g, start, WIDTH * r, 0)
        extra = [send(far, x_odd), send(far, mirror_odd)]
    full = n + 2 * WIDTH
    wide = -(-full // 8) * 8
    u, even_u, odd_u = call(
        functools.partial(update, n, r, generic),
        [(full * r, depth), (WIDTH * wide, depth), (WIDTH * wide, depth)],
        [g, mid, rim, edge_m, edge_e] + extra + [d, m, even, odd, order],
        scratch=[VMEM((wide * r, depth), jnp.float32), VMEM((size, depth), jnp.float32)],
    )
    odd_u = send(odd_u, y_odd)
    even_u = send(even_u, y_even)
    (out,) = call(
        functools.partial(smooth, n, r, 16),
        [(size, depth)],
        [u, even_u, odd_u, radius, inverse],
        scratch=[VMEM((wide * r, depth), jnp.float32), VMEM((WIDTH, full * r, depth), jnp.float32)],
    )
    return (
        e2.reshape(3, n, r, depth),
        h2.reshape(3, n, r, depth),
        out.reshape(n, r, depth),
    )


def solution(mesh):
    in_specs = (
        P(None, "gx", "gy", None),
        P(None, "gx", "gy", None),
        P(None, "gx", "gy", None),
        P(None, "gx", "gy", None),
        P("gx", "gy", None),
        P(None, None, "gx", "gy", None),
        P("gx", "gy", None),
        P("gy"),
        P("gx", "gy"),
    )
    out_specs = (P(None, "gx", "gy", None), P(None, "gx", "gy", None), P("gx", "gy", None))
    return jax.shard_map(local, mesh=mesh, in_specs=in_specs, out_specs=out_specs, check_vma=False)
```

```python
import functools
import math

import jax
import jax.numpy as jnp
from jax import lax
from jax.experimental import pallas as pl
from jax.experimental.pallas import tpu as pltpu
from jax.sharding import PartitionSpec as P

STEPS = 2
RMAX = 4

COURANT = 0.5
DAMPING = 0.9
OMEGA_SQUARED = 0.3
LORENTZ_STRENGTH = 2.0
EPS_MATERIAL = 4.0
UPDATE_STEP = 0.25
SHARPNESS = 4.0
THRESHOLD = 0.5

AXES = ("gx", "gy")
WIDTH = RMAX - 1
SLOTS = 20
BASE = 8
REACH = STEPS
VMEM = pltpu.VMEM


def late_rows(n):
    up = ((0, -1), (0, n), (1, -1), (1, n - 1), (2, 0), (2, n - 1), (3, 0), (3, n - 2), (3, n - 1), (4, n))
    down = ((0, -1), (0, n - 1), (1, 0), (1, n - 1), (2, -1), (3, -2), (3, -1), (3, n), (4, -1), (4, n))
    return up, down


LATE = 16


def x_even(x, y, nx, ny):
    return x ^ 1, y


def x_odd(x, y, nx, ny):
    other = x + 1 if x % 2 else x - 1
    return (other, y) if 0 <= other < nx else (x, y ^ 1)


def y_even(x, y, nx, ny):
    return x, y ^ 1


def y_odd(x, y, nx, ny):
    other = y + 1 if y % 2 else y - 1
    return (x, other) if 0 <= other < ny else (x ^ 1, y)


def mirror(x, y, nx, ny):
    return nx - 1 - x, y


def mirror_even(x, y, nx, ny):
    return nx - 1 - (x ^ 1), y


def mirror_odd(x, y, nx, ny):
    other = x + 1 if x % 2 else x - 1
    return (nx - 1 - other, y) if 0 <= other < nx else (nx - 1 - x, y)


def send(block, rule):
    nx, ny = lax.axis_size("gx"), lax.axis_size("gy")
    route = []
    for x in range(nx):
        for y in range(ny):
            to_x, to_y = rule(x, y, nx, ny)
            route.append((x * ny + y, to_x * ny + to_y))
    return lax.ppermute(block, AXES, route)


def odd_x():
    return lax.rem(lax.axis_index("gx"), 2) == 1


def odd_y():
    return lax.rem(lax.axis_index("gy"), 2) == 1


def edges():
    x, y = lax.axis_index("gx"), lax.axis_index("gy")
    return (x > 0, x < lax.axis_size("gx") - 1, y > 0, y < lax.axis_size("gy") - 1)


def rows_of(shape):
    return lax.broadcasted_iota(jnp.int32, shape, len(shape) - 2)


def lanes_of(shape):
    return lax.broadcasted_iota(jnp.int32, shape, len(shape) - 1)


def ahead_z(v):
    depth = v.shape[-1]
    return jnp.where(lanes_of(v.shape) == depth - 1, 0.0, pltpu.roll(v, depth - 1, v.ndim - 1))


def behind_z(v):
    return jnp.where(lanes_of(v.shape) == 0, 0.0, pltpu.roll(v, 1, v.ndim - 1))


def ahead_y(v, edge=0.0):
    rows = v.shape[-2]
    return jnp.where(rows_of(v.shape) == rows - 1, edge, pltpu.roll(v, rows - 1, v.ndim - 2))


def behind_y(v, edge=0.0):
    return jnp.where(rows_of(v.shape) == 0, edge, pltpu.roll(v, 1, v.ndim - 2))


def keep(flag, v):
    return jnp.where(flag, v, 0.0)


def call(kernel, outs, args, aliases=None, flops=0, scratch=()):
    spec = pl.BlockSpec(memory_space=VMEM)
    traffic = 4 * (sum(math.prod(s) for s in outs) + sum(math.prod(a.shape) for a in args))
    return pl.pallas_call(
        kernel,
        out_shape=tuple(VMEM(s, jnp.float32) for s in outs),
        in_specs=[spec] * len(args),
        out_specs=tuple([spec] * len(outs)),
        scratch_shapes=scratch,
        input_output_aliases=aliases or {},
        cost_estimate=pl.CostEstimate(flops=flops, bytes_accessed=traffic, transcendentals=0),
        compiler_params=pltpu.CompilerParams(vmem_limit_bytes=16 * 2**20),
    )(*[pltpu.with_memory_space_constraint(a, VMEM) for a in args])


def pack_x(n, r, e, h, p, q, d, m, even_out, odd_out, e_at, h_at, p_at, q_at, d_at, m_at, sems):
    copies = []
    for end in range(2):
        for k, (ref, held, planes) in enumerate(
            ((e, e_at, 2), (h, h_at, 2), (p, p_at, 1), (q, q_at, 1), (d, d_at, WIDTH), (m, m_at, WIDTH))
        ):
            rows = pl.ds((n - planes) * r if end else 0, planes * r)
            src = ref.at[:, rows, :] if len(ref.shape) == 3 else ref.at[rows, :]
            copies.append(pltpu.make_async_copy(src, held.at[end], sems.at[end, k]))
    for copy in copies:
        copy.start()
    for copy in copies:
        copy.wait()
    odd = odd_x()

    def take(ref, planes, k, c=None):
        low, high = slice(k * r, (k + 1) * r), slice((planes - 1 - k) * r, (planes - k) * r)
        if c is None:
            return ref[0, low, :], ref[1, high, :]
        return ref[0, c, low, :], ref[1, c, high, :]

    def put(slot, pair):
        at = slice(slot * r, (slot + 1) * r)
        even_out[at, :] = jnp.where(odd, pair[0], pair[1])
        odd_out[at, :] = jnp.where(odd, pair[1], pair[0])

    for c in range(3):
        put(c, take(e_at, 2, 0, c))
        put(3 + c, take(h_at, 2, 0, c))
        put(6 + c, [DAMPING * b - OMEGA_SQUARED * a for a, b in zip(take(p_at, 1, 0, c), take(q_at, 1, 0, c))])
        put(10 + c, take(e_at, 2, 1, c))
    put(9, take(d_at, WIDTH, 0))
    put(13, take(h_at, 2, 1, 1))
    put(14, take(h_at, 2, 1, 2))
    put(15, take(d_at, WIDTH, 1))
    put(16, take(d_at, WIDTH, 2))
    for k in range(WIDTH):
        put(17 + k, [v.astype(jnp.float32) for v in take(m_at, WIDTH, k)])


def new_h(h, e, e_next, edge_x=0.0, edge_z=0.0):
    ex, ey, ez = e
    return (
        h[0] - COURANT * ((ahead_y(ez, edge_z) - ez) - (ahead_z(ey) - ey)),
        h[1] - COURANT * ((ahead_z(ex) - ex) - (e_next[2] - ez)),
        h[2] - COURANT * ((e_next[1] - ey) - (ahead_y(ex, edge_x) - ex)),
    )


def curl_h(h, h_last, edge_x=0.0, edge_z=0.0):
    hx, hy, hz = h
    return (
        (hz - behind_y(hz, edge_z)) - (hy - behind_z(hy)),
        (hx - behind_z(hx)) - (hz - h_last[2]),
        (hy - h_last[1]) - (hx - behind_y(hx, edge_x)),
    )


def half_over_eps(d):
    return COURANT / (1.0 + (EPS_MATERIAL - 1.0) * d)


def step_inner(n, r, block, e, h, p, q, d, h_out, e_out, c_out, t_out, even_y, odd_y_out):
    def plane(ref, x, c=None):
        at = pl.ds(pl.multiple_of(x * r, r), r)
        return ref[at, :] if c is None else ref[c, at, :]

    def put(ref, x, v, c=None):
        at = pl.ds(pl.multiple_of(x * r, r), r)
        if c is None:
            ref[at, :] = v
        else:
            ref[c, at, :] = v

    def one(x, last):
        now = [plane(e, x, c) for c in range(3)]
        nxt = [plane(e, jnp.minimum(x + 1, n - 1), c) for c in range(3)]
        mine = new_h([plane(h, x, c) for c in range(3)], now, nxt)
        dd = plane(d, x)
        half = half_over_eps(dd)
        put(c_out, x + 1, half)
        curl = curl_h(mine, last)
        for c in range(3):
            old = plane(p, x, c)
            rate = DAMPING * plane(q, x, c) - OMEGA_SQUARED * old + (OMEGA_SQUARED * LORENTZ_STRENGTH) * dd * now[c]
            put(t_out, x, (DAMPING - OMEGA_SQUARED) * rate - OMEGA_SQUARED * old, c)
            put(h_out, x + 1, mine[c], c)
            put(e_out, x + 1, now[c] + half * (curl[c] - 2.0 * rate), c)
        return mine

    def body(i, last):
        for k in range(block):
            last = one(i * block + k, last)
        return last

    zero = jnp.zeros((r, e.shape[-1]), jnp.float32)
    for c in range(3):
        put(h_out, n + 1, zero, c)
        put(e_out, n + 1, zero, c)
    lax.fori_loop(0, n // block, body, (zero, zero, zero))
    flip_y = odd_y()
    for k, (u, v) in enumerate(zip(*faces(n, r, n, 0, e, h_out, e_out, c_out))):
        even_y[k * n : (k + 1) * n, :] = jnp.where(flip_y, v, u)
        odd_y_out[k * n : (k + 1) * n, :] = jnp.where(flip_y, u, v)


def faces(n, r, size, x, e, h_out, e_out, c_out):
    def row(ref, y, first, c=None):
        at = pl.ds((first + 1) * r + y, size, stride=r)
        return ref[at, :] if c is None else ref[c, at, :]

    last = r - 1
    g_x, g_z = row(h_out, last, x, 0), row(h_out, last, x, 2)
    a_x, a_y, a_z = row(e_out, last, x, 0), row(e_out, last, x, 1), row(e_out, last, x, 2)
    a_y1 = row(e_out, last, x + 1, 1)
    up = (
        g_x,
        g_z,
        g_x + COURANT * a_z + COURANT * (ahead_z(a_y) - a_y),
        g_z - COURANT * (a_y1 - a_y) - COURANT * a_x,
        row(c_out, last, x),
    )
    down = (
        row(e_out, 0, x, 0),
        row(e_out, 0, x, 2),
        row(c_out, 0, x),
        e[0, pl.ds(x * r, size, stride=r), :],
        e[2, pl.ds(x * r, size, stride=r), :],
    )
    return up, down


def step_edges(n, r, e, h, p, q, d, even, odd, h_in, e_in, c_in, h_out, e_out, c_out, rows_out, even_y, odd_y_out):
    del h_in, e_in, c_in
    flip = odd_x()
    below, above, _, _ = edges()

    def lo(slot):
        at = slice(slot * r, (slot + 1) * r)
        return keep(below, jnp.where(flip, even[at, :], odd[at, :]))

    def hi(slot):
        at = slice(slot * r, (slot + 1) * r)
        return keep(above, jnp.where(flip, odd[at, :], even[at, :]))

    def own(ref, x):
        return [ref[c, x * r : (x + 1) * r, :] for c in range(3)]

    def at(x):
        return slice((x + 1) * r, (x + 2) * r)

    e_m2, e_m1 = [lo(10), lo(11), lo(12)], [lo(0), lo(1), lo(2)]
    e_n, e_n1 = [hi(0), hi(1), hi(2)], [hi(10), hi(11), hi(12)]
    e_0, e_l = own(e, 0), own(e, n - 1)
    h_m2 = new_h([lo(13), lo(13), lo(14)], e_m2, e_m1)
    h_m1 = [keep(below, v) for v in new_h([lo(3), lo(4), lo(5)], e_m1, e_0)]
    h_l = new_h(own(h, n - 1), e_l, e_n)
    h_n = new_h([hi(3), hi(4), hi(5)], e_n, e_n1)
    h_0 = [h_out[c, at(0), :] for c in range(3)]
    h_l1 = [h_out[c, at(n - 2), :] for c in range(3)]

    def new_e(x, electric, magnetic, last, drift, density, flag=None):
        half = half_over_eps(density)
        if flag is not None:
            half = keep(flag, half)
            c_out[at(x), :] = half
        curl = curl_h(magnetic, last)
        for c in range(3):
            rate = drift[c] + (OMEGA_SQUARED * LORENTZ_STRENGTH) * density * electric[c]
            e_out[c, at(x), :] = electric[c] + half * (curl[c] - 2.0 * rate)

    def drift(x):
        return [DAMPING * b - OMEGA_SQUARED * a for a, b in zip(own(p, x), own(q, x))]

    for c in range(3):
        h_out[c, at(-1), :] = h_m1[c]
        h_out[c, at(n - 1), :] = h_l[c]
        h_out[c, at(n), :] = h_n[c]
    new_e(-1, e_m1, h_m1, h_m2, [lo(6), lo(7), lo(8)], lo(9), below)
    new_e(0, e_0, h_0, h_m1, drift(0), d[:r, :])
    new_e(n - 1, e_l, h_l, h_l1, drift(n - 1), d[(n - 1) * r :, :])
    new_e(n, e_n, h_n, h_l, [hi(6), hi(7), hi(8)], hi(9), above)

    for k, c in enumerate((0, 2)):
        rows_out[k, BASE - 1 : BASE, :] = e_m1[c][:1]
        rows_out[k, BASE : BASE + n, :] = e[c, pl.ds(0, n, stride=r), :]
        rows_out[k, BASE + n : BASE + n + 1, :] = e_n[c][:1]

    def up(field, x):
        def at_last(ref, c, x):
            start = (x + 1) * r + r - 1
            return ref[c, start : start + 1, :]

        g_x, g_z = at_last(h_out, 0, x), at_last(h_out, 2, x)
        if field == 0:
            return g_x
        if field == 1:
            return g_z
        if field == 4:
            return c_out[(x + 2) * r - 1 : (x + 2) * r, :]
        a_y = at_last(e_out, 1, x)
        if field == 2:
            return g_x + COURANT * at_last(e_out, 2, x) + COURANT * (ahead_z(a_y) - a_y)
        return g_z - COURANT * (at_last(e_out, 1, x + 1) - a_y) - COURANT * at_last(e_out, 0, x)

    def down(field, x):
        start = (x + 1) * r
        if field < 2:
            return e_out[2 * field, start : start + 1, :]
        if field == 2:
            return c_out[start : start + 1, :]
        return {-2: e_m2, -1: e_m1, n: e_n}[x][2 * (field - 3)][:1]

    flip_y = odd_y()
    zero = jnp.zeros((1, e.shape[-1]), jnp.float32)
    upward, downward = late_rows(n)
    for k in range(LATE):
        u = up(*upward[k]) if k < len(upward) else zero
        v = down(*downward[k]) if k < len(downward) else zero
        even_y[k : k + 1, :] = jnp.where(flip_y, v, u)
        odd_y_out[k : k + 1, :] = jnp.where(flip_y, u, v)


def step_mid(n, r, block, h, e, c_ref, t, d, f, out, g):
    below, _, _, _ = edges()

    def fields(ref, x):
        at = pl.ds(pl.multiple_of((x + 1) * r, r), r)
        return [ref[c, at, :] for c in range(3)]

    def one(x, last_h):
        now = fields(e, x)
        mine = new_h(fields(h, x), now, fields(e, x + 1))
        at = pl.ds(pl.multiple_of(x * r, r), r)
        half = c_ref[pl.ds(pl.multiple_of((x + 1) * r, r), r), :]
        dd = d[at, :]
        curl = curl_h(mine, last_h)
        total = None
        for c in range(3):
            rate = t[c, at, :] + (OMEGA_SQUARED * LORENTZ_STRENGTH) * dd * now[c]
            after = now[c] + half * (curl[c] - 2.0 * rate)
            part = now[c] * f[c, at, :] + after * f[3 + c, at, :]
            total = part if total is None else total + part
        g[at, :] = total
        return mine

    def body(i, last_h):
        for k in range(block):
            last_h = one(i * block + k, last_h)
        return last_h

    start = tuple(keep(below, v) for v in new_h(fields(h, -1), fields(e, -1), fields(e, 0)))
    lax.fori_loop(0, n // block, body, start)
    for j in range(REACH, r - REACH):
        out[(j - REACH) * n : (j - REACH + 1) * n, :] = g[pl.ds(j, n, stride=r), :]


def step_last(n, r, late, h, e, c_ref, t, d, rows, even, odd, *refs):
    if late:
        odd_late, even_late, f, _, _, _, e_out, h_out, g_out, rim_out, edge_out, face, fix = refs
    else:
        f, e_out, h_out, g_out, face, fix = refs
    flip = odd_y()
    below, above, low, high = edges()
    hxm, hzm, dx, dz, ry, exp_, ezp, hxm2, hzm2, wm = range(10)
    last = r - 1
    apart = jnp.zeros((BASE, h.shape[-1]), jnp.float32)
    for k in range(5):
        at = slice(k * n, (k + 1) * n)
        for side in range(2):
            face[side, k, :BASE, :] = apart
            face[side, k, BASE + n :, :] = apart
        face[0, k, BASE : BASE + n, :] = jnp.where(flip, even[at, :], odd[at, :])
        face[1, k, BASE : BASE + n, :] = jnp.where(flip, odd[at, :], even[at, :])
    if late:
        for k, ((field_u, x_u), (field_v, x_v)) in enumerate(zip(*late_rows(n))):
            at = slice(k, k + 1)
            face[0, field_u, BASE + x_u : BASE + x_u + 1, :] = jnp.where(flip, even_late[at, :], odd_late[at, :])
            face[1, field_v, BASE + x_v : BASE + x_v + 1, :] = jnp.where(flip, odd_late[at, :], even_late[at, :])

    def up(k, x=0, size=n):
        return keep(low, face[0, k, BASE + x : BASE + x + size, :])

    def down(k, x=0, size=n):
        return keep(high, face[1, k, BASE + x : BASE + x + size, :])

    def put(which, v, x=0):
        fix[which, BASE + x : BASE + x + v.shape[0], :] = v

    def get(which, x=0, size=n):
        return fix[which, BASE + x : BASE + x + size, :]

    def row_e(k, x=0, size=n):
        return rows[k, BASE + x : BASE + x + size, :]

    def strided(ref, y, c, x=0):
        return ref[c, pl.ds((x + 1) * r + y, n, stride=r), :]

    for x, size in ((0, n), (-1, 1), (n, 1)):
        put(hxm, keep(low, up(0, x, size) - COURANT * row_e(1, x, size)), x)
        put(dx, -COURANT * down(4, x, size), x)
        put(dz, COURANT * down(3, x, size), x)
    put(dz, COURANT * down(3, -2, 1), -2)
    for x, size in ((0, n), (-1, 1)):
        put(hzm, keep(low, up(1, x, size) + COURANT * row_e(0, x, size)), x)
    put(hzm, jnp.zeros((1, h.shape[-1]), jnp.float32), n)
    for x, size in ((0, n), (-1, 1), (n, 1)):
        delta = get(dx, x, size)
        put(ry, delta - behind_z(delta) - get(dz, x, size) + get(dz, x - 1, size), x)

    half = down(2)
    put(exp_, down(0) - half * (strided(h, last, 2) + get(dz)))
    put(exp_, down(0, -1, 1) - down(2, -1, 1) * (h[2, last : last + 1, :] + get(dz, -1, 1)), -1)
    put(ezp, down(1) + half * (strided(h, last, 0) + get(dx)))
    half = up(4)

    def gain(x, size, factor):
        delta = -COURANT * row_e(1, x, size)
        step = COURANT * (row_e(0, x, size) - row_e(0, x - 1, size))
        return factor * (delta - behind_z(delta) - step)

    put(wm, gain(0, n, half))
    put(wm, gain(n, 1, up(4, n, 1)), n)
    delta_x, delta_z = -COURANT * row_e(1), COURANT * row_e(0)
    change = get(wm)
    here = c_ref[pl.ds(r, n, stride=r), :]
    first_z = strided(e, 0, 2) + here * get(hxm)
    first_x = strided(e, 0, 0) - here * get(hzm)
    add = up(2) + delta_x - COURANT * half * delta_x + COURANT * (ahead_z(change) - change) - COURANT * first_z
    put(hxm2, keep(low, add))
    add = up(3) + delta_z - COURANT * half * delta_z - COURANT * (get(wm, 1) - change) + COURANT * first_x
    put(hzm2, keep(low, add))

    shape = (r, h.shape[-1])
    first_row, last_row = rows_of(shape) == 0, rows_of(shape) == last

    def spread(which, x):
        return fix[which, pl.ds(BASE + x, 1), :]

    def after_one(x):
        at = pl.ds(pl.multiple_of((x + 1) * r, r), r)
        half = c_ref[at, :]
        d_x, d_z = jnp.where(last_row, spread(dx, x), 0.0), jnp.where(last_row, spread(dz, x), 0.0)
        magnetic = (h[0, at, :] + d_x, h[1, at, :], h[2, at, :] + d_z)
        electric = (
            e[0, at, :] + half * jnp.where(first_row, -spread(hzm, x), d_z),
            e[1, at, :] + half * jnp.where(last_row, spread(ry, x), 0.0),
            e[2, at, :] + half * jnp.where(first_row, spread(hxm, x), -d_x),
        )
        return magnetic, electric

    def second_h(x, magnetic, now, ahead):
        return new_h(magnetic, now, ahead, spread(exp_, x), spread(ezp, x))

    def one(x, carry):
        last_h, magnetic, now = carry
        next_magnetic, ahead = after_one(x + 1)
        mine = second_h(x, magnetic, now, ahead)
        at = pl.ds(pl.multiple_of(x * r, r), r)
        half = c_ref[pl.ds(pl.multiple_of((x + 1) * r, r), r), :]
        dd = d[at, :]
        curl = curl_h(mine, last_h, spread(hxm2, x), spread(hzm2, x))
        total = None
        for c in range(3):
            rate = t[c, at, :] + (OMEGA_SQUARED * LORENTZ_STRENGTH) * dd * now[c]
            after = now[c] + half * (curl[c] - 2.0 * rate)
            e_out[c, at, :] = after
            h_out[c, at, :] = mine[c]
            part = now[c] * f[c, at, :] + after * f[3 + c, at, :]
            total = part if total is None else total + part
        g_out[at, :] = total
        return mine, next_magnetic, ahead

    def run(first, end):
        magnetic, now = after_one(first - 1)
        next_magnetic, ahead = after_one(first)
        last_h = second_h(first - 1, magnetic, now, ahead)
        if first == 0:
            last_h = tuple(keep(below, v) for v in last_h)
        carry = (last_h, next_magnetic, ahead)
        for x in range(first, end):
            carry = one(x, carry)

    if not late:
        run(REACH, n - REACH)
        return
    run(0, REACH)
    run(n - REACH, n)
    for k, j in enumerate(rim_rows(r)):
        rim_out[k * n : (k + 1) * n, :] = g_out[pl.ds(j, n, stride=r), :]
    first = jnp.where(odd_x(), 0, n - WIDTH)
    edge_out[...] = g_out[pl.ds(pl.multiple_of(first * r, r), WIDTH * r), :]


def rim_rows(r):
    return [j for j in range(r) if not REACH <= j < r - REACH]


def update(n, r, generic, *refs):
    if generic:
        g, mid, rim, edge_m, edge, far, far_m, d, m, even, odd, order, u_out, even_y, odd_y_out, u_pad, other = refs
    else:
        g, mid, rim, edge_m, edge, d, m, even, odd, order, u_out, even_y, odd_y_out, u_pad, other = refs
    for k, j in enumerate(range(REACH, r - REACH)):
        other[pl.ds(j, n, stride=r), :] = mid[k * n : (k + 1) * n, :]
    for k, j in enumerate(rim_rows(r)):
        other[pl.ds(j, n, stride=r), :] = rim[k * n : (k + 1) * n, :]
    flip = odd_x()
    below, above, _, _ = edges()
    perm = order[...]

    def paired(v):
        return jnp.take_along_axis(v, perm, axis=0, mode="promise_in_bounds")

    def plane(ref, x):
        return ref[pl.ds(pl.multiple_of(x * r, r), r), :]

    def put(k, v):
        at = pl.ds(pl.multiple_of(k * r, r), r)
        u_out[at, :] = v
        u_pad[at, :] = v

    scale = 0.5 * UPDATE_STEP
    for x in range(n):
        put(x + WIDTH, plane(d, x) - scale * plane(m, x).astype(jnp.float32) * (plane(g, x) + paired(plane(other, n - 1 - x))))
    slots = (9, 15, 16)
    for j in range(WIDTH):
        high, low = n + WIDTH + j, WIDTH - 1 - j
        back, forth = jnp.where(flip, j, WIDTH - 1 - j), jnp.where(flip, WIDTH - 1 - j, j)
        u = plane(even, slots[j]) - scale * plane(even, 17 + j) * (plane(edge, forth) + paired(plane(edge_m, back)))
        put(jnp.where(flip, low, high), u)
        if generic:
            near, mirrored = plane(far, back), plane(far_m, forth)
        else:
            near = plane(other, jnp.where(flip, j, n - 1 - j))
            mirrored = plane(g, jnp.where(flip, n - 1 - j, j))
        u = plane(odd, slots[j]) - scale * plane(odd, 17 + j) * (near + paired(mirrored))
        put(jnp.where(flip, high, low), keep(jnp.where(flip, above, below), u))
    flip_y = odd_y()
    wide = u_pad.shape[0] // r
    for j in range(WIDTH):
        upper = u_pad[pl.ds(r - WIDTH + j, wide, stride=r), :]
        lower = u_pad[pl.ds(j, wide, stride=r), :]
        at = slice(j * wide, (j + 1) * wide)
        even_y[at, :] = jnp.where(flip_y, lower, upper)
        odd_y_out[at, :] = jnp.where(flip_y, upper, lower)


CLASSES = (
    (0.0, ((0, 0),)),
    (1.0, ((0, 1), (1, 0))),
    (2.0, ((1, 1),)),
    (4.0, ((2, 0), (0, 2))),
    (5.0, ((2, 1), (1, 2))),
    (8.0, ((2, 2),)),
    (9.0, ((3, 0), (0, 3))),
    (10.0, ((3, 1), (1, 3))),
    (13.0, ((3, 2), (2, 3))),
    (18.0, ((3, 3),)),
)


def weight(radius, square):
    return jnp.maximum(radius - math.sqrt(square), 0.0)


def cover(n, r, block, radius, out):
    x0, y0 = lax.axis_index("gx") * n, lax.axis_index("gy") * r
    total_x, total_y = n * lax.axis_size("gx"), r * lax.axis_size("gy")
    shape = (r, out.shape[-1])
    y = y0 + rows_of(shape)
    ones = jnp.ones(shape, jnp.float32)

    def there(where, total):
        return ((where >= 0) & (where < total)).astype(jnp.float32)

    across = [ones] + [there(y - b, total_y) + there(y + b, total_y) for b in range(1, RMAX)]

    def one(x):
        at = pl.ds(pl.multiple_of(x * r, r), r)
        rad = radius[at, :]
        where = jnp.full(shape, x0 + x, jnp.int32)
        along = [ones] + [there(where - a, total_x) + there(where + a, total_x) for a in range(1, RMAX)]
        total = None
        for square, members in CLASSES:
            part = sum(across[b] * along[a] for b, a in members)
            part = weight(rad, square) * part
            total = part if total is None else total + part
        out[at, :] = 1.0 / total

    def body(i, carry):
        for k in range(block):
            one(i * block + k)
        return carry

    lax.fori_loop(0, n // block, body, 0)


def smooth(n, r, block, u, even, odd, radius, inverse, out, halo, sums):
    flip = odd_y()
    _, _, low, high = edges()
    wide = even.shape[0] // WIDTH
    full = n + 2 * WIDTH
    for j in range(WIDTH):
        at = slice(j * wide, (j + 1) * wide)
        lower = keep(low, jnp.where(flip, even[at, :], odd[at, :]))
        upper = keep(high, jnp.where(flip, odd[at, :], even[at, :]))
        halo[pl.ds(r - WIDTH + j, wide, stride=r), :] = lower
        halo[pl.ds(j, wide, stride=r), :] = upper
    shape = (r, u.shape[-1])
    row = rows_of(shape)

    def fold(k):
        at = pl.ds(pl.multiple_of(k * r, r), r)
        mine, beside = u[at, :], halo[at, :]
        for b in range(1, RMAX):
            upper = pltpu.roll(jnp.where(row < b, beside, mine), r - b, 0)
            lower = pltpu.roll(jnp.where(row >= r - b, beside, mine), b, 0)
            sums[b - 1, at, :] = upper + lower

    def fold_block(i, carry):
        for k in range(block):
            fold(i * block + k)
        return carry

    whole = full // block
    lax.fori_loop(0, whole, fold_block, 0)
    for k in range(whole * block, full):
        fold(k)

    top = math.tanh(SHARPNESS * THRESHOLD)
    bottom = top + math.tanh(SHARPNESS * (1.0 - THRESHOLD))

    def one(x):
        at = pl.ds(pl.multiple_of(x * r, r), r)
        rad = radius[at, :]

        def line(b, a):
            where = pl.ds(pl.multiple_of((x + WIDTH + a) * r, r), r)
            return u[where, :] if b == 0 else sums[b - 1, where, :]

        total = None
        for square, members in CLASSES:
            part = None
            for b, a in members:
                v = line(b, 0) if a == 0 else line(b, a) + line(b, -a)
                part = v if part is None else part + v
            part = weight(rad, square) * part
            total = part if total is None else total + part
        filtered = total * inverse[at, :]
        out[at, :] = (top + jnp.tanh(SHARPNESS * (filtered - THRESHOLD))) / bottom

    def body(i, carry):
        for k in range(block):
            one(i * block + k)
        return carry

    lax.fori_loop(0, n // block, body, 0)


def local(
    adj_electric,
    adj_magnetic,
    polarization,
    pol_rate,
    density,
    forward_rate,
    design_mask,
    partner_rows,
    filter_radius,
):
    n, r, depth = density.shape
    size = n * r
    e, h = adj_electric.reshape(3, size, depth), adj_magnetic.reshape(3, size, depth)
    p, q = polarization.reshape(3, size, depth), pol_rate.reshape(3, size, depth)
    d, m = density.reshape(size, depth), design_mask.reshape(size, depth)
    f = forward_rate.reshape(3 * STEPS, size, depth)
    more = size + 2 * r
    face_x = (SLOTS * r, depth)
    face_y = (5 * n, depth)
    lines = n + 2 * BASE

    f32 = jnp.float32
    even, odd = pl.pallas_call(
        functools.partial(pack_x, n, r),
        out_shape=(VMEM(face_x, f32), VMEM(face_x, f32)),
        in_specs=[pl.BlockSpec(memory_space=pl.ANY)] * 6,
        out_specs=(pl.BlockSpec(memory_space=VMEM), pl.BlockSpec(memory_space=VMEM)),
        scratch_shapes=[
            VMEM((2, 3, 2 * r, depth), f32),
            VMEM((2, 3, 2 * r, depth), f32),
            VMEM((2, 3, r, depth), f32),
            VMEM((2, 3, r, depth), f32),
            VMEM((2, WIDTH * r, depth), f32),
            VMEM((2, WIDTH * r, depth), jnp.int32),
            pltpu.SemaphoreType.DMA((2, 6)),
        ],
    )(e, h, p, q, d, m)
    even = send(even, x_even)
    odd = send(odd, x_odd)

    inner = functools.partial(step_inner, n, r, 32)
    h1, e1, c1, t1, even_y, odd_y_ = call(
        inner,
        [(3, more, depth)] * 2 + [(more, depth), (3, size, depth)] + [face_y] * 2,
        [e, h, p, q, d],
        flops=100 * size * depth,
    )
    odd_y_ = send(odd_y_, y_odd)
    even_y = send(even_y, y_even)
    ends = functools.partial(step_edges, n, r)
    h1, e1, c1, rows, even_late, odd_late = call(
        ends,
        [(3, more, depth)] * 2 + [(more, depth), (2, lines, depth)] + [(LATE, depth)] * 2,
        [e, h, p, q, d, even, odd, h1, e1, c1],
        aliases={7: 0, 8: 1, 9: 2},
    )
    odd_late = send(odd_late, y_odd)
    even_late = send(even_late, y_even)
    (mid,) = call(
        functools.partial(step_mid, n, r, 32),
        [((r - 2 * REACH) * n, depth)],
        [h1, e1, c1, t1, d, f],
        flops=100 * size * depth,
        scratch=[VMEM((size, depth), jnp.float32)],
    )
    mid = send(mid, mirror)

    radius = jnp.broadcast_to(filter_radius.astype(jnp.float32)[:, :, None], (n, r, depth)).reshape(size, depth)
    order = jnp.broadcast_to(partner_rows[:, None], (r, depth))
    (inverse,) = call(functools.partial(cover, n, r, 16), [(size, depth)], [radius], flops=100 * size * depth)

    known = [h1, e1, c1, t1, d, rows, even_y, odd_y_]
    fields = [(3, size, depth)] * 2 + [(size, depth)]
    lists = [VMEM((2, 5, lines, depth), f32), VMEM((10, lines, depth), f32)]
    e2, h2, g = call(functools.partial(step_last, n, r, False), fields, known + [f], flops=150 * size * depth, scratch=lists)
    e2, h2, g, rim, edge = call(
        functools.partial(step_last, n, r, True),
        fields + [(2 * REACH * n, depth), (WIDTH * r, depth)],
        known + [odd_late, even_late, f, e2, h2, g],
        aliases={11: 0, 12: 1, 13: 2},
        scratch=lists,
    )
    rim = send(rim, mirror)
    edge_m = send(edge, mirror_even)
    edge_e = send(edge, x_even)
    generic = lax.axis_size("gx") != 4
    extra = []
    if generic:
        start = jnp.where(lax.axis_index("gx") % 2 == 1, (n - WIDTH) * r, 0)
        far = lax.dynamic_slice_in_dim(g, start, WIDTH * r, 0)
        extra = [send(far, x_odd), send(far, mirror_odd)]
    full = n + 2 * WIDTH
    wide = -(-full // 8) * 8
    u, even_u, odd_u = call(
        functools.partial(update, n, r, generic),
        [(full * r, depth), (WIDTH * wide, depth), (WIDTH * wide, depth)],
        [g, mid, rim, edge_m, edge_e] + extra + [d, m, even, odd, order],
        scratch=[VMEM((wide * r, depth), jnp.float32), VMEM((size, depth), jnp.float32)],
    )
    odd_u = send(odd_u, y_odd)
    even_u = send(even_u, y_even)
    (out,) = call(
        functools.partial(smooth, n, r, 32),
        [(size, depth)],
        [u, even_u, odd_u, radius, inverse],
        scratch=[VMEM((wide * r, depth), jnp.float32), VMEM((WIDTH, full * r, depth), jnp.float32)],
    )
    return (
        e2.reshape(3, n, r, depth),
        h2.reshape(3, n, r, depth),
        out.reshape(n, r, depth),
    )


def solution(mesh):
    in_specs = (
        P(None, "gx", "gy", None),
        P(None, "gx", "gy", None),
        P(None, "gx", "gy", None),
        P(None, "gx", "gy", None),
        P("gx", "gy", None),
        P(None, None, "gx", "gy", None),
        P("gx", "gy", None),
        P("gy"),
        P("gx", "gy"),
    )
    out_specs = (P(None, "gx", "gy", None), P(None, "gx", "gy", None), P("gx", "gy", None))
    return jax.shard_map(local, mesh=mesh, in_specs=in_specs, out_specs=out_specs, check_vma=False)
```

```python
import functools
import math

import jax
import jax.numpy as jnp
from jax import lax
from jax.experimental import pallas as pl
from jax.experimental.pallas import tpu as pltpu
from jax.sharding import PartitionSpec as P

STEPS = 2
RMAX = 4

COURANT = 0.5
DAMPING = 0.9
OMEGA_SQUARED = 0.3
LORENTZ_STRENGTH = 2.0
EPS_MATERIAL = 4.0
UPDATE_STEP = 0.25
SHARPNESS = 4.0
THRESHOLD = 0.5

AXES = ("gx", "gy")
WIDTH = RMAX - 1
SLOTS = 20
BASE = 8
REACH = STEPS
VMEM = pltpu.VMEM


def late_rows(n):
    up = ((0, -1), (0, n), (1, -1), (1, n - 1), (2, 0), (2, n - 1), (3, 0), (3, n - 2), (3, n - 1), (4, n))
    down = ((0, -1), (0, n - 1), (1, 0), (1, n - 1), (2, -1), (3, -2), (3, -1), (3, n), (4, -1), (4, n))
    return up, down


LATE = 16


def x_even(x, y, nx, ny):
    return x ^ 1, y


def x_odd(x, y, nx, ny):
    other = x + 1 if x % 2 else x - 1
    return (other, y) if 0 <= other < nx else (x, y ^ 1)


def y_even(x, y, nx, ny):
    return x, y ^ 1


def y_odd(x, y, nx, ny):
    other = y + 1 if y % 2 else y - 1
    return (x, other) if 0 <= other < ny else (x ^ 1, y)


def mirror(x, y, nx, ny):
    return nx - 1 - x, y


def mirror_even(x, y, nx, ny):
    return nx - 1 - (x ^ 1), y


def mirror_odd(x, y, nx, ny):
    other = x + 1 if x % 2 else x - 1
    return (nx - 1 - other, y) if 0 <= other < nx else (nx - 1 - x, y)


def send(block, rule):
    nx, ny = lax.axis_size("gx"), lax.axis_size("gy")
    route = []
    for x in range(nx):
        for y in range(ny):
            to_x, to_y = rule(x, y, nx, ny)
            route.append((x * ny + y, to_x * ny + to_y))
    return lax.ppermute(block, AXES, route)


def odd_x():
    return lax.rem(lax.axis_index("gx"), 2) == 1


def odd_y():
    return lax.rem(lax.axis_index("gy"), 2) == 1


def edges():
    x, y = lax.axis_index("gx"), lax.axis_index("gy")
    return (x > 0, x < lax.axis_size("gx") - 1, y > 0, y < lax.axis_size("gy") - 1)


def rows_of(shape):
    return lax.broadcasted_iota(jnp.int32, shape, len(shape) - 2)


def lanes_of(shape):
    return lax.broadcasted_iota(jnp.int32, shape, len(shape) - 1)


def ahead_z(v):
    depth = v.shape[-1]
    return jnp.where(lanes_of(v.shape) == depth - 1, 0.0, pltpu.roll(v, depth - 1, v.ndim - 1))


def behind_z(v):
    return jnp.where(lanes_of(v.shape) == 0, 0.0, pltpu.roll(v, 1, v.ndim - 1))


def ahead_y(v, edge=0.0):
    rows = v.shape[-2]
    return jnp.where(rows_of(v.shape) == rows - 1, edge, pltpu.roll(v, rows - 1, v.ndim - 2))


def behind_y(v, edge=0.0):
    return jnp.where(rows_of(v.shape) == 0, edge, pltpu.roll(v, 1, v.ndim - 2))


def keep(flag, v):
    return jnp.where(flag, v, 0.0)


def call(kernel, outs, args, aliases=None, flops=0, scratch=()):
    spec = pl.BlockSpec(memory_space=VMEM)
    traffic = 4 * (sum(math.prod(s) for s in outs) + sum(math.prod(a.shape) for a in args))
    return pl.pallas_call(
        kernel,
        out_shape=tuple(VMEM(s, jnp.float32) for s in outs),
        in_specs=[spec] * len(args),
        out_specs=tuple([spec] * len(outs)),
        scratch_shapes=scratch,
        input_output_aliases=aliases or {},
        cost_estimate=pl.CostEstimate(flops=flops, bytes_accessed=traffic, transcendentals=0),
        compiler_params=pltpu.CompilerParams(vmem_limit_bytes=16 * 2**20),
    )(*[pltpu.with_memory_space_constraint(a, VMEM) for a in args])


def pack_x(n, r, e, h, p, q, d, m, even_out, odd_out, e_at, h_at, p_at, q_at, d_at, m_at, sems):
    copies = []
    for end in range(2):
        for k, (ref, held, planes) in enumerate(
            ((e, e_at, 2), (h, h_at, 2), (p, p_at, 1), (q, q_at, 1), (d, d_at, WIDTH), (m, m_at, WIDTH))
        ):
            rows = pl.ds((n - planes) * r if end else 0, planes * r)
            src = ref.at[:, rows, :] if len(ref.shape) == 3 else ref.at[rows, :]
            copies.append(pltpu.make_async_copy(src, held.at[end], sems.at[end, k]))
    for copy in copies:
        copy.start()
    for copy in copies:
        copy.wait()
    odd = odd_x()

    def take(ref, planes, k, c=None):
        low, high = slice(k * r, (k + 1) * r), slice((planes - 1 - k) * r, (planes - k) * r)
        if c is None:
            return ref[0, low, :], ref[1, high, :]
        return ref[0, c, low, :], ref[1, c, high, :]

    def put(slot, pair):
        at = slice(slot * r, (slot + 1) * r)
        even_out[at, :] = jnp.where(odd, pair[0], pair[1])
        odd_out[at, :] = jnp.where(odd, pair[1], pair[0])

    for c in range(3):
        put(c, take(e_at, 2, 0, c))
        put(3 + c, take(h_at, 2, 0, c))
        put(6 + c, [DAMPING * b - OMEGA_SQUARED * a for a, b in zip(take(p_at, 1, 0, c), take(q_at, 1, 0, c))])
        put(10 + c, take(e_at, 2, 1, c))
    put(9, take(d_at, WIDTH, 0))
    put(13, take(h_at, 2, 1, 1))
    put(14, take(h_at, 2, 1, 2))
    put(15, take(d_at, WIDTH, 1))
    put(16, take(d_at, WIDTH, 2))
    for k in range(WIDTH):
        put(17 + k, [v.astype(jnp.float32) for v in take(m_at, WIDTH, k)])


def new_h(h, e, e_next, edge_x=0.0, edge_z=0.0):
    ex, ey, ez = e
    return (
        h[0] - COURANT * ((ahead_y(ez, edge_z) - ez) - (ahead_z(ey) - ey)),
        h[1] - COURANT * ((ahead_z(ex) - ex) - (e_next[2] - ez)),
        h[2] - COURANT * ((e_next[1] - ey) - (ahead_y(ex, edge_x) - ex)),
    )


def curl_h(h, h_last, edge_x=0.0, edge_z=0.0):
    hx, hy, hz = h
    return (
        (hz - behind_y(hz, edge_z)) - (hy - behind_z(hy)),
        (hx - behind_z(hx)) - (hz - h_last[2]),
        (hy - h_last[1]) - (hx - behind_y(hx, edge_x)),
    )


def half_over_eps(d):
    return COURANT / (1.0 + (EPS_MATERIAL - 1.0) * d)


def step_inner(n, r, block, e, h, p, q, d, h_out, e_out, c_out, t_out, even_y, odd_y_out):
    def plane(ref, x, c=None):
        at = pl.ds(pl.multiple_of(x * r, r), r)
        return ref[at, :] if c is None else ref[c, at, :]

    def put(ref, x, v, c=None):
        at = pl.ds(pl.multiple_of(x * r, r), r)
        if c is None:
            ref[at, :] = v
        else:
            ref[c, at, :] = v

    def one(x, last):
        now = [plane(e, x, c) for c in range(3)]
        nxt = [plane(e, jnp.minimum(x + 1, n - 1), c) for c in range(3)]
        mine = new_h([plane(h, x, c) for c in range(3)], now, nxt)
        dd = plane(d, x)
        half = half_over_eps(dd)
        put(c_out, x + 1, half)
        curl = curl_h(mine, last)
        for c in range(3):
            old = plane(p, x, c)
            rate = DAMPING * plane(q, x, c) - OMEGA_SQUARED * old + (OMEGA_SQUARED * LORENTZ_STRENGTH) * dd * now[c]
            put(t_out, x, (DAMPING - OMEGA_SQUARED) * rate - OMEGA_SQUARED * old, c)
            put(h_out, x + 1, mine[c], c)
            put(e_out, x + 1, now[c] + half * (curl[c] - 2.0 * rate), c)
        return mine

    def body(i, last):
        for k in range(block):
            last = one(i * block + k, last)
        return last

    zero = jnp.zeros((r, e.shape[-1]), jnp.float32)
    for c in range(3):
        put(h_out, n + 1, zero, c)
        put(e_out, n + 1, zero, c)
    lax.fori_loop(0, n // block, body, (zero, zero, zero))
    flip_y = odd_y()
    for k, (u, v) in enumerate(zip(*faces(n, r, n, 0, e, h_out, e_out, c_out))):
        even_y[k * n : (k + 1) * n, :] = jnp.where(flip_y, v, u)
        odd_y_out[k * n : (k + 1) * n, :] = jnp.where(flip_y, u, v)


def faces(n, r, size, x, e, h_out, e_out, c_out):
    def row(ref, y, first, c=None):
        at = pl.ds((first + 1) * r + y, size, stride=r)
        return ref[at, :] if c is None else ref[c, at, :]

    last = r - 1
    g_x, g_z = row(h_out, last, x, 0), row(h_out, last, x, 2)
    a_x, a_y, a_z = row(e_out, last, x, 0), row(e_out, last, x, 1), row(e_out, last, x, 2)
    a_y1 = row(e_out, last, x + 1, 1)
    up = (
        g_x,
        g_z,
        g_x + COURANT * a_z + COURANT * (ahead_z(a_y) - a_y),
        g_z - COURANT * (a_y1 - a_y) - COURANT * a_x,
        row(c_out, last, x),
    )
    down = (
        row(e_out, 0, x, 0),
        row(e_out, 0, x, 2),
        row(c_out, 0, x),
        e[0, pl.ds(x * r, size, stride=r), :],
        e[2, pl.ds(x * r, size, stride=r), :],
    )
    return up, down


def step_edges(n, r, e, h, p, q, d, even, odd, h_in, e_in, c_in, h_out, e_out, c_out, rows_out, even_y, odd_y_out):
    del h_in, e_in, c_in
    flip = odd_x()
    below, above, _, _ = edges()

    def lo(slot):
        at = slice(slot * r, (slot + 1) * r)
        return keep(below, jnp.where(flip, even[at, :], odd[at, :]))

    def hi(slot):
        at = slice(slot * r, (slot + 1) * r)
        return keep(above, jnp.where(flip, odd[at, :], even[at, :]))

    def own(ref, x):
        return [ref[c, x * r : (x + 1) * r, :] for c in range(3)]

    def at(x):
        return slice((x + 1) * r, (x + 2) * r)

    e_m2, e_m1 = [lo(10), lo(11), lo(12)], [lo(0), lo(1), lo(2)]
    e_n, e_n1 = [hi(0), hi(1), hi(2)], [hi(10), hi(11), hi(12)]
    e_0, e_l = own(e, 0), own(e, n - 1)
    h_m2 = new_h([lo(13), lo(13), lo(14)], e_m2, e_m1)
    h_m1 = [keep(below, v) for v in new_h([lo(3), lo(4), lo(5)], e_m1, e_0)]
    h_l = new_h(own(h, n - 1), e_l, e_n)
    h_n = new_h([hi(3), hi(4), hi(5)], e_n, e_n1)
    h_0 = [h_out[c, at(0), :] for c in range(3)]
    h_l1 = [h_out[c, at(n - 2), :] for c in range(3)]

    def new_e(x, electric, magnetic, last, drift, density, flag=None):
        half = half_over_eps(density)
        if flag is not None:
            half = keep(flag, half)
            c_out[at(x), :] = half
        curl = curl_h(magnetic, last)
        for c in range(3):
            rate = drift[c] + (OMEGA_SQUARED * LORENTZ_STRENGTH) * density * electric[c]
            e_out[c, at(x), :] = electric[c] + half * (curl[c] - 2.0 * rate)

    def drift(x):
        return [DAMPING * b - OMEGA_SQUARED * a for a, b in zip(own(p, x), own(q, x))]

    for c in range(3):
        h_out[c, at(-1), :] = h_m1[c]
        h_out[c, at(n - 1), :] = h_l[c]
        h_out[c, at(n), :] = h_n[c]
    new_e(-1, e_m1, h_m1, h_m2, [lo(6), lo(7), lo(8)], lo(9), below)
    new_e(0, e_0, h_0, h_m1, drift(0), d[:r, :])
    new_e(n - 1, e_l, h_l, h_l1, drift(n - 1), d[(n - 1) * r :, :])
    new_e(n, e_n, h_n, h_l, [hi(6), hi(7), hi(8)], hi(9), above)

    for k, c in enumerate((0, 2)):
        rows_out[k, BASE - 1 : BASE, :] = e_m1[c][:1]
        rows_out[k, BASE : BASE + n, :] = e[c, pl.ds(0, n, stride=r), :]
        rows_out[k, BASE + n : BASE + n + 1, :] = e_n[c][:1]

    def up(field, x):
        def at_last(ref, c, x):
            start = (x + 1) * r + r - 1
            return ref[c, start : start + 1, :]

        g_x, g_z = at_last(h_out, 0, x), at_last(h_out, 2, x)
        if field == 0:
            return g_x
        if field == 1:
            return g_z
        if field == 4:
            return c_out[(x + 2) * r - 1 : (x + 2) * r, :]
        a_y = at_last(e_out, 1, x)
        if field == 2:
            return g_x + COURANT * at_last(e_out, 2, x) + COURANT * (ahead_z(a_y) - a_y)
        return g_z - COURANT * (at_last(e_out, 1, x + 1) - a_y) - COURANT * at_last(e_out, 0, x)

    def down(field, x):
        start = (x + 1) * r
        if field < 2:
            return e_out[2 * field, start : start + 1, :]
        if field == 2:
            return c_out[start : start + 1, :]
        return {-2: e_m2, -1: e_m1, n: e_n}[x][2 * (field - 3)][:1]

    flip_y = odd_y()
    zero = jnp.zeros((1, e.shape[-1]), jnp.float32)
    upward, downward = late_rows(n)
    for k in range(LATE):
        u = up(*upward[k]) if k < len(upward) else zero
        v = down(*downward[k]) if k < len(downward) else zero
        even_y[k : k + 1, :] = jnp.where(flip_y, v, u)
        odd_y_out[k : k + 1, :] = jnp.where(flip_y, u, v)


def step_mid(n, r, block, h, e, c_ref, t, d, f, out, g):
    below, _, _, _ = edges()

    def fields(ref, x):
        at = pl.ds(pl.multiple_of((x + 1) * r, r), r)
        return [ref[c, at, :] for c in range(3)]

    def one(x, last_h):
        now = fields(e, x)
        mine = new_h(fields(h, x), now, fields(e, x + 1))
        at = pl.ds(pl.multiple_of(x * r, r), r)
        half = c_ref[pl.ds(pl.multiple_of((x + 1) * r, r), r), :]
        dd = d[at, :]
        curl = curl_h(mine, last_h)
        total = None
        for c in range(3):
            rate = t[c, at, :] + (OMEGA_SQUARED * LORENTZ_STRENGTH) * dd * now[c]
            after = now[c] + half * (curl[c] - 2.0 * rate)
            part = now[c] * f[c, at, :] + after * f[3 + c, at, :]
            total = part if total is None else total + part
        g[at, :] = total
        return mine

    def body(i, last_h):
        for k in range(block):
            last_h = one(i * block + k, last_h)
        return last_h

    start = tuple(keep(below, v) for v in new_h(fields(h, -1), fields(e, -1), fields(e, 0)))
    lax.fori_loop(0, n // block, body, start)
    for j in range(REACH, r - REACH):
        out[(j - REACH) * n : (j - REACH + 1) * n, :] = g[pl.ds(j, n, stride=r), :]


def step_last(n, r, late, h, e, c_ref, t, d, rows, even, odd, *refs):
    if late:
        odd_late, even_late, f, _, _, _, e_out, h_out, g_out, rim_out, edge_out, face, fix = refs
    else:
        f, e_out, h_out, g_out, face, fix = refs
    flip = odd_y()
    below, above, low, high = edges()
    hxm, hzm, dx, dz, ry, exp_, ezp, hxm2, hzm2, wm = range(10)
    last = r - 1
    apart = jnp.zeros((BASE, h.shape[-1]), jnp.float32)
    for k in range(5):
        at = slice(k * n, (k + 1) * n)
        for side in range(2):
            face[side, k, :BASE, :] = apart
            face[side, k, BASE + n :, :] = apart
        face[0, k, BASE : BASE + n, :] = jnp.where(flip, even[at, :], odd[at, :])
        face[1, k, BASE : BASE + n, :] = jnp.where(flip, odd[at, :], even[at, :])
    if late:
        for k, ((field_u, x_u), (field_v, x_v)) in enumerate(zip(*late_rows(n))):
            at = slice(k, k + 1)
            face[0, field_u, BASE + x_u : BASE + x_u + 1, :] = jnp.where(flip, even_late[at, :], odd_late[at, :])
            face[1, field_v, BASE + x_v : BASE + x_v + 1, :] = jnp.where(flip, odd_late[at, :], even_late[at, :])

    def up(k, x=0, size=n):
        return keep(low, face[0, k, BASE + x : BASE + x + size, :])

    def down(k, x=0, size=n):
        return keep(high, face[1, k, BASE + x : BASE + x + size, :])

    def put(which, v, x=0):
        fix[which, BASE + x : BASE + x + v.shape[0], :] = v

    def get(which, x=0, size=n):
        return fix[which, BASE + x : BASE + x + size, :]

    def row_e(k, x=0, size=n):
        return rows[k, BASE + x : BASE + x + size, :]

    def strided(ref, y, c, x=0):
        return ref[c, pl.ds((x + 1) * r + y, n, stride=r), :]

    for x, size in ((0, n), (-1, 1), (n, 1)):
        put(hxm, keep(low, up(0, x, size) - COURANT * row_e(1, x, size)), x)
        put(dx, -COURANT * down(4, x, size), x)
        put(dz, COURANT * down(3, x, size), x)
    put(dz, COURANT * down(3, -2, 1), -2)
    for x, size in ((0, n), (-1, 1)):
        put(hzm, keep(low, up(1, x, size) + COURANT * row_e(0, x, size)), x)
    put(hzm, jnp.zeros((1, h.shape[-1]), jnp.float32), n)
    for x, size in ((0, n), (-1, 1), (n, 1)):
        delta = get(dx, x, size)
        put(ry, delta - behind_z(delta) - get(dz, x, size) + get(dz, x - 1, size), x)

    half = down(2)
    put(exp_, down(0) - half * (strided(h, last, 2) + get(dz)))
    put(exp_, down(0, -1, 1) - down(2, -1, 1) * (h[2, last : last + 1, :] + get(dz, -1, 1)), -1)
    put(ezp, down(1) + half * (strided(h, last, 0) + get(dx)))
    half = up(4)

    def gain(x, size, factor):
        delta = -COURANT * row_e(1, x, size)
        step = COURANT * (row_e(0, x, size) - row_e(0, x - 1, size))
        return factor * (delta - behind_z(delta) - step)

    put(wm, gain(0, n, half))
    put(wm, gain(n, 1, up(4, n, 1)), n)
    delta_x, delta_z = -COURANT * row_e(1), COURANT * row_e(0)
    change = get(wm)
    here = c_ref[pl.ds(r, n, stride=r), :]
    first_z = strided(e, 0, 2) + here * get(hxm)
    first_x = strided(e, 0, 0) - here * get(hzm)
    add = up(2) + delta_x - COURANT * half * delta_x + COURANT * (ahead_z(change) - change) - COURANT * first_z
    put(hxm2, keep(low, add))
    add = up(3) + delta_z - COURANT * half * delta_z - COURANT * (get(wm, 1) - change) + COURANT * first_x
    put(hzm2, keep(low, add))

    shape = (r, h.shape[-1])
    first_row, last_row = rows_of(shape) == 0, rows_of(shape) == last

    def spread(which, x):
        return fix[which, pl.ds(BASE + x, 1), :]

    def after_one(x):
        at = pl.ds(pl.multiple_of((x + 1) * r, r), r)
        half = c_ref[at, :]
        d_x, d_z = jnp.where(last_row, spread(dx, x), 0.0), jnp.where(last_row, spread(dz, x), 0.0)
        magnetic = (h[0, at, :] + d_x, h[1, at, :], h[2, at, :] + d_z)
        electric = (
            e[0, at, :] + half * jnp.where(first_row, -spread(hzm, x), d_z),
            e[1, at, :] + half * jnp.where(last_row, spread(ry, x), 0.0),
            e[2, at, :] + half * jnp.where(first_row, spread(hxm, x), -d_x),
        )
        return magnetic, electric

    def second_h(x, magnetic, now, ahead):
        return new_h(magnetic, now, ahead, spread(exp_, x), spread(ezp, x))

    def one(x, carry):
        last_h, magnetic, now = carry
        next_magnetic, ahead = after_one(x + 1)
        mine = second_h(x, magnetic, now, ahead)
        at = pl.ds(pl.multiple_of(x * r, r), r)
        half = c_ref[pl.ds(pl.multiple_of((x + 1) * r, r), r), :]
        dd = d[at, :]
        curl = curl_h(mine, last_h, spread(hxm2, x), spread(hzm2, x))
        total = None
        for c in range(3):
            rate = t[c, at, :] + (OMEGA_SQUARED * LORENTZ_STRENGTH) * dd * now[c]
            after = now[c] + half * (curl[c] - 2.0 * rate)
            e_out[c, at, :] = after
            h_out[c, at, :] = mine[c]
            part = now[c] * f[c, at, :] + after * f[3 + c, at, :]
            total = part if total is None else total + part
        g_out[at, :] = total
        return mine, next_magnetic, ahead

    def run(first, end):
        magnetic, now = after_one(first - 1)
        next_magnetic, ahead = after_one(first)
        last_h = second_h(first - 1, magnetic, now, ahead)
        if first == 0:
            last_h = tuple(keep(below, v) for v in last_h)
        carry = (last_h, next_magnetic, ahead)
        for x in range(first, end):
            carry = one(x, carry)

    if not late:
        run(REACH, n - REACH)
        return
    run(0, REACH)
    run(n - REACH, n)
    for k, j in enumerate(rim_rows(r)):
        rim_out[k * n : (k + 1) * n, :] = g_out[pl.ds(j, n, stride=r), :]
    first = jnp.where(odd_x(), 0, n - WIDTH)
    edge_out[...] = g_out[pl.ds(pl.multiple_of(first * r, r), WIDTH * r), :]


def rim_rows(r):
    return [j for j in range(r) if not REACH <= j < r - REACH]


def update(n, r, generic, *refs):
    if generic:
        g, mid, edge_m, rim, edge, far, far_m, d, m, even, odd, order, u_out, even_y, odd_y_out, u_pad, other = refs
    else:
        g, mid, edge_m, rim, edge, d, m, even, odd, order, u_out, even_y, odd_y_out, u_pad, other = refs
    for k, j in enumerate(range(REACH, r - REACH)):
        other[pl.ds(j, n, stride=r), :] = mid[k * n : (k + 1) * n, :]
    for k, j in enumerate(rim_rows(r)):
        other[pl.ds(j, n, stride=r), :] = rim[k * n : (k + 1) * n, :]
    flip = odd_x()
    below, above, _, _ = edges()
    perm = order[...]

    def paired(v):
        return jnp.take_along_axis(v, perm, axis=0, mode="promise_in_bounds")

    def plane(ref, x):
        return ref[pl.ds(pl.multiple_of(x * r, r), r), :]

    def put(k, v):
        at = pl.ds(pl.multiple_of(k * r, r), r)
        u_out[at, :] = v
        u_pad[at, :] = v

    scale = 0.5 * UPDATE_STEP
    for x in range(n):
        put(x + WIDTH, plane(d, x) - scale * plane(m, x).astype(jnp.float32) * (plane(g, x) + paired(plane(other, n - 1 - x))))
    slots = (9, 15, 16)
    for j in range(WIDTH):
        high, low = n + WIDTH + j, WIDTH - 1 - j
        back, forth = jnp.where(flip, j, WIDTH - 1 - j), jnp.where(flip, WIDTH - 1 - j, j)
        u = plane(even, slots[j]) - scale * plane(even, 17 + j) * (plane(edge, forth) + paired(plane(edge_m, back)))
        put(jnp.where(flip, low, high), u)
        if generic:
            near, mirrored = plane(far, back), plane(far_m, forth)
        else:
            near = plane(other, jnp.where(flip, j, n - 1 - j))
            mirrored = plane(g, jnp.where(flip, n - 1 - j, j))
        u = plane(odd, slots[j]) - scale * plane(odd, 17 + j) * (near + paired(mirrored))
        put(jnp.where(flip, high, low), keep(jnp.where(flip, above, below), u))
    flip_y = odd_y()
    wide = u_pad.shape[0] // r
    for j in range(WIDTH):
        upper = u_pad[pl.ds(r - WIDTH + j, wide, stride=r), :]
        lower = u_pad[pl.ds(j, wide, stride=r), :]
        at = slice(j * wide, (j + 1) * wide)
        even_y[at, :] = jnp.where(flip_y, lower, upper)
        odd_y_out[at, :] = jnp.where(flip_y, upper, lower)


CLASSES = (
    (0.0, ((0, 0),)),
    (1.0, ((0, 1), (1, 0))),
    (2.0, ((1, 1),)),
    (4.0, ((2, 0), (0, 2))),
    (5.0, ((2, 1), (1, 2))),
    (8.0, ((2, 2),)),
    (9.0, ((3, 0), (0, 3))),
    (10.0, ((3, 1), (1, 3))),
    (13.0, ((3, 2), (2, 3))),
    (18.0, ((3, 3),)),
)


def weight(radius, square):
    return jnp.maximum(radius - math.sqrt(square), 0.0)


def cover(n, r, block, radius, out):
    x0, y0 = lax.axis_index("gx") * n, lax.axis_index("gy") * r
    total_x, total_y = n * lax.axis_size("gx"), r * lax.axis_size("gy")
    shape = (r, out.shape[-1])
    y = y0 + rows_of(shape)
    ones = jnp.ones(shape, jnp.float32)

    def there(where, total):
        return ((where >= 0) & (where < total)).astype(jnp.float32)

    across = [ones] + [there(y - b, total_y) + there(y + b, total_y) for b in range(1, RMAX)]

    def one(x):
        at = pl.ds(pl.multiple_of(x * r, r), r)
        rad = radius[at, :]
        where = jnp.full(shape, x0 + x, jnp.int32)
        along = [ones] + [there(where - a, total_x) + there(where + a, total_x) for a in range(1, RMAX)]
        total = None
        for square, members in CLASSES:
            part = sum(across[b] * along[a] for b, a in members)
            part = weight(rad, square) * part
            total = part if total is None else total + part
        out[at, :] = 1.0 / total

    def body(i, carry):
        for k in range(block):
            one(i * block + k)
        return carry

    lax.fori_loop(0, n // block, body, 0)


def smooth(n, r, block, u, even, odd, radius, inverse, out, halo, sums):
    flip = odd_y()
    _, _, low, high = edges()
    wide = even.shape[0] // WIDTH
    full = n + 2 * WIDTH
    for j in range(WIDTH):
        at = slice(j * wide, (j + 1) * wide)
        lower = keep(low, jnp.where(flip, even[at, :], odd[at, :]))
        upper = keep(high, jnp.where(flip, odd[at, :], even[at, :]))
        halo[pl.ds(r - WIDTH + j, wide, stride=r), :] = lower
        halo[pl.ds(j, wide, stride=r), :] = upper
    shape = (r, u.shape[-1])
    row = rows_of(shape)

    def fold(k):
        at = pl.ds(pl.multiple_of(k * r, r), r)
        mine, beside = u[at, :], halo[at, :]
        for b in range(1, RMAX):
            upper = pltpu.roll(jnp.where(row < b, beside, mine), r - b, 0)
            lower = pltpu.roll(jnp.where(row >= r - b, beside, mine), b, 0)
            sums[b - 1, at, :] = upper + lower

    def fold_block(i, carry):
        for k in range(block):
            fold(i * block + k)
        return carry

    whole = full // block
    lax.fori_loop(0, whole, fold_block, 0)
    for k in range(whole * block, full):
        fold(k)

    top = math.tanh(SHARPNESS * THRESHOLD)
    bottom = top + math.tanh(SHARPNESS * (1.0 - THRESHOLD))

    def one(x):
        at = pl.ds(pl.multiple_of(x * r, r), r)
        rad = radius[at, :]

        def line(b, a):
            where = pl.ds(pl.multiple_of((x + WIDTH + a) * r, r), r)
            return u[where, :] if b == 0 else sums[b - 1, where, :]

        total = None
        for square, members in CLASSES:
            part = None
            for b, a in members:
                v = line(b, 0) if a == 0 else line(b, a) + line(b, -a)
                part = v if part is None else part + v
            part = weight(rad, square) * part
            total = part if total is None else total + part
        filtered = total * inverse[at, :]
        out[at, :] = (top + jnp.tanh(SHARPNESS * (filtered - THRESHOLD))) / bottom

    def body(i, carry):
        for k in range(block):
            one(i * block + k)
        return carry

    lax.fori_loop(0, n // block, body, 0)


def local(
    adj_electric,
    adj_magnetic,
    polarization,
    pol_rate,
    density,
    forward_rate,
    design_mask,
    partner_rows,
    filter_radius,
):
    n, r, depth = density.shape
    size = n * r
    e, h = adj_electric.reshape(3, size, depth), adj_magnetic.reshape(3, size, depth)
    p, q = polarization.reshape(3, size, depth), pol_rate.reshape(3, size, depth)
    d, m = density.reshape(size, depth), design_mask.reshape(size, depth)
    f = forward_rate.reshape(3 * STEPS, size, depth)
    more = size + 2 * r
    face_x = (SLOTS * r, depth)
    face_y = (5 * n, depth)
    lines = n + 2 * BASE

    f32 = jnp.float32
    even, odd = pl.pallas_call(
        functools.partial(pack_x, n, r),
        out_shape=(VMEM(face_x, f32), VMEM(face_x, f32)),
        in_specs=[pl.BlockSpec(memory_space=pl.ANY)] * 6,
        out_specs=(pl.BlockSpec(memory_space=VMEM), pl.BlockSpec(memory_space=VMEM)),
        scratch_shapes=[
            VMEM((2, 3, 2 * r, depth), f32),
            VMEM((2, 3, 2 * r, depth), f32),
            VMEM((2, 3, r, depth), f32),
            VMEM((2, 3, r, depth), f32),
            VMEM((2, WIDTH * r, depth), f32),
            VMEM((2, WIDTH * r, depth), jnp.int32),
            pltpu.SemaphoreType.DMA((2, 6)),
        ],
    )(e, h, p, q, d, m)
    even = send(even, x_even)
    odd = send(odd, x_odd)

    inner = functools.partial(step_inner, n, r, 32)
    h1, e1, c1, t1, even_y, odd_y_ = call(
        inner,
        [(3, more, depth)] * 2 + [(more, depth), (3, size, depth)] + [face_y] * 2,
        [e, h, p, q, d],
        flops=100 * size * depth,
    )
    odd_y_ = send(odd_y_, y_odd)
    even_y = send(even_y, y_even)
    ends = functools.partial(step_edges, n, r)
    h1, e1, c1, rows, even_late, odd_late = call(
        ends,
        [(3, more, depth)] * 2 + [(more, depth), (2, lines, depth)] + [(LATE, depth)] * 2,
        [e, h, p, q, d, even, odd, h1, e1, c1],
        aliases={7: 0, 8: 1, 9: 2},
    )
    odd_late = send(odd_late, y_odd)
    even_late = send(even_late, y_even)
    (mid,) = call(
        functools.partial(step_mid, n, r, 32),
        [((r - 2 * REACH) * n, depth)],
        [h1, e1, c1, t1, d, f],
        flops=100 * size * depth,
        scratch=[VMEM((size, depth), jnp.float32)],
    )
    mid = send(mid, mirror)

    radius = jnp.broadcast_to(filter_radius.astype(jnp.float32)[:, :, None], (n, r, depth)).reshape(size, depth)
    order = jnp.broadcast_to(partner_rows[:, None], (r, depth))
    (inverse,) = call(functools.partial(cover, n, r, 16), [(size, depth)], [radius], flops=100 * size * depth)

    known = [h1, e1, c1, t1, d, rows, even_y, odd_y_]
    fields = [(3, size, depth)] * 2 + [(size, depth)]
    lists = [VMEM((2, 5, lines, depth), f32), VMEM((10, lines, depth), f32)]
    e2, h2, g = call(functools.partial(step_last, n, r, False), fields, known + [f], flops=150 * size * depth, scratch=lists)
    e2, h2, g, rim, edge = call(
        functools.partial(step_last, n, r, True),
        fields + [(2 * REACH * n, depth), (WIDTH * r, depth)],
        known + [odd_late, even_late, f, e2, h2, g],
        aliases={11: 0, 12: 1, 13: 2},
        scratch=lists,
    )
    rim = send(rim, mirror)
    edge_m = send(edge, mirror_even)
    edge_e = send(edge, x_even)
    generic = lax.axis_size("gx") != 4
    extra = []
    if generic:
        start = jnp.where(lax.axis_index("gx") % 2 == 1, (n - WIDTH) * r, 0)
        far = lax.dynamic_slice_in_dim(g, start, WIDTH * r, 0)
        extra = [send(far, x_odd), send(far, mirror_odd)]
    full = n + 2 * WIDTH
    wide = -(-full // 8) * 8
    u, even_u, odd_u = call(
        functools.partial(update, n, r, generic),
        [(full * r, depth), (WIDTH * wide, depth), (WIDTH * wide, depth)],
        [g, mid, edge_m, rim, edge_e] + extra + [d, m, even, odd, order],
        scratch=[VMEM((wide * r, depth), jnp.float32), VMEM((size, depth), jnp.float32)],
    )
    odd_u = send(odd_u, y_odd)
    even_u = send(even_u, y_even)
    (out,) = call(
        functools.partial(smooth, n, r, 32),
        [(size, depth)],
        [u, even_u, odd_u, radius, inverse],
        scratch=[VMEM((wide * r, depth), jnp.float32), VMEM((WIDTH, full * r, depth), jnp.float32)],
    )
    return (
        e2.reshape(3, n, r, depth),
        h2.reshape(3, n, r, depth),
        out.reshape(n, r, depth),
    )


def solution(mesh):
    in_specs = (
        P(None, "gx", "gy", None),
        P(None, "gx", "gy", None),
        P(None, "gx", "gy", None),
        P(None, "gx", "gy", None),
        P("gx", "gy", None),
        P(None, None, "gx", "gy", None),
        P("gx", "gy", None),
        P("gy"),
        P("gx", "gy"),
    )
    out_specs = (P(None, "gx", "gy", None), P(None, "gx", "gy", None), P("gx", "gy", None))
    return jax.shard_map(local, mesh=mesh, in_specs=in_specs, out_specs=out_specs, check_vma=False)
```
